32 devices in a mesh: fsdp: 4 (over y, x), ctx: 2 (over core), tp: 4 (over z).
Axes of the slice: x: 2, y: 2, z: 4, core: 2. Of those that a mesh axis runs over, the one named last changes fastest.
Arguments:
- tokens: bfloat16 [8192, 768], P(('fsdp', 'ctx')), may hold values from -6 to 6
- grad_out: bfloat16 [8192, 768], P(('fsdp', 'ctx')), may hold values from -6 to 6
- w_qkv: bfloat16 [768, 3, 768], P(('fsdp', 'ctx'), None, 'tp'), may hold values from -0.21875 to 0.21875
- w_attn_out: bfloat16 [768, 768], P(('fsdp', 'ctx'), 'tp'), may hold values from -1.75 to 1.75
- rel_bias: float32 [32, 12], P(None, 'tp'), may hold values from -4 to 4
- gain_attn: bfloat16 [768], P(('fsdp', 'ctx')), may hold values from 0.099609375 to 1.8984375
- gain_ffn: bfloat16 [768], P(('fsdp', 'ctx')), may hold values from 0.099609375 to 1.8984375
- w_router: bfloat16 [768, 4], P(('fsdp', 'ctx')), may hold values from -0.15625 to 0.15625
- w_in: bfloat16 [4, 768, 3072], P('fsdp', None, 'tp'), may hold values from -0.21875 to 0.21875
- w_down: bfloat16 [4, 768, 3072], P('fsdp', None, 'tp'), may hold values from -0.4375 to 0.4375
- expert_ids: int32 [8192, 1], P(('fsdp', 'ctx')), may hold values from 0 to 3; in each aligned block of 1024 rows (0 to 1023, 1024 to 2047, ...) at most 512 rows name the same one
- doc_ids: int32 [8192], P('fsdp'), may hold values from 0 to 3, as said below
Outputs:
- out: bfloat16 [8192, 768], P(('fsdp', 'ctx'), 'tp')
- grad_tokens: float32 [8192, 768], P(('fsdp', 'ctx'), 'tp')
- grad_w_qkv: float32 [768, 3, 768], P(('fsdp', 'ctx'), None, 'tp')
- grad_w_attn_out: float32 [768, 768], P(('fsdp', 'ctx'), 'tp')
- grad_rel_bias: float32 [32, 12], P(('fsdp', 'ctx'), 'tp')
- grad_gain_attn: float32 [768], P(('fsdp', 'ctx'))
- grad_gain_ffn: float32 [768], P(('fsdp', 'ctx'))
- grad_w_router: float32 [768, 4], P(('fsdp', 'ctx'))
- grad_w_in: float32 [4, 768, 3072], P('fsdp', 'ctx', 'tp')
- grad_w_down: float32 [4, 768, 3072], P('fsdp', 'ctx', 'tp')
The draws below stay inside these ranges and needn't reach their ends.
Inputs may be any that keep to these rules, and one draw needn't show every extreme that they name: `expert_ids`: in each aligned block of 1024 rows no expert is named more than 512 times, and in every draw some block names some expert exactly 512 times. `doc_ids`: within each packed sequence of 2048 tokens the ids start at 0, never fall, and end at 3.
All inputs are finite; a program needn't handle non-finite values.
Results may differ from the reference program's by a relative error of at most 0.02.
Values may be sent and summed in bfloat16 or wider, within the bound.
No kernel may reach another device: no remote copies, remote signals or barrier semaphores. Data moves between devices by JAX's collectives and lax.ppermute only.
A program may use at most 192 MiB of HBM per device.

```python
import math
import jax
import jax.numpy as jnp
import numpy as np
from jax import lax

D = 768
HEADS = 12
HEAD_DIM = 64
FF = 3072
BUCKETS = 32
DOCS = 4
TOK_DEV = 1024
EXPERTS = 4
SEQ = 2048
TOKENS = 8192
CAP = 512


def draw_doc_ids(key, part):
    key = jax.random.fold_in(key, 11)
    pack_count = TOKENS // SEQ
    boundaries = jax.random.randint(key, (pack_count, DOCS - 1), 1, SEQ - 1)
    boundaries = jnp.where(boundaries >= TOK_DEV, boundaries + 1, boundaries)
    positions = jnp.arange(SEQ, dtype=jnp.int32)
    counted = (positions[None, :, None] >= boundaries[:, None, :]).astype(jnp.int32)
    return jnp.sum(counted, axis=-1).reshape(TOKENS).astype(jnp.int32)


def levels(key, extent, cuts, smallest, high):
    def one(axis_at, blocks):
        heights = jax.random.uniform(jax.random.fold_in(jax.random.fold_in(key, 6), axis_at), (blocks,), jnp.float32, smallest / len(cuts), high / len(cuts))
        return jnp.repeat(jnp.exp(heights), extent[axis_at] // blocks).reshape((-1,) + (1,) * (len(extent) - axis_at - 1))

    level = one(*cuts[0])
    for cut in cuts[1:]:
        level = level * one(*cut)
    return level


def deal_out(own_key, own, number, rows, count, top, reach, lean):
    sequence = jax.random.permutation(own_key, count)
    packed, common = shares(count, rows * top, reach, lean, True), shares(count, rows * top, reach, lean, False)
    places = jnp.arange(count)

    def named(sizes, offset_by):
        used = int((sizes > 0).sum())
        fixed = max(1, used // 4)
        passed = fixed + (places - fixed + offset_by * (used - fixed)) % max(1, count - fixed)
        return jnp.zeros((count,), jnp.int32).at[sequence[jnp.where(places < fixed, places, passed)]].set(jnp.asarray(sizes, jnp.int32))

    sizes = jnp.where(number % 4 == 0, named(packed, number // 4), named(common, number - number // 4 - 1))
    mixed = jax.random.permutation(jax.random.fold_in(own, 3), count)
    giver, taker = mixed[0:count // 2 * 2:2], mixed[1:count // 2 * 2:2]
    room = jnp.minimum(sizes[giver] - 1, reach - sizes[taker]) // 2
    room = jnp.where((giver == sequence[0]) | (taker == sequence[0]) | (sizes[taker] == 0), 0, jnp.maximum(room, 0))
    passed = jax.random.randint(jax.random.fold_in(own, 4), (count // 2,), 0, 1 << 20) % (room + 1)
    sizes = sizes.at[giver].add(-passed).at[taker].add(passed)
    members = jnp.searchsorted(jnp.cumsum(sizes), jnp.arange(rows * top), side="right").astype(jnp.int32)
    table = members.reshape(top, rows).T
    table = table[jax.random.permutation(jax.random.fold_in(own, 1), rows)]
    offset_by = jax.random.randint(jax.random.fold_in(own, 2), (rows, 1), 0, top)
    return jnp.take_along_axis(table, (jnp.arange(top)[None, :] + offset_by) % top, axis=1)


def shares(number_of, total, limit, lean, full):
    weights = [(1 << 20) // math.isqrt(grade ** lean) + 1 for grade in range(1, number_of + 1)]
    largest = limit if full else min(limit, max(-(-total // number_of), total * weights[0] // sum(weights)))
    least = 1 if total - largest >= number_of - 1 else 0
    counts, rest = [largest] + [least] * (number_of - 1), total - largest - least * (number_of - 1)
    while rest > 0:
        free = [i for i in range(1, number_of) if counts[i] < largest] or [i for i in range(1, number_of) if counts[i] < limit]
        pool, left = sum([weights[i] for i in free]), rest
        for i in free:
            more = min(limit - counts[i], max(1, left * weights[i] // pool), rest)
            counts[i] = counts[i] + more
            rest = rest - more
    return np.array(counts)


def centred(rng, extent, width, bound, pieces=(), kind=jnp.bfloat16):
    drawn = jax.random.normal(rng, extent, jnp.float32) * width
    if len(pieces) > 0:
        drawn = levels(rng, extent, pieces, -0.22, 0.18) * drawn
    return jnp.clip(drawn, min=-bound, max=bound).astype(kind)


def setup_inputs(seed: int = 0) -> dict:
    splits = jax.random.split(jax.random.key(seed), 13)
    tokens = centred(splits[0], (TOKENS, D), 1.0, 6.0, ((0, 8),))
    grad_out = centred(splits[1], (TOKENS, D), 1.0, 6.0, ((0, 8),))
    w_qkv = centred(splits[2], (D, 3, HEADS * HEAD_DIM), D ** -0.5, 0.21875, ((0, 8), (2, 4)))
    w_attn_out = centred(splits[3], (D, HEADS * HEAD_DIM), (HEADS * HEAD_DIM // 64) ** -0.5, 1.75, ((0, 8), (1, 4)))
    rel_bias = centred(splits[4], (BUCKETS, HEADS), 1.0, 4.0, ((1, 4),), jnp.float32)
    gain_attn = jnp.clip(1.0 + 0.18 * jax.random.normal(splits[5], (D,), jnp.float32), 0.099609375, 1.8984375).astype(jnp.bfloat16)
    gain_ffn = jnp.clip(1.0 + 0.18 * jax.random.normal(splits[6], (D,), jnp.float32), 0.099609375, 1.8984375).astype(jnp.bfloat16)
    w_router = centred(splits[7], (D, EXPERTS), (2 * D) ** -0.5, 0.15625, ((0, 8),))
    w_in = centred(splits[8], (EXPERTS, D, FF), D ** -0.5, 0.21875, ((0, 4), (2, 4)))
    w_down = centred(splits[9], (EXPERTS, D, FF), (max(1, FF // (EXPERTS * EXPERTS))) ** -0.5, 0.4375, ((0, 4), (2, 4)))
    expert_ids_keys = jax.random.split(jax.random.fold_in(splits[10], 1), TOKENS // TOK_DEV)
    expert_ids_turns = jax.random.permutation(jax.random.fold_in(splits[10], 3), TOKENS // TOK_DEV)
    expert_ids = jax.vmap(lambda own, number: deal_out(jax.random.fold_in(splits[10], 2), own, number, TOK_DEV, EXPERTS, 1, CAP, 2))(expert_ids_keys, expert_ids_turns).reshape((TOKENS, 1))
    doc_ids = draw_doc_ids(jax.random.fold_in(splits[12], 71), 0)
    return dict(tokens=tokens, grad_out=grad_out, w_qkv=w_qkv, w_attn_out=w_attn_out, rel_bias=rel_bias, gain_attn=gain_attn, gain_ffn=gain_ffn, w_router=w_router, w_in=w_in, w_down=w_down, expert_ids=expert_ids, doc_ids=doc_ids)


norm_eps = 1e-06
masked_score = -1e+30
bucket_edges = (12, 16, 23, 32, 46, 64, 91)

@jax.custom_vjp
def low(v):
    return lax.optimization_barrier(v.astype(jnp.bfloat16)).astype(jnp.float32)

@jax.custom_vjp
def low_back(v):
    return v

def low_keep(v):
    return (low(v), None)

def low_pass(kept, grad):
    return (grad,)

def back_keep(v):
    return (v, None)

def back_low(kept, grad):
    return (low(grad),)
low.defvjp(low_keep, low_pass)
low_back.defvjp(back_keep, back_low)

def relative_bucket(offset):
    distance = jnp.abs(offset)
    far_bucket = jnp.zeros_like(distance) + 8
    for edge in bucket_edges:
        far_bucket = far_bucket + (distance >= edge).astype(jnp.int32)
    result = jnp.where(distance < 8, distance, far_bucket)
    return (result + jnp.where(offset > 0, 16, 0)).astype(jnp.int32)

def expert_slots(expert_ids):
    chosen = expert_ids[:, 0].reshape(-1, TOK_DEV).astype(jnp.int32)
    one_hot = (chosen[:, :, None] == jnp.arange(EXPERTS, dtype=jnp.int32)[None, None, :]).astype(jnp.int32)
    earlier = jnp.cumsum(one_hot, axis=1) - one_hot
    slot_index = lax.optimization_barrier(jnp.sum(earlier * one_hot, axis=-1))
    block_count = chosen.shape[0]
    block_index = jnp.arange(block_count, dtype=jnp.int32)[:, None]
    target = chosen * (block_count * CAP) + block_index * CAP + slot_index
    return target.reshape(-1).astype(jnp.int32)

def attend_pack(qkv_pack, docs, table):
    query = qkv_pack[:, 0].reshape(SEQ, HEADS, HEAD_DIM)
    keys_here = qkv_pack[:, 1].reshape(SEQ, HEADS, HEAD_DIM)
    values_here = qkv_pack[:, 2].reshape(SEQ, HEADS, HEAD_DIM)
    places = jnp.arange(SEQ, dtype=jnp.int32)
    buckets = relative_bucket(places[None, :] - places[:, None])
    bias = jnp.transpose(table[buckets], (2, 0, 1))
    raw = jnp.einsum('qhe,khe->hqk', query, keys_here, precision=lax.Precision.HIGHEST)
    scores = low_back(raw * HEAD_DIM ** (-0.5) + bias)
    allowed = (docs[:, None] == docs[None, :])[None]
    row_peak = lax.optimization_barrier(jnp.max(jnp.where(allowed, scores, masked_score), axis=-1, keepdims=True))
    weights = jnp.where(allowed, jnp.exp(scores - row_peak), 0.0)
    attn_probs = low(weights / lax.optimization_barrier(jnp.sum(weights, axis=-1, keepdims=True)))
    mixed_rows = jnp.einsum('hqk,khe->qhe', attn_probs, values_here, precision=lax.Precision.HIGHEST)
    return mixed_rows.reshape(SEQ, HEADS * HEAD_DIM)

def reference(tokens, grad_out, w_qkv, w_attn_out, rel_bias, gain_attn, gain_ffn, w_router, w_in, w_down, expert_ids, doc_ids):
    target = expert_slots(expert_ids)
    chosen = expert_ids[:, 0].astype(jnp.int32)
    slots_total = EXPERTS * (TOKENS // TOK_DEV) * CAP
    doc_packs = doc_ids.reshape(-1, SEQ).astype(jnp.int32)

    def forward(tokens_f, qkv_weight, out_weight, table, gain_one, gain_two, router, in_weight, down_weight):
        scale_one = lax.rsqrt(lax.optimization_barrier(jnp.mean(tokens_f * tokens_f, axis=-1, keepdims=True)) + norm_eps)
        normed_one = low(tokens_f * scale_one * gain_one)
        qkv_rows = low(low_back(jnp.einsum('td,dch->tch', normed_one, qkv_weight, precision=lax.Precision.HIGHEST)))
        qkv_packs = qkv_rows.reshape(-1, SEQ, 3, HEADS * HEAD_DIM)

        def pack_mix(inputs):
            return attend_pack(inputs[0], inputs[1], table)
        mixed_packs = lax.map(jax.checkpoint(pack_mix), (qkv_packs, doc_packs))
        mixed_rows = low(low_back(mixed_packs.reshape(-1, HEADS * HEAD_DIM)))
        attn = low_back(jnp.einsum('te,de->td', mixed_rows, out_weight, precision=lax.Precision.HIGHEST))
        hidden = tokens_f + attn
        scale_two = lax.rsqrt(lax.optimization_barrier(jnp.mean(hidden * hidden, axis=-1, keepdims=True)) + norm_eps)
        normed_two = low(hidden * scale_two * gain_two)
        logits = jnp.dot(normed_two, router, precision=lax.Precision.HIGHEST)
        route = jax.nn.softmax(logits, axis=-1)
        selected = chosen[:, None] == jnp.arange(EXPERTS, dtype=jnp.int32)[None, :]
        gate_value = lax.optimization_barrier(jnp.sum(jnp.where(selected, route, 0.0), axis=-1))
        buffer = jnp.zeros((slots_total, D), normed_two.dtype).at[target].set(normed_two).reshape(EXPERTS, -1, D)
        expert_inner = low_back(jnp.einsum('erd,edf->erf', buffer, in_weight, precision=lax.Precision.HIGHEST))
        active = low(jax.nn.gelu(expert_inner, approximate=False))
        expert_out = low(low_back(jnp.einsum('erf,edf->erd', active, down_weight, precision=lax.Precision.HIGHEST)))
        returned = expert_out.reshape(slots_total, D)[target]
        return hidden + gate_value[:, None] * returned
    floats = (tokens.astype(jnp.float32), w_qkv.astype(jnp.float32), w_attn_out.astype(jnp.float32), rel_bias.astype(jnp.float32), gain_attn.astype(jnp.float32), gain_ffn.astype(jnp.float32), w_router.astype(jnp.float32), w_in.astype(jnp.float32), w_down.astype(jnp.float32))
    output, pull = jax.vjp(forward, *floats)
    grads = pull(grad_out.astype(jnp.float32))
    return (output.astype(jnp.bfloat16), grads[0], grads[1], grads[2], grads[3], grads[4], grads[5], grads[6], grads[7], grads[8])
```

```python
from functools import partial

import jax
import jax.numpy as jnp
from jax import lax
from jax.experimental import pallas as pl
from jax.experimental.pallas import tpu as pltpu
from jax.sharding import PartitionSpec as P

norm_eps = 1e-06
bucket_edges = (12, 16, 23, 32, 46, 64, 91)
LANES = 128
TILE = 128
MIB = 1024 * 1024
NT = (((1,), (1,)), ((), ()))
TN = (((0,), (0,)), ((), ()))


BQ = 256
BK = 256
HD = 64
NEG = -1e30
FLOOR = -1e28
F32 = jnp.float32
BF = jnp.bfloat16


def call(kernel, grid, in_specs, out_specs, out_shape, scratch=(), prefetch=0, vmem=48, name=None):
    return pl.pallas_call(
        kernel,
        grid_spec=pltpu.PrefetchScalarGridSpec(
            num_scalar_prefetch=prefetch,
            grid=grid,
            in_specs=in_specs,
            out_specs=out_specs,
            scratch_shapes=list(scratch),
        ),
        out_shape=out_shape,
        compiler_params=pltpu.CompilerParams(
            dimension_semantics=("arbitrary",) * len(grid), vmem_limit_bytes=vmem * MIB
        ),
        name=name,
    )


def whole(*shape):
    return pl.BlockSpec(shape, lambda *_: (0,) * len(shape))


def shaped(shape, dtype):
    return jax.ShapeDtypeStruct(shape, dtype)


def relative_bucket(offset):
    distance = jnp.abs(offset)
    far_bucket = jnp.zeros_like(distance) + 8
    for edge in bucket_edges:
        far_bucket = far_bucket + (distance >= edge).astype(jnp.int32)
    result = jnp.where(distance < 8, distance, far_bucket)
    return result + jnp.where(offset > 0, 16, 0)


def dot(a, b, dims=None):
    if dims is None:
        return jnp.dot(a, b, preferred_element_type=F32)
    return lax.dot_general(a, b, dims, preferred_element_type=F32)


def to_row(column):
    n = column.shape[0]
    return jnp.broadcast_to(column, (n, LANES)).T[0:1, :]


def to_column(row):
    n = row.shape[1]
    return jnp.broadcast_to(row, (LANES, n)).T[:, 0:1]


def split3(x):
    hi = x.astype(BF)
    rest = x - hi.astype(F32)
    mid = rest.astype(BF)
    low = (rest - mid.astype(F32)).astype(BF)
    return hi, mid, low


def key_side(docs_col, rows):
    lane = lax.broadcasted_iota(jnp.int32, (rows, HD), 1)
    same = (docs_col == lane).astype(F32)
    ones = jnp.where((lane >= 4) & (lane < 7), 1.0, 0.0)
    return jnp.where(lane < 4, same, ones)


def query_side(docs_row, cols, tail):
    row = lax.broadcasted_iota(jnp.int32, (HD, cols), 0)
    other = jnp.where((row < 4) & (docs_row != row), NEG, 0.0)
    if tail is None:
        return other.astype(BF)
    hi, mid, low = (t.astype(F32) for t in split3(tail))
    part = jnp.where(row == 4, hi, jnp.where(row == 5, mid, jnp.where(row == 6, low, 0.0)))
    return jnp.where(row < 4, other, part).astype(BF)


def shifted(x, by):
    return x if by == 0 else pltpu.roll(x, x.shape[1] - by, 1)


def diagonal_sums(tile):
    total = jnp.zeros((8, 2 * BQ), F32)
    for first in range(0, BK, 8):
        strip = tile[first : first + 8, :]
        total = total + shifted(jnp.concatenate([strip, jnp.zeros((8, BQ), F32)], axis=1), first)
    result = jnp.zeros((1, 2 * BQ), F32)
    for r in range(8):
        result = result + shifted(total, r)[r : r + 1, :]
    return result


def ones_rows(cols):
    return jnp.where(lax.broadcasted_iota(jnp.int32, (16, cols), 0) == 0, 1.0, 0.0).astype(BF)


def fwd_kernel(heads, info, far, qkv_all, q_ref, dcol, drow, band, mixed_ref, low_ref, lse_ref, k_aug, v_t):
    i = pl.program_id(0)
    seq = qkv_all.shape[0]
    width = heads * HD

    @pl.when(i == 0)
    def _():
        for r in range(seq // BK):
            rows = pl.ds(r * BK, BK)
            side = key_side(dcol[rows, :], BK).astype(BF)
            vt = qkv_all[rows, 2 * width : 3 * width].astype(F32).T.astype(BF)
            for h in range(heads):
                k = qkv_all[rows, width + h * HD : width + (h + 1) * HD]
                k_aug[h, rows, :] = jnp.concatenate([k, side], axis=1)
                v_t[h, 0:HD, rows] = vt[h * HD : (h + 1) * HD, :]
                v_t[h, HD : HD + 16, rows] = ones_rows(BK)

    qb = info[0] + i
    lo = info[1 + i]
    hi = info[1 + pl.num_programs(0) + i]
    qt = (q_ref[...].astype(F32) * (HD**-0.5)).T.astype(BF)
    side = query_side(drow[...], BQ, None)
    q_aug = [jnp.concatenate([qt[h * HD : (h + 1) * HD, :], side], axis=0) for h in range(heads)]

    def step(kb, carry, bias_of):
        rows = pl.ds(pl.multiple_of(kb * BK, BK), BK)
        out = []
        for h in range(heads):
            peak, acc = carry[h]
            s = jnp.dot(k_aug[h, rows, :], q_aug[h], preferred_element_type=F32)
            s = s + bias_of(h, kb)
            new = jnp.maximum(peak, jnp.max(s, axis=0, keepdims=True))
            p = jnp.exp(s - new).astype(BF)
            acc = acc * jnp.exp(peak - new) + jnp.dot(v_t[h, :, rows], p, preferred_element_type=F32)
            out.append((new, acc))
        return tuple(out)

    carry = tuple(
        (jnp.full((1, BQ), FLOOR, F32), jnp.zeros((HD + 16, BQ), F32)) for _ in range(heads)
    )
    carry = lax.fori_loop(lo, jnp.minimum(hi, qb - 1), lambda kb, c: step(kb, c, lambda h, _: far[0, h]), carry)
    carry = lax.fori_loop(
        jnp.maximum(lo, qb - 1),
        jnp.minimum(hi, qb + 2),
        lambda kb, c: step(kb, c, lambda h, t: band[h, t - qb + 1]),
        carry,
    )
    carry = lax.fori_loop(jnp.maximum(lo, qb + 2), hi, lambda kb, c: step(kb, c, lambda h, _: far[1, h]), carry)
    for h in range(heads):
        peak, acc = carry[h]
        total = acc[HD : HD + 1, :]
        mixed = acc[0:HD, :] / total
        mixed_ref[h * HD : (h + 1) * HD, :] = mixed
        low_ref[h * HD : (h + 1) * HD, :] = mixed.astype(BF)
        lse_ref[h : h + 1, :] = peak + jnp.log(total)


def attention_fwd(info, far, qkv_all, dcol, drow, band, rows):
    seq, cols = qkv_all.shape
    width = cols // 3
    heads = width // HD
    steps = rows // BQ
    full = lambda shape: pl.BlockSpec(shape, lambda i, info: (0,) * len(shape))
    return pl.pallas_call(
        partial(fwd_kernel, heads),
        grid_spec=pltpu.PrefetchScalarGridSpec(
            num_scalar_prefetch=1,
            grid=(steps,),
            in_specs=[
                pl.BlockSpec(memory_space=pltpu.SMEM),
                full((seq, cols)),
                pl.BlockSpec((BQ, width), lambda i, info: (info[0] + i, 0)),
                full((seq, 1)),
                pl.BlockSpec((1, BQ), lambda i, info: (0, info[0] + i)),
                full((heads, 3, BK, BQ)),
            ],
            out_specs=[
                pl.BlockSpec((width, BQ), lambda i, info: (0, i)),
                pl.BlockSpec((width, BQ), lambda i, info: (0, i)),
                pl.BlockSpec((heads, BQ), lambda i, info: (0, i)),
            ],
            scratch_shapes=[
                pltpu.VMEM((heads, seq, 2 * HD), BF),
                pltpu.VMEM((heads, HD + 16, seq), BF),
            ],
        ),
        out_shape=[
            jax.ShapeDtypeStruct((width, rows), F32),
            jax.ShapeDtypeStruct((width, rows), BF),
            jax.ShapeDtypeStruct((heads, rows), F32),
        ],
        compiler_params=pltpu.CompilerParams(
            dimension_semantics=("arbitrary",), vmem_limit_bytes=40 * 1024 * 1024
        ),
        name="attention_fwd",
    )(info, far, qkv_all, qkv_all[:, 0:width], dcol, drow, band)


def bwd_kernel(
    heads, info, far, qkv_all, q_ref, dcol, drow, band, mixed_ref, lse_ref, dmix_ref,
    dq_ref, dkv_ref, skew_ref, side_ref, k_aug, v_aug, k_t, near_acc, dkv_acc,
):
    i = pl.program_id(0)
    seq = qkv_all.shape[0]
    width = heads * HD

    @pl.when(i == 0)
    def _():
        near_acc[...] = jnp.zeros_like(near_acc)
        dkv_acc[...] = jnp.zeros_like(dkv_acc)
        side_ref[...] = jnp.zeros_like(side_ref)
        for r in range(seq // BK):
            rows = pl.ds(r * BK, BK)
            side = key_side(dcol[rows, :], BK).astype(BF)
            lane = lax.broadcasted_iota(jnp.int32, (BK, HD), 1)
            ones = jnp.where(lane < 3, 1.0, 0.0).astype(BF)
            kt = qkv_all[rows, width : 2 * width].astype(F32).T.astype(BF)
            for h in range(heads):
                k = qkv_all[rows, width + h * HD : width + (h + 1) * HD]
                v = qkv_all[rows, 2 * width + h * HD : 2 * width + (h + 1) * HD]
                k_aug[h, rows, :] = jnp.concatenate([k, side], axis=1)
                v_aug[h, rows, :] = jnp.concatenate([v, ones], axis=1)
                k_t[h, 0:HD, rows] = kt[h * HD : (h + 1) * HD, :]
                k_t[h, HD : HD + 16, rows] = ones_rows(BK)

    qb = info[0] + i
    lo = info[1 + i]
    hi = info[1 + pl.num_programs(0) + i]
    q_scaled = q_ref[...].astype(F32) * (HD**-0.5)
    qt = q_scaled.T.astype(BF)
    q_rows = q_scaled.astype(BF)
    dmix_t = dmix_ref[...].astype(F32)
    dmix_rows = dmix_t.T.astype(BF)
    zero = jnp.zeros((BQ, HD), BF)
    row = lax.broadcasted_iota(jnp.int32, (HD, BQ), 0)
    q_aug, d_aug, rhs = [], [], []
    for h in range(heads):
        cols = slice(h * HD, (h + 1) * HD)
        lse = lse_ref[h : h + 1, :]
        kinds = []
        for tail in (far[0, h] - lse, -lse, far[1, h] - lse):
            kinds.append(jnp.concatenate([qt[cols, :], query_side(drow[...], BQ, tail)], axis=0))
        q_aug.append(kinds)
        delta = -jnp.sum(dmix_t[cols, :] * mixed_ref[cols, :], axis=0, keepdims=True)
        a, b, c = (t.astype(F32) for t in split3(delta))
        part = jnp.where(row == 0, a, jnp.where(row == 1, b, jnp.where(row == 2, c, 0.0)))
        d_aug.append(jnp.concatenate([dmix_t[cols, :].astype(BF), part.astype(BF)], axis=0))
        top = jnp.concatenate([dmix_rows[:, cols], zero], axis=1)
        low = jnp.concatenate([zero, q_rows[:, cols]], axis=1)
        rhs.append(jnp.concatenate([top, low], axis=0))

    def step(kb, carry, kind):
        rows = pl.ds(pl.multiple_of(kb * BK, BK), BK)
        out = []
        for h in range(heads):
            s = jnp.dot(k_aug[h, rows, :], q_aug[h][kind], preferred_element_type=F32)
            if kind == 1:
                s = s + band[h, kb - qb + 1]
            p = jnp.exp(s)
            dp = jnp.dot(v_aug[h, rows, :], d_aug[h], preferred_element_type=F32)
            ds = p * dp
            ds_low = ds.astype(BF)
            if kind == 1:
                near_acc[h, kb - qb + 1] = near_acc[h, kb - qb + 1] + ds_low.astype(F32)
            both = jnp.concatenate([p.astype(BF), ds_low], axis=1)
            dkv_acc[h, rows, :] += jnp.dot(both, rhs[h], preferred_element_type=F32)
            out.append(carry[h] + jnp.dot(k_t[h, :, rows], ds_low, preferred_element_type=F32))
        return tuple(out)

    zero_dq = jnp.zeros((HD + 16, BQ), F32)
    left = lax.fori_loop(lo, jnp.minimum(hi, qb - 1), lambda kb, c: step(kb, c, 0), (zero_dq,) * heads)
    near = lax.fori_loop(
        jnp.maximum(lo, qb - 1), jnp.minimum(hi, qb + 2), lambda kb, c: step(kb, c, 1), left
    )
    last = lax.fori_loop(jnp.maximum(lo, qb + 2), hi, lambda kb, c: step(kb, c, 2), near)
    for h in range(heads):
        dq_ref[h * HD : (h + 1) * HD, :] = (last[h][0:HD, :] * (HD**-0.5)).astype(BF)
        side_ref[2 * h : 2 * h + 1, :] += left[h][HD : HD + 1, :]
        side_ref[2 * h + 1 : 2 * h + 2, :] += last[h][HD : HD + 1, :] - near[h][HD : HD + 1, :]

    @pl.when(i == pl.num_programs(0) - 1)
    def _():
        for h in range(heads):
            for t in range(3):
                skew_ref[3 * h + t : 3 * h + t + 1, :] = diagonal_sums(near_acc.at[h, t])
        for r in range(seq // BK):
            rows = pl.ds(r * BK, BK)
            acc = [dkv_acc[h, rows, :] for h in range(heads)]
            dk = [a[:, HD : 2 * HD] for a in acc]
            dv = [a[:, 0:HD] for a in acc]
            dkv_ref[rows, :] = jnp.concatenate(dk + dv, axis=1).astype(BF)


def attention_bwd(info, far, qkv_all, dcol, drow, band, mixed, lse, dmix, rows):
    seq, cols = qkv_all.shape
    width = cols // 3
    heads = width // HD
    steps = rows // BQ
    full = lambda shape: pl.BlockSpec(shape, lambda i, info: (0,) * len(shape))
    return pl.pallas_call(
        partial(bwd_kernel, heads),
        grid_spec=pltpu.PrefetchScalarGridSpec(
            num_scalar_prefetch=1,
            grid=(steps,),
            in_specs=[
                pl.BlockSpec(memory_space=pltpu.SMEM),
                full((seq, cols)),
                pl.BlockSpec((BQ, width), lambda i, info: (info[0] + i, 0)),
                full((seq, 1)),
                pl.BlockSpec((1, BQ), lambda i, info: (0, info[0] + i)),
                full((heads, 3, BK, BQ)),
                pl.BlockSpec((width, BQ), lambda i, info: (0, i)),
                pl.BlockSpec((heads, BQ), lambda i, info: (0, i)),
                pl.BlockSpec((None, width, BQ), lambda i, info: (i, 0, 0)),
            ],
            out_specs=[
                pl.BlockSpec((width, BQ), lambda i, info: (0, i)),
                full((seq, 2 * width)),
                full((16, 2 * BK)),
                full((8, BQ)),
            ],
            scratch_shapes=[
                pltpu.VMEM((heads, seq, 2 * HD), BF),
                pltpu.VMEM((heads, seq, 2 * HD), BF),
                pltpu.VMEM((heads, HD + 16, seq), BF),
                pltpu.VMEM((heads, 3, BK, BQ), F32),
                pltpu.VMEM((heads, seq, 2 * HD), F32),
            ],
        ),
        out_shape=[
            jax.ShapeDtypeStruct((width, rows), BF),
            jax.ShapeDtypeStruct((seq, 2 * width), BF),
            jax.ShapeDtypeStruct((16, 2 * BK), F32),
            jax.ShapeDtypeStruct((8, BQ), F32),
        ],
        compiler_params=pltpu.CompilerParams(
            dimension_semantics=("arbitrary",), vmem_limit_bytes=56 * 1024 * 1024
        ),
        name="attention_bwd",
    )(info, far, qkv_all, qkv_all[:, 0:width], dcol, drow, band, mixed, lse, dmix)


def band_kernel(vec_ref, band_ref):
    heads = band_ref.shape[0]
    for h in range(heads):
        for t in range(3):
            wide = jnp.broadcast_to(vec_ref[3 * h + t : 3 * h + t + 1, :], (BK, 2 * BQ))
            band_ref[h, t] = pltpu.roll(wide, 0, 1, stride=1, stride_axis=0)[:, 0:BQ]


def qkv_kernel(tok_ref, gain_ref, w_ref, qkv_ref, norm_ref, scale_ref):
    x = tok_ref[...].astype(F32)
    scale = lax.rsqrt(jnp.mean(x * x, axis=-1, keepdims=True) + norm_eps)
    normed = (x * scale * gain_ref[...].astype(F32)).astype(BF)
    norm_ref[...] = normed
    scale_ref[...] = scale
    qkv_ref[...] = dot(normed, w_ref[...]).astype(BF)


def router_parts(hidden, gain, router, chosen, experts):
    scale = lax.rsqrt(jnp.mean(hidden * hidden, axis=-1, keepdims=True) + norm_eps)
    hat = hidden * scale
    normed = (hat * gain).astype(BF)
    lane = lax.broadcasted_iota(jnp.int32, (hidden.shape[0], LANES), 1)
    logits = jnp.where(lane < experts, dot(normed, router), NEG)
    weights = jnp.exp(logits - jnp.max(logits, axis=-1, keepdims=True))
    route = weights / jnp.sum(weights, axis=-1, keepdims=True)
    one_hot = jnp.where(lane == chosen, 1.0, 0.0)
    gate = jnp.sum(route * one_hot, axis=-1, keepdims=True)
    return scale, hat, normed, route, one_hot, gate


def hidden_kernel(
    experts, tok_ref, mixed_ref, wout_ref, gain_ref, router_ref, chosen_ref,
    hidden_ref, norm_ref, gate_ref,
):
    attn = dot(mixed_ref[...], wout_ref[...], TN)
    hidden = tok_ref[...].astype(F32) + attn
    parts = router_parts(hidden, gain_ref[...].astype(F32), router_ref[...], chosen_ref[...], experts)
    hidden_ref[...] = hidden
    norm_ref[...] = parts[2]
    gate_ref[...] = to_row(parts[5])


def expert_kernel(
    groups, owner, pos_row, pos_col, norm_ref, cot_ref, gate_ref, w_ref,
    back_ref, eo_ref, x_ref, de_ref, act_ref, di_ref, eo_s, dr_s,
):
    i = pl.program_id(0)
    rows = norm_ref.shape[0]
    width = norm_ref.shape[1]
    ff = w_ref.shape[1] // 2
    place = lax.broadcasted_iota(jnp.int32, (TILE, rows), 0) + i * TILE
    hit = pos_row[...] == place
    pick = jnp.where(hit, 1.0, 0.0).astype(BF)
    x = dot(pick, norm_ref[...]).astype(BF)
    cot = dot(pick, cot_ref[...])
    gate = jnp.sum(jnp.where(hit, gate_ref[...], 0.0), axis=1, keepdims=True)
    d_e = (gate * cot).astype(BF)
    w_in = w_ref[:, 0:ff]
    w_down = w_ref[:, ff : 2 * ff]
    inner = dot(x, w_in)
    half = 0.5 * (1.0 + lax.erf(inner * (0.5**0.5)))
    active = (inner * half).astype(BF)
    slope = half + inner * (jnp.exp(-0.5 * inner * inner) * 0.3989422804014327)
    d_inner = (dot(d_e, w_down) * slope).astype(BF)
    terms = dot(active, w_down, NT)
    d_rows = dot(d_inner, w_in, NT)
    d_gate = jnp.sum(cot * terms, axis=1, keepdims=True)
    lane = lax.broadcasted_iota(jnp.int32, (TILE, LANES), 1)
    hi, mid, low = (t.astype(F32) for t in split3(d_gate))
    extra = jnp.where(lane == 0, hi, jnp.where(lane == 1, mid, jnp.where(lane == 2, low, 0.0)))
    here = pl.ds(pl.multiple_of(i * TILE, TILE), TILE)
    eo_s[here, :] = terms.astype(BF)
    dr_s[here, :] = jnp.concatenate([d_rows.astype(BF), extra.astype(BF)], axis=1)
    x_ref[...] = x
    de_ref[...] = d_e
    act_ref[...] = active
    di_ref[...] = d_inner

    @pl.when(i == pl.num_programs(0) - 1)
    def _():
        total = dr_s.shape[0]
        part = rows // groups
        for g in range(groups):
            mine = pl.ds(g * part, part)
            place = lax.broadcasted_iota(jnp.int32, (part, total), 1)
            pick = jnp.where(pos_col[mine, :] == place, 1.0, 0.0).astype(BF)
            back = dot(pick, dr_s[...])
            back_ref[g, 0:part, :] = back[:, 0:width].astype(BF)
            tail = back[:, width : width + LANES].T
            d_gate = tail[0:1, :] + tail[1:2, :] + tail[2:3, :]
            row = lax.broadcasted_iota(jnp.int32, (16, part), 0)
            strip = jnp.where(row == 0, jnp.broadcast_to(d_gate, (16, part)), 0.0)
            fill = jnp.zeros((16, width - part), F32)
            back_ref[g, part : part + 16, :] = jnp.concatenate([strip, fill], axis=1).astype(BF)
            eo_ref[:, mine] = dot(pick, eo_s[...]).T.astype(BF)


def weight_grad_kernel(owner, x_ref, di_ref, de_ref, act_ref, out_ref, acc):
    i = pl.program_id(0)
    last = pl.num_programs(0) - 1
    me = owner[i]
    before = owner[jnp.maximum(i - 1, 0)]
    after = owner[jnp.minimum(i + 1, last)]
    ff = di_ref.shape[1]

    @pl.when((i == 0) | (before != me))
    def _():
        acc[...] = jnp.zeros_like(acc)

    acc[:, 0:ff] += dot(x_ref[...], di_ref[...], TN)
    acc[:, ff : 2 * ff] += dot(de_ref[...], act_ref[...], TN)

    @pl.when((i == last) | (after != me))
    def _():
        out_ref[...] = acc[...].astype(BF)


def hidden_back_kernel(
    experts, info, back_ref, hidden_ref, cot_ref, gain_ref, router_ref, chosen_ref, wout_ref, mixed_ref,
    dh_ref, dmix_ref, small_ref, gout_ref,
):
    part = hidden_ref.shape[0]
    gain = gain_ref[...].astype(F32)
    scale, hat, normed, route, one_hot, gate = router_parts(
        hidden_ref[...], gain, router_ref[...], chosen_ref[...], experts
    )
    d_gate = to_column(back_ref[part : part + 16, 0:part].astype(F32)[0:1, :])
    d_logits = (d_gate * gate) * (one_hot - route)
    parts = split3(d_logits)
    d_normed = back_ref[0:part, :].astype(F32)
    for p in parts:
        d_normed = d_normed + dot(p, router_ref[...], NT)
    g_router = jnp.zeros((LANES, hat.shape[1]), F32)
    for p in parts:
        g_router = g_router + dot(p, normed, TN)
    small_ref[0:experts, :] = g_router[0:experts, :]
    small_ref[experts : experts + 1, :] = jnp.sum(d_normed * hat, axis=0, keepdims=True)
    if small_ref.shape[0] > experts + 1:
        small_ref[experts + 1 :, :] = jnp.zeros(
            (small_ref.shape[0] - experts - 1, hat.shape[1]), F32
        )
    d_hat = d_normed * gain
    d_hidden = cot_ref[...].astype(F32) + scale * (
        d_hat - hat * jnp.mean(d_hat * hat, axis=-1, keepdims=True)
    )
    d_attn = d_hidden.astype(BF)
    dmix_ref[...] = dot(wout_ref[...], d_attn, NT).astype(BF)
    dh_ref[...] = d_hidden.T.astype(BF)
    gout_ref[...] = dot(mixed_ref[...], d_attn).astype(BF)


def qkv_back_kernel(
    groups, info, dq_ref, dkv_ref, got_ref, norm_ref, tok_ref, scale_ref, gain_ref, w_ref,
    terms_ref, gw_ref, gain_out_ref, acc,
):
    i = pl.program_id(0)
    width = dq_ref.shape[0]
    dkv = dkv_ref[...].astype(F32) + got_ref[...].astype(F32)
    d_qkv = jnp.concatenate([dq_ref[...].astype(F32).T, dkv], axis=1).astype(BF)
    hat = tok_ref[...].astype(F32) * scale_ref[...]
    terms = dot(d_qkv, w_ref[...], NT)
    weighted = terms * hat
    mean = jnp.mean(weighted * gain_ref[...].astype(F32), axis=-1, keepdims=True)

    @pl.when(i == 0)
    def _():
        acc[...] = jnp.zeros_like(acc)
        gain_out_ref[...] = jnp.zeros_like(gain_out_ref)

    gain_out_ref[0:1, :] += jnp.sum(weighted, axis=0, keepdims=True)
    acc[...] += dot(norm_ref[...], d_qkv, TN)
    flat = terms.T.astype(BF)
    mean_row = to_row(mean)
    hi, mid, low = (t.astype(F32) for t in split3(mean_row))
    row = lax.broadcasted_iota(jnp.int32, (16, mean_row.shape[1]), 0)
    strip = jnp.where(row == 0, hi, jnp.where(row == 1, mid, jnp.where(row == 2, low, 0.0))).astype(BF)
    for g in range(groups):
        terms_ref[g, 0:width, :] = flat[g * width : (g + 1) * width, :]
        terms_ref[g, width : width + 16, :] = strip

    @pl.when(i == pl.num_programs(0) - 1)
    def _():
        gw_ref[...] = acc[...].astype(gw_ref.dtype)


def token_grad_kernel(info, sum_ref, dh_ref, tok_ref, scale_ref, gain_ref, out_ref):
    width = dh_ref.shape[0]
    mean = jnp.sum(sum_ref[width : width + 16, :].astype(F32), axis=0, keepdims=True)
    terms = sum_ref[0:width, :].astype(F32)
    d_hat = terms.T * gain_ref[...].astype(F32)
    scale = scale_ref[...]
    hat = tok_ref[...].astype(F32) * scale
    out_ref[...] = dh_ref[...].astype(F32).T + scale * (d_hat - hat * to_column(mean))


def out_kernel(eo_ref, hidden_ref, gate_ref, out_ref):
    out_ref[...] = (hidden_ref[...] + (eo_ref[...].astype(F32) * gate_ref[...]).T).astype(BF)


def placement(chosen, experts, tiles):
    rows = chosen.shape[0]
    ids = jnp.arange(experts, dtype=jnp.int32)
    one_hot = chosen[:, None] == ids[None, :]
    below = jnp.arange(rows)[:, None] > jnp.arange(rows)[None, :]
    earlier = dot(below.astype(BF), one_hot.astype(BF)).astype(jnp.int32)
    count = jnp.sum(one_hot.astype(jnp.int32), axis=0)
    used = jnp.maximum((count + TILE - 1) // TILE, 1)
    ends = jnp.sum(jnp.where(ids[None, :] <= ids[:, None], used[None, :], 0), axis=1)
    first = (ends - used) * TILE
    pos = jnp.sum(jnp.where(one_hot, earlier + first[None, :], 0), axis=1).astype(jnp.int32)
    tile_ids = jnp.arange(tiles, dtype=jnp.int32)
    owner = jnp.sum((ends[None, :] <= tile_ids[:, None]).astype(jnp.int32), axis=1)
    return pos, jnp.minimum(owner, experts - 1).astype(jnp.int32)


def shards(
    tokens,
    grad_out,
    w_qkv,
    w_attn_out,
    rel_bias,
    gain_attn,
    gain_ffn,
    w_router,
    w_in,
    w_down,
    expert_ids,
    doc_ids,
):
    rows, model = tokens.shape
    heads = rel_bias.shape[1]
    width = w_qkv.shape[2]
    own = w_qkv.shape[0]
    experts = w_router.shape[1]
    ff = w_in.shape[2]
    seq = doc_ids.shape[0]
    ctx_n = lax.axis_size("ctx")
    tp_n = lax.axis_size("tp")
    ctx_at = lax.axis_index("ctx")
    tp_at = lax.axis_index("tp")
    dense_at = lax.axis_index("fsdp") * ctx_n + ctx_at
    part = rows // tp_n
    share = model // tp_n
    blocks = rows // BQ
    dense = ("fsdp", "ctx")

    small = jnp.concatenate(
        (
            w_qkv.reshape(own, 3 * width),
            w_attn_out,
            w_router,
            gain_attn[:, None],
            gain_ffn[:, None],
            jnp.zeros((own, LANES - experts - 2), BF),
        ),
        axis=1,
    )
    small_all = lax.all_gather(small, dense, axis=0, tiled=True)
    tokens_all = lax.all_gather(tokens, "ctx", axis=0, tiled=True)
    half = model // ctx_n
    w_both = jnp.concatenate((w_in.reshape(-1, ff), w_down.reshape(-1, ff)), axis=1)
    w_half = lax.dynamic_slice_in_dim(w_both, ctx_at * half, half, 0)
    w_experts = lax.all_gather(w_half, dense, axis=0, tiled=True)
    qkv_full = small_all[:, 0 : 3 * width]
    out_mine = small_all[:, 3 * width : 4 * width]
    tail = small_all[:, 4 * width :]
    gain_one = tail[:, experts][None, :]
    gain_two = tail[:, experts + 1][None, :]
    router = jnp.where(jnp.arange(LANES)[None, :] < experts, tail, jnp.zeros_like(tail))
    out_t = lax.all_gather(out_mine.T, "tp", axis=0, tiled=True)

    chosen = expert_ids[:, 0]
    tiles = rows // TILE + experts - 1
    pos, owner = placement(chosen, experts, tiles)
    docs_row = doc_ids[None, :]
    docs_col = doc_ids[:, None]
    firsts = lax.dynamic_slice_in_dim(doc_ids.reshape(-1, BQ)[:, 0], ctx_at * blocks, blocks)
    lasts = lax.dynamic_slice_in_dim(doc_ids.reshape(-1, BQ)[:, BQ - 1], ctx_at * blocks, blocks)
    low = jnp.sum((docs_row < firsts[:, None]).astype(jnp.int32), axis=1) // BK
    high = (jnp.sum((docs_row <= lasts[:, None]).astype(jnp.int32), axis=1) + BK - 1) // BK
    info = jnp.concatenate(((ctx_at * blocks)[None], low, high)).astype(jnp.int32)
    wrapped = jnp.arange(2 * BQ, dtype=jnp.int32)
    wrapped = jnp.where(wrapped < BQ, wrapped, wrapped - 2 * BQ)
    offsets = (jnp.arange(3, dtype=jnp.int32)[:, None] - 1) * BK - wrapped[None, :]
    selector = relative_bucket(offsets)[:, :, None] == jnp.arange(rel_bias.shape[0])[None, None, :]
    selector = selector.astype(F32)
    vectors = jnp.einsum("tcb,bh->htc", selector, rel_bias, precision=lax.Precision.HIGHEST)
    far = jnp.stack((rel_bias[15], rel_bias[31]))
    band = call(
        band_kernel,
        (1,),
        [whole(3 * heads, 2 * BQ)],
        whole(heads, 3, BK, BQ),
        shaped((heads, 3, BK, BQ), F32),
        name="bias_band",
    )(vectors.reshape(3 * heads, 2 * BQ))

    qkv_all, normed_one, scale_one = call(
        qkv_kernel,
        (seq // BQ,),
        [pl.BlockSpec((BQ, model), lambda i: (i, 0)), whole(1, model), whole(model, 3 * width)],
        [
            pl.BlockSpec((BQ, 3 * width), lambda i: (i, 0)),
            pl.BlockSpec((BQ, model), lambda i: (i, 0)),
            pl.BlockSpec((BQ, 1), lambda i: (i, 0)),
        ],
        [shaped((seq, 3 * width), BF), shaped((seq, model), BF), shaped((seq, 1), F32)],
        name="norm_qkv",
    )(tokens_all, gain_one, qkv_full)
    mixed, mixed_low, lse = attention_fwd(info, far, qkv_all, docs_col, docs_row, band, rows)
    mixed_all = lax.all_gather(mixed_low, "tp", axis=0, tiled=True)

    chosen_col = expert_ids
    hidden, normed_two, gate_row = call(
        partial(hidden_kernel, experts),
        (blocks,),
        [
            pl.BlockSpec((BQ, model), lambda i: (i, 0)),
            pl.BlockSpec((model, BQ), lambda i: (0, i)),
            whole(model, model),
            whole(1, model),
            whole(model, LANES),
            pl.BlockSpec((BQ, 1), lambda i: (i, 0)),
        ],
        [
            pl.BlockSpec((BQ, model), lambda i: (i, 0)),
            pl.BlockSpec((BQ, model), lambda i: (i, 0)),
            pl.BlockSpec((1, BQ), lambda i: (0, i)),
        ],
        [shaped((rows, model), F32), shaped((rows, model), BF), shaped((1, rows), F32)],
        name="hidden_router",
    )(tokens, mixed_all, out_t, gain_two, router, chosen_col)
    sorted_rows = tiles * TILE
    sorted_spec = lambda cols: pl.BlockSpec((TILE, cols), lambda i, owner: (i, 0))
    back, eo_t, x_sorted, d_expert, active, d_inner = call(
        partial(expert_kernel, tp_n),
        (tiles,),
        [
            whole(1, rows),
            whole(rows, 1),
            whole(rows, model),
            whole(rows, model),
            whole(1, rows),
            pl.BlockSpec((model, 2 * ff), lambda i, owner: (owner[i], 0)),
        ],
        [
            whole(tp_n, part + 16, model),
            whole(model, rows),
            sorted_spec(model),
            sorted_spec(model),
            sorted_spec(ff),
            sorted_spec(ff),
        ],
        [
            shaped((tp_n, part + 16, model), BF),
            shaped((model, rows), BF),
            shaped((sorted_rows, model), BF),
            shaped((sorted_rows, model), BF),
            shaped((sorted_rows, ff), BF),
            shaped((sorted_rows, ff), BF),
        ],
        scratch=[pltpu.VMEM((sorted_rows, model), BF), pltpu.VMEM((sorted_rows, model + LANES), BF)],
        prefetch=1,
        name="experts",
    )(owner, pos[None, :], pos[:, None], normed_two, grad_out, gate_row, w_experts)
    back_mine = lax.psum_scatter(
        back.reshape(tp_n * (part + 16), model), "tp", scatter_dimension=0, tiled=True
    )
    grad_experts = call(
        weight_grad_kernel,
        (tiles,),
        [sorted_spec(model), sorted_spec(ff), sorted_spec(model), sorted_spec(ff)],
        pl.BlockSpec((model, 2 * ff), lambda i, owner: (owner[i], 0)),
        shaped((experts * model, 2 * ff), BF),
        scratch=[pltpu.VMEM((model, 2 * ff), F32)],
        prefetch=1,
        name="expert_weight_grads",
    )(owner, x_sorted, d_inner, d_expert, active)

    at = jnp.stack((tp_at, ctx_at * blocks)).astype(jnp.int32)
    small_rows = -(-(experts + 1) // 8) * 8
    row_block = pl.BlockSpec((part, model), lambda i, at: (at[0], 0))
    dh_t, dmix_t, small_grads, grad_out_t = call(
        partial(hidden_back_kernel, experts),
        (1,),
        [
            whole(part + 16, model),
            row_block,
            row_block,
            whole(1, model),
            whole(model, LANES),
            pl.BlockSpec((part, 1), lambda i, at: (at[0], 0)),
            whole(model, model),
            pl.BlockSpec((model, part), lambda i, at: (0, at[0])),
        ],
        [whole(model, part), whole(model, part), whole(small_rows, model), whole(model, model)],
        [
            shaped((model, part), BF),
            shaped((model, part), BF),
            shaped((small_rows, model), F32),
            shaped((model, model), BF),
        ],
        prefetch=1,
        name="hidden_back",
    )(at, back_mine, hidden, grad_out, gain_two, router, chosen_col, out_t, mixed_all)
    dmix = lax.all_to_all(dmix_t.reshape(tp_n, width, part), "tp", 0, 0)
    dh = lax.all_to_all(dh_t.reshape(tp_n, width, part), "tp", 0, 0)
    grad_experts_mine = lax.psum_scatter(grad_experts, dense, scatter_dimension=0, tiled=True)
    eo_mine = lax.psum_scatter(eo_t, "tp", scatter_dimension=0, tiled=True)
    grad_out_tp = lax.psum_scatter(grad_out_t, "tp", scatter_dimension=0, tiled=True)
    small_sums = lax.psum(small_grads, ("fsdp", "ctx", "tp"))

    dq_t, dkv, skew, sides = attention_bwd(
        info, far, qkv_all, docs_col, docs_row, band, mixed, lse, dmix, rows
    )
    if ctx_n == 2:
        other = lax.dynamic_slice_in_dim(dkv, (1 - ctx_at) * rows, rows)
        got = lax.ppermute(other, "ctx", [(0, 1), (1, 0)])
        mine = lax.dynamic_slice_in_dim(dkv, ctx_at * rows, rows)
    else:
        mine = lax.psum_scatter(dkv, "ctx", scatter_dimension=0, tiled=True)
        got = jnp.zeros_like(mine)
    terms, grad_qkv, gain_sum = call(
        partial(qkv_back_kernel, tp_n),
        (blocks,),
        [
            pl.BlockSpec((width, BQ), lambda i, at: (0, i)),
            pl.BlockSpec((BQ, 2 * width), lambda i, at: (i, 0)),
            pl.BlockSpec((BQ, 2 * width), lambda i, at: (i, 0)),
            pl.BlockSpec((BQ, model), lambda i, at: (at[1] + i, 0)),
            pl.BlockSpec((BQ, model), lambda i, at: (i, 0)),
            pl.BlockSpec((BQ, 1), lambda i, at: (at[1] + i, 0)),
            whole(1, model),
            whole(model, 3 * width),
        ],
        [
            pl.BlockSpec((tp_n, width + 16, BQ), lambda i, at: (0, 0, i)),
            whole(model, 3 * width),
            whole(8, model),
        ],
        [
            shaped((tp_n, width + 16, rows), BF),
            shaped((model, 3 * width), BF),
            shaped((8, model), F32),
        ],
        scratch=[pltpu.VMEM((model, 3 * width), F32)],
        prefetch=1,
        name="qkv_back",
    )(at, dq_t, mine, got, normed_one, tokens, scale_one, gain_one, qkv_full)
    terms_mine = lax.psum_scatter(
        terms.reshape(tp_n * (width + 16), rows), "tp", scatter_dimension=0, tiled=True
    )
    grad_dense = lax.psum_scatter(
        jnp.concatenate((grad_qkv, grad_out_tp.T), axis=1), dense, scatter_dimension=0, tiled=True
    ).astype(F32)

    diagonals = skew[0 : 3 * heads].reshape(heads, 3, 2 * BQ)
    table = jnp.einsum("htc,tcb->bh", diagonals, selector, precision=lax.Precision.HIGHEST)
    side = jnp.sum(sides[0 : 2 * heads], axis=1).reshape(heads, 2)
    bucket_ids = jnp.arange(rel_bias.shape[0])[:, None]
    table = table + jnp.where(bucket_ids == 15, side[None, :, 0], 0.0)
    table = table + jnp.where(bucket_ids == 31, side[None, :, 1], 0.0)
    slots = jnp.where(jnp.arange(tp_n)[:, None] == tp_at, table.reshape(1, -1), 0.0)
    late = jnp.concatenate((gain_sum[0], slots.reshape(-1)))
    late_sums = lax.psum(late, ("fsdp", "ctx", "tp"))
    table_all = late_sums[model:].reshape(tp_n, rel_bias.shape[0], heads)
    table_mine = lax.dynamic_index_in_dim(table_all, tp_at, 0, keepdims=False)
    table_rows = rel_bias.shape[0] // (lax.axis_size("fsdp") * ctx_n)
    grad_table = lax.dynamic_slice_in_dim(table_mine, dense_at * table_rows, table_rows)
    grad_gain_one = lax.dynamic_slice_in_dim(late_sums[:model], dense_at * own, own)
    small_mine = lax.dynamic_slice_in_dim(small_sums, dense_at * own, own, 1)
    grad_router = small_mine[0:experts].T
    grad_gain_two = small_mine[experts]

    columns = tp_at * share
    hidden_share = lax.dynamic_slice_in_dim(hidden, columns, share, 1)
    tokens_share = lax.dynamic_slice_in_dim(tokens, columns, share, 1)
    gain_share = lax.dynamic_slice_in_dim(gain_one, columns, share, 1)
    out_share = call(
        out_kernel,
        (blocks,),
        [
            pl.BlockSpec((share, BQ), lambda i: (0, i)),
            pl.BlockSpec((BQ, share), lambda i: (i, 0)),
            pl.BlockSpec((1, BQ), lambda i: (0, i)),
        ],
        pl.BlockSpec((BQ, share), lambda i: (i, 0)),
        shaped((rows, share), BF),
        name="layer_output",
    )(eo_mine, hidden_share, gate_row)
    grad_tokens = call(
        token_grad_kernel,
        (tp_n,),
        [
            pl.BlockSpec((width + 16, part), lambda i, at: (0, i)),
            pl.BlockSpec((None, width, part), lambda i, at: (i, 0, 0)),
            pl.BlockSpec((part, share), lambda i, at: (i, 0)),
            pl.BlockSpec((part, 1), lambda i, at: (at[0] + i, 0)),
            whole(1, share),
        ],
        pl.BlockSpec((part, share), lambda i, at: (i, 0)),
        shaped((rows, share), F32),
        prefetch=1,
        name="token_grads",
    )((ctx_at * tp_n)[None].astype(jnp.int32), terms_mine, dh, tokens_share, scale_one, gain_share)
    grad_experts_f = grad_experts_mine.astype(F32)
    return (
        out_share,
        grad_tokens,
        grad_dense[:, 0 : 3 * width].reshape(own, 3, width),
        grad_dense[:, 3 * width :],
        grad_table,
        grad_gain_one,
        grad_gain_two,
        grad_router,
        grad_experts_f[None, :, 0:ff],
        grad_experts_f[None, :, ff:],
    )


def solution(mesh):
    placed = (
        P(("fsdp", "ctx"), None),
        P(("fsdp", "ctx"), None),
        P(("fsdp", "ctx"), None, "tp"),
        P(("fsdp", "ctx"), "tp"),
        P(None, "tp"),
        P(("fsdp", "ctx")),
        P(("fsdp", "ctx")),
        P(("fsdp", "ctx"), None),
        P("fsdp", None, "tp"),
        P("fsdp", None, "tp"),
        P(("fsdp", "ctx"), None),
        P("fsdp"),
    )
    return jax.shard_map(
        shards,
        mesh=mesh,
        in_specs=placed,
        out_specs=(
            P(("fsdp", "ctx"), "tp"),
            P(("fsdp", "ctx"), "tp"),
            P(("fsdp", "ctx"), None, "tp"),
            P(("fsdp", "ctx"), "tp"),
            P(("fsdp", "ctx"), "tp"),
            P(("fsdp", "ctx")),
            P(("fsdp", "ctx")),
            P(("fsdp", "ctx"), None),
            P("fsdp", "ctx", "tp"),
            P("fsdp", "ctx", "tp"),
        ),
        check_vma=False,
    )
```

```python
from functools import partial

import jax
import jax.numpy as jnp
from jax import lax
from jax.experimental import pallas as pl
from jax.experimental.pallas import tpu as pltpu
from jax.sharding import PartitionSpec as P

norm_eps = 1e-06
bucket_edges = (12, 16, 23, 32, 46, 64, 91)
LANES = 128
TILE = 128
MIB = 1024 * 1024
NT = (((1,), (1,)), ((), ()))
TN = (((0,), (0,)), ((), ()))


BQ = 256
BK = 256
HD = 64
NEG = -1e30
FLOOR = -1e28
F32 = jnp.float32
BF = jnp.bfloat16


def call(kernel, grid, in_specs, out_specs, out_shape, scratch=(), prefetch=0, vmem=58, name=None, us=1):
    return pl.pallas_call(
        kernel,
        grid_spec=pltpu.PrefetchScalarGridSpec(
            num_scalar_prefetch=prefetch,
            grid=grid,
            in_specs=in_specs,
            out_specs=out_specs,
            scratch_shapes=list(scratch),
        ),
        out_shape=out_shape,
        compiler_params=pltpu.CompilerParams(
            dimension_semantics=("arbitrary",) * len(grid), vmem_limit_bytes=vmem * MIB
        ),
        cost_estimate=pl.CostEstimate(
            flops=int(us * 1e9), bytes_accessed=int(us * 3e6), transcendentals=0
        ),
        name=name,
    )


def whole(*shape):
    return pl.BlockSpec(shape, lambda *_: (0,) * len(shape))


def shaped(shape, dtype):
    return jax.ShapeDtypeStruct(shape, dtype)


def relative_bucket(offset):
    distance = jnp.abs(offset)
    far_bucket = jnp.zeros_like(distance) + 8
    for edge in bucket_edges:
        far_bucket = far_bucket + (distance >= edge).astype(jnp.int32)
    result = jnp.where(distance < 8, distance, far_bucket)
    return result + jnp.where(offset > 0, 16, 0)


def dot(a, b, dims=None):
    if dims is None:
        return jnp.dot(a, b, preferred_element_type=F32)
    return lax.dot_general(a, b, dims, preferred_element_type=F32)


def to_row(column):
    n = column.shape[0]
    return jnp.broadcast_to(column, (n, LANES)).T[0:1, :]


def to_column(row):
    n = row.shape[1]
    return jnp.broadcast_to(row, (LANES, n)).T[:, 0:1]


def split3(x):
    hi = x.astype(BF)
    rest = x - hi.astype(F32)
    mid = rest.astype(BF)
    low = (rest - mid.astype(F32)).astype(BF)
    return hi, mid, low


def key_side(docs_col, rows):
    lane = lax.broadcasted_iota(jnp.int32, (rows, HD), 1)
    same = (docs_col == lane.astype(F32)).astype(F32)
    ones = jnp.where((lane >= 4) & (lane < 7), 1.0, 0.0)
    return jnp.where(lane < 4, same, ones)


def query_side(docs_row, cols, tail):
    row = lax.broadcasted_iota(jnp.int32, (HD, cols), 0)
    other = jnp.where((row < 4) & (docs_row != row.astype(F32)), NEG, 0.0)
    if tail is None:
        return other.astype(BF)
    hi, mid, low = (t.astype(F32) for t in split3(tail))
    part = jnp.where(row == 4, hi, jnp.where(row == 5, mid, jnp.where(row == 6, low, 0.0)))
    return jnp.where(row < 4, other, part).astype(BF)


def shifted(x, by):
    return x if by == 0 else pltpu.roll(x, x.shape[1] - by, 1)


def diagonal_sums(tile):
    total = jnp.zeros((8, 2 * BQ), F32)
    for first in range(0, BK, 8):
        strip = tile[first : first + 8, :]
        total = total + shifted(jnp.concatenate([strip, jnp.zeros((8, BQ), F32)], axis=1), first)
    result = jnp.zeros((1, 2 * BQ), F32)
    for r in range(8):
        result = result + shifted(total, r)[r : r + 1, :]
    return result


def ones_rows(cols):
    return jnp.where(lax.broadcasted_iota(jnp.int32, (16, cols), 0) == 0, 1.0, 0.0).astype(BF)


def fwd_kernel(heads, info, far, qkv_all, dcol, drow, band, mixed_ref, low_ref, lse_ref, k_aug, v_t):
    i = pl.program_id(0)
    seq = qkv_all.shape[0]
    width = heads * HD

    @pl.when(i == 0)
    def _():
        for r in range(seq // BK):
            rows = pl.ds(r * BK, BK)
            side = key_side(to_column(dcol[:, r * BK : (r + 1) * BK]), BK).astype(BF)
            vt = qkv_all[rows, 2 * width : 3 * width].astype(F32).T.astype(BF)
            for h in range(heads):
                k = qkv_all[rows, width + h * HD : width + (h + 1) * HD]
                k_aug[h, rows, :] = jnp.concatenate([k, side], axis=1)
                v_t[h, 0:HD, rows] = vt[h * HD : (h + 1) * HD, :]
                v_t[h, HD : HD + 16, rows] = ones_rows(BK)

    qb = info[0] + i
    lo = info[1 + i]
    hi = info[1 + pl.num_programs(0) + i]
    qt = (qkv_all[pl.ds(pl.multiple_of(qb * BQ, BQ), BQ), 0:width].astype(F32) * (HD**-0.5)).T.astype(BF)
    side = query_side(drow[...], BQ, None)
    q_aug = [jnp.concatenate([qt[h * HD : (h + 1) * HD, :], side], axis=0) for h in range(heads)]

    def step(kb, carry, bias_of):
        rows = pl.ds(pl.multiple_of(kb * BK, BK), BK)
        out = []
        for h in range(heads):
            peak, acc = carry[h]
            s = jnp.dot(k_aug[h, rows, :], q_aug[h], preferred_element_type=F32)
            s = s + bias_of(h, kb)
            new = jnp.maximum(peak, jnp.max(s, axis=0, keepdims=True))
            p = jnp.exp(s - new).astype(BF)
            acc = acc * jnp.exp(peak - new) + jnp.dot(v_t[h, :, rows], p, preferred_element_type=F32)
            out.append((new, acc))
        return tuple(out)

    carry = tuple(
        (jnp.full((1, BQ), FLOOR, F32), jnp.zeros((HD + 16, BQ), F32)) for _ in range(heads)
    )
    carry = lax.fori_loop(lo, jnp.minimum(hi, qb - 1), lambda kb, c: step(kb, c, lambda h, _: far[0, h]), carry)
    carry = lax.fori_loop(
        jnp.maximum(lo, qb - 1),
        jnp.minimum(hi, qb + 2),
        lambda kb, c: step(kb, c, lambda h, t: band[h, t - qb + 1]),
        carry,
    )
    carry = lax.fori_loop(jnp.maximum(lo, qb + 2), hi, lambda kb, c: step(kb, c, lambda h, _: far[1, h]), carry)
    for h in range(heads):
        peak, acc = carry[h]
        total = acc[HD : HD + 1, :]
        mixed = acc[0:HD, :] / total
        mixed_ref[h * HD : (h + 1) * HD, :] = mixed
        low_ref[h * HD : (h + 1) * HD, :] = mixed.astype(BF)
        lse_ref[h : h + 1, :] = peak + jnp.log(total)


def attention_fwd(info, far, qkv_all, dcol, drow, band, rows):
    seq, cols = qkv_all.shape
    width = cols // 3
    heads = width // HD
    steps = rows // BQ
    full = lambda shape: pl.BlockSpec(shape, lambda i, info: (0,) * len(shape))
    return pl.pallas_call(
        partial(fwd_kernel, heads),
        grid_spec=pltpu.PrefetchScalarGridSpec(
            num_scalar_prefetch=1,
            grid=(steps,),
            in_specs=[
                pl.BlockSpec(memory_space=pltpu.SMEM),
                full((seq, cols)),
                full((1, seq)),
                pl.BlockSpec((1, BQ), lambda i, info: (0, info[0] + i)),
                full((heads, 3, BK, BQ)),
            ],
            out_specs=[
                pl.BlockSpec((width, BQ), lambda i, info: (0, i)),
                pl.BlockSpec((width, BQ), lambda i, info: (0, i)),
                pl.BlockSpec((heads, BQ), lambda i, info: (0, i)),
            ],
            scratch_shapes=[
                pltpu.VMEM((heads, seq, 2 * HD), BF),
                pltpu.VMEM((heads, HD + 16, seq), BF),
            ],
        ),
        out_shape=[
            jax.ShapeDtypeStruct((width, rows), F32),
            jax.ShapeDtypeStruct((width, rows), BF),
            jax.ShapeDtypeStruct((heads, rows), F32),
        ],
        compiler_params=pltpu.CompilerParams(
            dimension_semantics=("arbitrary",), vmem_limit_bytes=58 * 1024 * 1024
        ),
        cost_estimate=pl.CostEstimate(
            flops=int(19 * 1e9), bytes_accessed=int(19 * 3e6), transcendentals=0
        ),
        name="attention_fwd",
    )(info, far, qkv_all, dcol, drow, band)


def bwd_kernel(
    heads, info, far, qkv_all, dcol, drow, band, mixed_ref, lse_ref, m0, m1, m2, m3,
    dq_ref, dkv_ref, skew_ref, side_ref, k_aug, v_aug, k_t, near_acc, dkv_acc,
):
    i = pl.program_id(0)
    seq = qkv_all.shape[0]
    width = heads * HD

    @pl.when(i == 0)
    def _():
        near_acc[...] = jnp.zeros_like(near_acc)
        dkv_acc[...] = jnp.zeros_like(dkv_acc)
        side_ref[...] = jnp.zeros_like(side_ref)
        for r in range(seq // BK):
            rows = pl.ds(r * BK, BK)
            side = key_side(to_column(dcol[:, r * BK : (r + 1) * BK]), BK).astype(BF)
            lane = lax.broadcasted_iota(jnp.int32, (BK, HD), 1)
            ones = jnp.where(lane < 3, 1.0, 0.0).astype(BF)
            kt = qkv_all[rows, width : 2 * width].astype(F32).T.astype(BF)
            for h in range(heads):
                k = qkv_all[rows, width + h * HD : width + (h + 1) * HD]
                v = qkv_all[rows, 2 * width + h * HD : 2 * width + (h + 1) * HD]
                k_aug[h, rows, :] = jnp.concatenate([k, side], axis=1)
                v_aug[h, rows, :] = jnp.concatenate([v, ones], axis=1)
                k_t[h, 0:HD, rows] = kt[h * HD : (h + 1) * HD, :]
                k_t[h, HD : HD + 16, rows] = ones_rows(BK)

    steps = pl.num_programs(0)
    block = lax.rem(info[1 + 2 * steps] + steps - i, steps)
    qb = info[0] + block
    lo = info[1 + block]
    hi = info[1 + steps + block]
    dmix = m0[...]
    for s, ref in ((1, m1), (2, m2), (3, m3)):
        dmix = jnp.where(i == s, ref[...], dmix)
    q_scaled = qkv_all[pl.ds(pl.multiple_of(qb * BQ, BQ), BQ), 0:width].astype(F32) * (HD**-0.5)
    qt = q_scaled.T.astype(BF)
    q_rows = q_scaled.astype(BF)
    dmix_t = dmix.astype(F32)
    dmix_rows = dmix_t.T.astype(BF)
    zero = jnp.zeros((BQ, HD), BF)
    row = lax.broadcasted_iota(jnp.int32, (HD, BQ), 0)
    q_aug, d_aug, rhs = [], [], []
    for h in range(heads):
        cols = slice(h * HD, (h + 1) * HD)
        lse = lse_ref[h : h + 1, :]
        kinds = []
        for tail in (far[0, h] - lse, -lse, far[1, h] - lse):
            kinds.append(jnp.concatenate([qt[cols, :], query_side(drow[...], BQ, tail)], axis=0))
        q_aug.append(kinds)
        delta = -jnp.sum(dmix_t[cols, :] * mixed_ref[cols, :], axis=0, keepdims=True)
        a, b, c = (t.astype(F32) for t in split3(delta))
        part = jnp.where(row == 0, a, jnp.where(row == 1, b, jnp.where(row == 2, c, 0.0)))
        d_aug.append(jnp.concatenate([dmix_t[cols, :].astype(BF), part.astype(BF)], axis=0))
        top = jnp.concatenate([dmix_rows[:, cols], zero], axis=1)
        low = jnp.concatenate([zero, q_rows[:, cols]], axis=1)
        rhs.append(jnp.concatenate([top, low], axis=0))

    def step(kb, carry, kind):
        rows = pl.ds(pl.multiple_of(kb * BK, BK), BK)
        out = []
        for h in range(heads):
            s = jnp.dot(k_aug[h, rows, :], q_aug[h][kind], preferred_element_type=F32)
            if kind == 1:
                s = s + band[h, kb - qb + 1]
            p = jnp.exp(s)
            dp = jnp.dot(v_aug[h, rows, :], d_aug[h], preferred_element_type=F32)
            ds = p * dp
            ds_low = ds.astype(BF)
            if kind == 1:
                near_acc[h, kb - qb + 1] = near_acc[h, kb - qb + 1] + ds_low.astype(F32)
            both = jnp.concatenate([p.astype(BF), ds_low], axis=1)
            dkv_acc[h, rows, :] += jnp.dot(both, rhs[h], preferred_element_type=F32)
            out.append(carry[h] + jnp.dot(k_t[h, :, rows], ds_low, preferred_element_type=F32))
        return tuple(out)

    zero_dq = jnp.zeros((HD + 16, BQ), F32)
    left = lax.fori_loop(lo, jnp.minimum(hi, qb - 1), lambda kb, c: step(kb, c, 0), (zero_dq,) * heads)
    near = lax.fori_loop(
        jnp.maximum(lo, qb - 1), jnp.minimum(hi, qb + 2), lambda kb, c: step(kb, c, 1), left
    )
    last = lax.fori_loop(jnp.maximum(lo, qb + 2), hi, lambda kb, c: step(kb, c, 2), near)
    for h in range(heads):
        dq_ref[h * HD : (h + 1) * HD, :] = (last[h][0:HD, :] * (HD**-0.5)).astype(BF)
        side_ref[2 * h : 2 * h + 1, :] += left[h][HD : HD + 1, :]
        side_ref[2 * h + 1 : 2 * h + 2, :] += last[h][HD : HD + 1, :] - near[h][HD : HD + 1, :]

    @pl.when(i == pl.num_programs(0) - 1)
    def _():
        for h in range(heads):
            for t in range(3):
                skew_ref[3 * h + t : 3 * h + t + 1, :] = diagonal_sums(near_acc.at[h, t])
        for r in range(seq // BK):
            rows = pl.ds(r * BK, BK)
            acc = [dkv_acc[h, rows, :] for h in range(heads)]
            dk = [a[:, HD : 2 * HD] for a in acc]
            dv = [a[:, 0:HD] for a in acc]
            dkv_ref[rows, :] = jnp.concatenate(dk + dv, axis=1).astype(BF)


def attention_bwd(info, far, qkv_all, dcol, drow, band, mixed, lse, dmix, rows):
    seq, cols = qkv_all.shape
    width = cols // 3
    heads = width // HD
    steps = rows // BQ
    full = lambda shape: pl.BlockSpec(shape, lambda i, info: (0,) * len(shape))
    block = lambda i, info: lax.rem(info[1 + 2 * steps] + steps - i, steps)
    return pl.pallas_call(
        partial(bwd_kernel, heads),
        grid_spec=pltpu.PrefetchScalarGridSpec(
            num_scalar_prefetch=1,
            grid=(steps,),
            in_specs=[
                pl.BlockSpec(memory_space=pltpu.SMEM),
                full((seq, cols)),
                full((1, seq)),
                pl.BlockSpec((1, BQ), lambda i, info: (0, info[0] + block(i, info))),
                full((heads, 3, BK, BQ)),
                pl.BlockSpec((width, BQ), lambda i, info: (0, block(i, info))),
                pl.BlockSpec((heads, BQ), lambda i, info: (0, block(i, info))),
                *[full((width, BQ))] * 4,
            ],
            out_specs=[
                pl.BlockSpec((width, BQ), lambda i, info: (0, block(i, info))),
                full((seq, 2 * width)),
                full((16, 2 * BK)),
                full((8, BQ)),
            ],
            scratch_shapes=[
                pltpu.VMEM((heads, seq, 2 * HD), BF),
                pltpu.VMEM((heads, seq, 2 * HD), BF),
                pltpu.VMEM((heads, HD + 16, seq), BF),
                pltpu.VMEM((heads, 3, BK, BQ), F32),
                pltpu.VMEM((heads, seq, 2 * HD), F32),
            ],
        ),
        out_shape=[
            jax.ShapeDtypeStruct((width, rows), BF),
            jax.ShapeDtypeStruct((seq, 2 * width), BF),
            jax.ShapeDtypeStruct((16, 2 * BK), F32),
            jax.ShapeDtypeStruct((8, BQ), F32),
        ],
        compiler_params=pltpu.CompilerParams(
            dimension_semantics=("arbitrary",), vmem_limit_bytes=58 * 1024 * 1024
        ),
        cost_estimate=pl.CostEstimate(
            flops=int(24 * 1e9), bytes_accessed=int(24 * 3e6), transcendentals=0
        ),
        name="attention_bwd",
    )(info, far, qkv_all, dcol, drow, band, mixed, lse, *dmix)


def band_kernel(vec_ref, band_ref):
    heads = band_ref.shape[0]
    for h in range(heads):
        for t in range(3):
            wide = jnp.broadcast_to(vec_ref[3 * h + t : 3 * h + t + 1, :], (BK, 2 * BQ))
            band_ref[h, t] = pltpu.roll(wide, 0, 1, stride=1, stride_axis=0)[:, 0:BQ]


def pack_kernel(qkv_ref, router_ref, one_ref, two_ref, out_ref):
    experts, rows = router_ref.shape
    fill = jnp.zeros((LANES - experts - 2, rows), F32)
    tail = [r[...].astype(F32) for r in (router_ref, one_ref, two_ref)]
    tail = jnp.concatenate([*tail, fill], axis=0).T.astype(BF)
    out_ref[...] = jnp.concatenate([*(qkv_ref[c] for c in range(3)), tail], axis=1)


def qkv_kernel(
    cols, experts, count, at, own_ref, other_ref, *refs
):
    pieces = refs[:count]
    qkv_ref, norm_ref, scale_ref, small_ref, gains_ref = refs[count:]
    i = pl.program_id(0)

    @pl.when(i == 0)
    def _():
        slot = 0
        for piece in pieces:
            for s in range(piece.shape[0]):
                first = pl.multiple_of(at[slot], 16)
                small_ref[pl.ds(first, piece.shape[1]), :] = piece[s]
                slot += 1
        tail = small_ref[:, cols:].astype(F32).T
        gains_ref[...] = tail[experts : experts + 8, :]

    x = jnp.where(i < pl.num_programs(0) // 2, own_ref[...], other_ref[...]).astype(F32)
    scale = lax.rsqrt(jnp.mean(x * x, axis=-1, keepdims=True) + norm_eps)
    normed = (x * scale * gains_ref[0:1, :]).astype(BF)
    norm_ref[...] = normed
    scale_ref[...] = to_row(scale)
    qkv_ref[...] = dot(normed, small_ref[:, 0:cols]).astype(BF)


def router_parts(hidden, gain, router, chosen, experts):
    scale = lax.rsqrt(jnp.mean(hidden * hidden, axis=-1, keepdims=True) + norm_eps)
    hat = hidden * scale
    normed = (hat * gain).astype(BF)
    lane = lax.broadcasted_iota(jnp.int32, (hidden.shape[0], LANES), 1)
    logits = jnp.where(lane < experts, dot(normed, router), NEG)
    weights = jnp.exp(logits - jnp.max(logits, axis=-1, keepdims=True))
    route = weights / jnp.sum(weights, axis=-1, keepdims=True)
    one_hot = jnp.where(lane.astype(F32) == chosen, 1.0, 0.0)
    gate = jnp.sum(route * one_hot, axis=-1, keepdims=True)
    return scale, hat, normed, route, one_hot, gate


def hidden_kernel(experts, at, *refs):
    tok_ref, mix_refs, wout_ref = refs[0], refs[1:5], refs[5]
    gains_ref, small_ref, chosen_ref, hidden_ref, norm_ref, gate_ref = refs[6:]
    mixed = jnp.concatenate([r[...] for r in mix_refs], axis=0)
    both = mixed.astype(F32).T.astype(BF)
    hidden = tok_ref[...].astype(F32) + dot(both, wout_ref[...], NT)
    parts = router_parts(hidden, gains_ref[1:2, :], small_ref[...], to_column(chosen_ref[...]), experts)
    hidden_ref[...] = hidden
    norm_ref[...] = parts[2]
    gate_ref[...] = to_row(parts[5])


def expert_kernel(
    owner, at, pos_row, norm_ref, cot_ref, gate_ref, w_ref,
    b0, b1, b2, b3, eo_ref, x_ref, de_ref, act_ref, di_ref, eo_s, dr_s, pos_col,
):
    i = pl.program_id(0)
    z = at[0]
    rows = norm_ref.shape[0]
    width = norm_ref.shape[1]
    ff = w_ref.shape[1] // 2
    place = lax.broadcasted_iota(jnp.int32, (TILE, rows), 0) + i * TILE
    hit = pos_row[...] == place
    pick = jnp.where(hit, 1.0, 0.0).astype(BF)
    x = dot(pick, norm_ref[...]).astype(BF)
    cot = dot(pick, cot_ref[...])
    gate = jnp.sum(jnp.where(hit, gate_ref[...], 0.0), axis=1, keepdims=True)
    d_e = (gate * cot).astype(BF)
    w_in = w_ref[:, 0:ff]
    w_down = w_ref[:, ff : 2 * ff]
    inner = dot(x, w_in)
    half = 0.5 * (1.0 + lax.erf(inner * (0.5**0.5)))
    active = (inner * half).astype(BF)
    slope = half + inner * (jnp.exp(-0.5 * inner * inner) * 0.3989422804014327)
    d_inner = (dot(d_e, w_down) * slope).astype(BF)
    terms = dot(active, w_down, NT)
    d_rows = dot(d_inner, w_in, NT)
    d_gate = jnp.sum(cot * terms, axis=1, keepdims=True)
    lane = lax.broadcasted_iota(jnp.int32, (TILE, LANES), 1)
    hi, mid, low = (t.astype(F32) for t in split3(d_gate))
    extra = jnp.where(lane == 0, hi, jnp.where(lane == 1, mid, jnp.where(lane == 2, low, 0.0)))
    here = pl.ds(pl.multiple_of(i * TILE, TILE), TILE)
    eo_s[here, :] = terms.astype(BF)
    dr_s[here, :] = jnp.concatenate([d_rows.astype(BF), extra.astype(BF)], axis=1)
    x_ref[...] = x
    de_ref[...] = d_e
    act_ref[...] = active
    di_ref[...] = d_inner

    @pl.when(i == pl.num_programs(0) - 1)
    def _():
        total = dr_s.shape[0]
        part = rows // 4
        pos_col[...] = jnp.broadcast_to(pos_row[...].astype(F32), (LANES, rows)).T
        for r, back_ref in enumerate((b0, b1, b2, b3)):
            g = lax.rem(z + r, 4)
            mine = pl.ds(pl.multiple_of(g * part, part), part)
            place = lax.broadcasted_iota(jnp.int32, (part, total), 1).astype(F32)
            pick = jnp.where(pos_col[mine, 0:1] == place, 1.0, 0.0).astype(BF)
            back = dot(pick, dr_s[...])
            back_ref[0:part, :] = back[:, 0:width].astype(BF)
            tail = back[:, width : width + LANES].T
            d_gate = tail[0:1, :] + tail[1:2, :] + tail[2:3, :]
            row = lax.broadcasted_iota(jnp.int32, (16, part), 0)
            strip = jnp.where(row == 0, jnp.broadcast_to(d_gate, (16, part)), 0.0)
            fill = jnp.zeros((16, width - part), F32)
            back_ref[part : part + 16, :] = jnp.concatenate([strip, fill], axis=1).astype(BF)
            eo_ref[:, mine] = dot(pick, eo_s[...]).T.astype(BF)


def weight_grad_kernel(owner, slot, at, rows_ref, cols_ref, keep_ref, send_ref, acc):
    i = pl.program_id(0)
    last = pl.num_programs(0) - 1
    me = owner[i]
    before = owner[jnp.maximum(i - 1, 0)]
    after = owner[jnp.minimum(i + 1, last)]

    @pl.when((i == 0) | (before != me))
    def _():
        acc[...] = jnp.zeros_like(acc)

    acc[...] += dot(rows_ref[...], cols_ref[...], TN)

    @pl.when((i == last) | (after != me))
    def _():
        half = keep_ref.shape[0]
        keep_ref[...] = acc[pl.ds(pl.multiple_of(at[1] * half, half), half), :].astype(BF)
        send_ref[...] = acc[pl.ds(pl.multiple_of((1 - at[1]) * half, half), half), :].astype(BF)


def split_rows(at, first_slot, acc, outs):
    if len(outs) == 1:
        outs[0][...] = acc[...].astype(BF)
        return
    slot = first_slot
    for out in outs:
        step = out.shape[0] // 4
        for s in range(4):
            first = pl.multiple_of(at[slot], 8)
            out[s * step : (s + 1) * step, :] = acc[pl.ds(first, step), :].astype(BF)
            slot += 1


def hidden_back_kernel(experts, at, *refs):
    back_refs, (hidden_ref, cot_ref, gains_ref, router_ref, chosen_ref) = refs[:4], refs[4:9]
    wout_ref, mix_refs = refs[9], refs[10:14]
    dmix_refs, dh_ref, small_ref, gout_ref = refs[14:18], refs[18], refs[19], refs[20]
    part, model = hidden_ref.shape
    back = sum(r[...].astype(F32) for r in back_refs)
    gain = gains_ref[1:2, :]
    router = router_ref[...]
    scale, hat, normed, route, one_hot, gate = router_parts(
        hidden_ref[...], gain, router, to_column(chosen_ref[...]), experts
    )
    d_gate = to_column(back[part : part + 1, 0:part])
    d_logits = (d_gate * gate) * (one_hot - route)
    parts = split3(d_logits)
    d_normed = back[0:part, :]
    g_router = jnp.zeros((LANES, model), F32)
    for p in parts:
        d_normed = d_normed + dot(p, router, NT)
        g_router = g_router + dot(p, normed, TN)
    small_ref[...] = jnp.zeros_like(small_ref)
    small_ref[0:experts, :] = g_router[0:experts, :]
    small_ref[experts : experts + 1, :] = jnp.sum(d_normed * hat, axis=0, keepdims=True)
    d_hat = d_normed * gain
    d_hidden = cot_ref[...].astype(F32) + scale * (
        d_hat - hat * jnp.mean(d_hat * hat, axis=-1, keepdims=True)
    )
    d_attn = d_hidden.astype(BF)
    d_attn_t = d_hidden.T.astype(BF)
    d_mixed = dot(d_attn, wout_ref[...]).T.astype(BF)
    width = model // 4
    for s in range(4):
        r = (4 - s) % 4
        dmix_refs[r][...] = d_mixed[s * width : (s + 1) * width, :]
    dh_ref[...] = d_hidden
    mixed = jnp.concatenate([r[...] for r in mix_refs], axis=0)
    gout_ref[...] = dot(d_attn_t, mixed, NT)


def qkv_back_kernel(
    at, dq_ref, dkv_ref, got_ref, norm_ref, tok_ref, scale_ref, gains_ref, w_ref, dh_ref, gout_ref,
    terms_ref, gain_out_ref, *rest,
):
    *gw_refs, acc = rest
    i = pl.program_id(0)
    width = dq_ref.shape[0]
    dkv = dkv_ref[...].astype(F32) + got_ref[...].astype(F32)
    d_qkv = jnp.concatenate([dq_ref[...].astype(F32).T, dkv], axis=1).astype(BF)
    scale = to_column(scale_ref[...])
    hat = tok_ref[...].astype(F32) * scale
    terms = dot(d_qkv, w_ref[:, 0 : 3 * width], NT)
    d_hat = terms * gains_ref[0:1, :]
    mean = jnp.mean(d_hat * hat, axis=-1, keepdims=True)
    grad = scale * (d_hat - hat * mean) + jnp.where(i == at[0], dh_ref[...], 0.0)

    @pl.when(i == 0)
    def _():
        acc[:, 0 : 3 * width] = jnp.zeros((acc.shape[0], 3 * width), F32)
        acc[:, 3 * width :] = gout_ref[...]
        gain_out_ref[...] = jnp.zeros_like(gain_out_ref)

    gain_out_ref[0:1, :] += jnp.sum(terms * hat, axis=0, keepdims=True)
    acc[:, 0 : 3 * width] += dot(norm_ref[...], d_qkv, TN)
    terms_ref[...] = grad.T.astype(BF)

    @pl.when(i == pl.num_programs(0) - 1)
    def _():
        split_rows(at, 4, acc, gw_refs)


def out_kernel(eo_ref, hidden_ref, gate_ref, out_ref):
    out_ref[...] = (hidden_ref[...] + eo_ref[...].astype(F32) * gate_ref[...]).astype(BF)


def placement(chosen, experts, tiles):
    rows = chosen.shape[0]
    ids = jnp.arange(experts, dtype=jnp.int32)
    one_hot = chosen[:, None] == ids[None, :]
    below = jnp.arange(rows)[:, None] > jnp.arange(rows)[None, :]
    earlier = dot(below.astype(BF), one_hot.astype(BF)).astype(jnp.int32)
    count = jnp.sum(one_hot.astype(jnp.int32), axis=0)
    used = jnp.maximum((count + TILE - 1) // TILE, 1)
    ends = jnp.sum(jnp.where(ids[None, :] <= ids[:, None], used[None, :], 0), axis=1)
    first = (ends - used) * TILE
    pos = jnp.sum(jnp.where(one_hot, earlier + first[None, :], 0), axis=1).astype(jnp.int32)
    tile_ids = jnp.arange(tiles, dtype=jnp.int32)
    owner = jnp.sum((ends[None, :] <= tile_ids[:, None]).astype(jnp.int32), axis=1)
    return pos, jnp.minimum(owner, experts - 1).astype(jnp.int32)


def xor_step(x, axis, s):
    return lax.ppermute(x, axis, [(i, i ^ s) for i in range(lax.axis_size(axis))])


def turn(x, s):
    return lax.ppermute(x, "tp", [(i, (i + s) % 4) for i in range(4)])


def gather_turns(x):
    return [x] + [turn(x, s) for s in (1, 2, 3)]


def scatter_turns(pieces):
    return [pieces[0]] + [turn(pieces[r], r) for r in (1, 2, 3)]


def after(x, *others):
    return lax.optimization_barrier((x, others))[0]


def dense_scatter(parts):
    if len(parts) == 1:
        return lax.psum_scatter(parts[0], ("fsdp", "ctx"), scatter_dimension=0, tiled=True).astype(F32)
    keep, send = parts
    both = keep + xor_step(send, "ctx", 1)
    step = keep.shape[0] // 4
    total = both[0:step].astype(F32)
    for s in (1, 2, 3):
        total = total + xor_step(both[s * step : (s + 1) * step], "fsdp", s).astype(F32)
    return total


def sum_all(x):
    if lax.axis_size("fsdp") != 4 or lax.axis_size("ctx") != 2:
        return lax.psum(x, ("fsdp", "ctx", "tp"))
    x = x + xor_step(x, "ctx", 1)
    x = x + xor_step(x, "fsdp", 1) + xor_step(x, "fsdp", 2) + xor_step(x, "fsdp", 3)
    return x + turn(x, 1) + turn(x, 2) + turn(x, 3)


def shards(
    tokens,
    grad_out,
    w_qkv,
    w_attn_out,
    rel_bias,
    gain_attn,
    gain_ffn,
    w_router,
    w_in,
    w_down,
    expert_ids,
    doc_ids,
):
    rows, model = tokens.shape
    heads = rel_bias.shape[1]
    width = w_qkv.shape[2]
    own = w_qkv.shape[0]
    experts = w_router.shape[1]
    ff = w_in.shape[2]
    seq = doc_ids.shape[0]
    fsdp_n = lax.axis_size("fsdp")
    ctx_n = lax.axis_size("ctx")
    tp_n = lax.axis_size("tp")
    fsdp_at = lax.axis_index("fsdp")
    ctx_at = lax.axis_index("ctx")
    tp_at = lax.axis_index("tp")
    dense_at = fsdp_at * ctx_n + ctx_at
    part = rows // tp_n
    share = model // tp_n
    blocks = rows // BQ
    dense = ("fsdp", "ctx")
    square = fsdp_n == 4 and ctx_n == 2

    qkv_cols = 3 * width
    cols = qkv_cols + LANES
    small = call(
        pack_kernel,
        (1,),
        [whole(3, own, width), whole(experts, own), whole(1, own), whole(1, own)],
        whole(own, cols),
        shaped((own, cols), BF),
        name="pack_small",
    )(w_qkv.transpose(1, 0, 2), w_router.T, gain_attn[None, :], gain_ffn[None, :])
    half = model // ctx_n
    mine_rows = lambda at: jnp.concatenate(
        [lax.dynamic_slice_in_dim(w.reshape(-1, ff), at * half, half, 0) for w in (w_in, w_down)], axis=1
    )
    if square:
        near = jnp.stack([small] + [xor_step(small, "fsdp", s) for s in (1, 2, 3)])
        small_parts = [near, xor_step(near, "ctx", 1)]
        starts = [((fsdp_at ^ s) * 2 + c) * own for c in (ctx_at, 1 - ctx_at) for s in range(4)]
    else:
        small_parts = [lax.all_gather(small, dense, axis=0, tiled=True)[None]]
        starts = [jnp.int32(0)]
    tokens_other = xor_step(tokens, "ctx", 1)
    out_line = jnp.concatenate(gather_turns(w_attn_out), axis=1)
    out_all = lax.all_gather(out_line, dense, axis=0, tiled=True)
    w_half = mine_rows(ctx_at)

    tiles = (rows + experts * (TILE - 1)) // TILE
    pos, owner = placement(expert_ids[:, 0], experts, tiles)
    pos = pos[None, :]
    chosen = expert_ids[:, 0].astype(F32)[None, :]
    docs = doc_ids.astype(F32)[None, :]
    firsts = lax.dynamic_slice_in_dim(doc_ids.reshape(-1, BQ)[:, 0], ctx_at * blocks, blocks)
    lasts = lax.dynamic_slice_in_dim(doc_ids.reshape(-1, BQ)[:, BQ - 1], ctx_at * blocks, blocks)
    low = jnp.sum((doc_ids[None, :] < firsts[:, None]).astype(jnp.int32), axis=1) // BK
    high = (jnp.sum((doc_ids[None, :] <= lasts[:, None]).astype(jnp.int32), axis=1) + BK - 1) // BK
    info = jnp.concatenate(((ctx_at * blocks)[None], low, high, tp_at[None])).astype(jnp.int32)
    wrapped = jnp.arange(2 * BQ, dtype=jnp.int32)
    wrapped = jnp.where(wrapped < BQ, wrapped, wrapped - 2 * BQ)
    offsets = (jnp.arange(3, dtype=jnp.int32)[:, None] - 1) * BK - wrapped[None, :]
    selector = relative_bucket(offsets)[:, :, None] == jnp.arange(rel_bias.shape[0])[None, None, :]
    selector = selector.astype(F32)
    vectors = jnp.einsum("tcb,bh->htc", selector, rel_bias, precision=lax.Precision.HIGHEST)
    far = jnp.stack((rel_bias[15], rel_bias[31]))
    band = call(
        band_kernel,
        (1,),
        [whole(3 * heads, 2 * BQ)],
        whole(heads, 3, BK, BQ),
        shaped((heads, 3, BK, BQ), F32),
        name="bias_band",
    )(vectors.reshape(3 * heads, 2 * BQ))
    columns = tp_at * share
    starts = [s.astype(jnp.int32) for s in starts]
    at = jnp.stack([tp_at, ctx_at, ctx_at * blocks, fsdp_at] + starts).astype(jnp.int32)
    starts = jnp.stack(starts + [ctx_at * blocks]).astype(jnp.int32)
    early = (w_half, pos, owner, chosen, docs, info, band, far, at, starts, selector)
    (small_parts, tokens_other, early) = lax.optimization_barrier((small_parts, tokens_other, early))
    w_half, pos, owner, chosen, docs, info, band, far, at, starts, selector = early

    w_experts = lax.all_gather(w_half, dense, axis=0, tiled=True)
    slot = owner ^ fsdp_at if square else owner
    slot = slot.astype(jnp.int32)

    steps = seq // BQ
    n_own = steps // 2
    base = lambda i, at: at[len_starts] + i
    len_starts = starts.shape[0] - 1
    turned = lambda i, at: jnp.where(i < n_own, at[len_starts] + i, n_own - at[len_starts] + i - n_own)
    qkv_all, normed_one, scale_one, small_all, gains = call(
        partial(qkv_kernel, qkv_cols, experts, len(small_parts)),
        (steps,),
        [
            pl.BlockSpec((BQ, model), lambda i, at: (jnp.minimum(i, n_own - 1), 0)),
            pl.BlockSpec((BQ, model), lambda i, at: (jnp.maximum(i - n_own, 0), 0)),
            *[whole(*p.shape) for p in small_parts],
        ],
        [
            pl.BlockSpec((BQ, qkv_cols), lambda i, at: (turned(i, at), 0)),
            pl.BlockSpec((BQ, model), lambda i, at: (turned(i, at), 0)),
            pl.BlockSpec((1, BQ), lambda i, at: (0, turned(i, at))),
            whole(model, cols),
            whole(8, model),
        ],
        [
            shaped((seq, qkv_cols), BF),
            shaped((seq, model), BF),
            shaped((1, seq), F32),
            shaped((model, cols), BF),
            shaped((8, model), F32),
        ],
        prefetch=1,
        us=8,
        name="norm_qkv",
    )(starts, tokens, tokens_other, *small_parts)
    mixed, mixed_low, lse = attention_fwd(info, far, qkv_all, docs, docs, band, rows)
    mixed_turns = gather_turns(mixed_low)

    router_block = whole(model, LANES)
    router = small_all[:, qkv_cols:]
    hidden, normed_two, gate_row = call(
        partial(hidden_kernel, experts),
        (blocks,),
        [
            pl.BlockSpec((BQ, model), lambda i, at: (i, 0)),
            *[pl.BlockSpec((width, BQ), lambda i, at: (0, i))] * 4,
            whole(model, model),
            whole(8, model),
            router_block,
            pl.BlockSpec((1, BQ), lambda i, at: (0, i)),
        ],
        [
            pl.BlockSpec((BQ, model), lambda i, at: (i, 0)),
            pl.BlockSpec((BQ, model), lambda i, at: (i, 0)),
            pl.BlockSpec((1, BQ), lambda i, at: (0, i)),
        ],
        [shaped((rows, model), F32), shaped((rows, model), BF), shaped((1, rows), F32)],
        prefetch=1,
        us=7,
        name="hidden_router",
    )(at, tokens, *mixed_turns, out_all, gains, router, chosen)
    sorted_rows = tiles * TILE
    sorted_spec = lambda cols: pl.BlockSpec((TILE, cols), lambda i, *_: (i, 0))
    *back, eo_t, x_sorted, d_expert, active, d_inner = call(
        expert_kernel,
        (tiles,),
        [
            whole(1, rows),
            whole(rows, model),
            whole(rows, model),
            whole(1, rows),
            pl.BlockSpec((model, 2 * ff), lambda i, owner, at: (owner[i], 0)),
        ],
        [
            *[whole(part + 16, model)] * 4,
            whole(model, rows),
            sorted_spec(model),
            sorted_spec(model),
            sorted_spec(ff),
            sorted_spec(ff),
        ],
        [
            *[shaped((part + 16, model), BF)] * 4,
            shaped((model, rows), BF),
            shaped((sorted_rows, model), BF),
            shaped((sorted_rows, model), BF),
            shaped((sorted_rows, ff), BF),
            shaped((sorted_rows, ff), BF),
        ],
        scratch=[
            pltpu.VMEM((sorted_rows, model), BF),
            pltpu.VMEM((sorted_rows, model + LANES), BF),
            pltpu.VMEM((rows, LANES), F32),
        ],
        prefetch=2,
        us=30,
        name="experts",
    )(owner, at, pos, normed_two, grad_out, gate_row, w_experts)
    back_mine = scatter_turns(back)
    exchanged = []
    for left, right in ((x_sorted, d_inner), (d_expert, active)):
        keep, send = call(
            weight_grad_kernel,
            (tiles,),
            [sorted_spec(model), sorted_spec(ff)],
            [pl.BlockSpec((half, ff), lambda i, owner, slot, at: (slot[i], 0))] * 2,
            [shaped((experts * half, ff), BF)] * 2,
            scratch=[pltpu.VMEM((model, ff), F32)],
            prefetch=3,
            us=0.1,
            name="expert_weight_grads",
        )(owner, slot, at, left, right)
        exchanged.append((keep, xor_step(send, "ctx", 1)))
    (keep_in, got_in), (keep_down, got_down) = exchanged
    both_in = keep_in + got_in
    back_mine, both_in, keep_down = lax.optimization_barrier((back_mine, both_in, keep_down))

    small_rows = -(-(experts + 1) // 8) * 8
    row_block = pl.BlockSpec((part, model), lambda i, at: (at[0], 0))
    col_block = pl.BlockSpec((width, part), lambda i, at: (0, at[0]))
    piece = whole(width, part)
    grad_rows = [model // 2] * 2 if square else [model]
    outs = call(
        partial(hidden_back_kernel, experts),
        (1,),
        [
            *[whole(part + 16, model)] * 4,
            row_block,
            row_block,
            whole(8, model),
            router_block,
            pl.BlockSpec((1, part), lambda i, at: (0, at[0])),
            whole(model, model),
            *[col_block] * 4,
        ],
        [*[piece] * 4, whole(part, model), whole(small_rows, model), whole(model, model)],
        [
            *[shaped((width, part), BF)] * 4,
            shaped((part, model), F32),
            shaped((small_rows, model), F32),
            shaped((model, model), F32),
        ],
        prefetch=1,
        us=6,
        name="hidden_back",
    )(at, *back_mine, hidden, grad_out, gains, router, chosen, out_all, *mixed_turns)
    dmix_out, d_hidden, small_grads, grad_out_w = outs[0:4], outs[4], outs[5], outs[6]
    dmix = scatter_turns(dmix_out)
    both_down = keep_down + got_down
    expert_sums = []
    for both in (both_in, both_down):
        if square:
            pieces = [both[s * half : (s + 1) * half] for s in range(4)]
            expert_sums.append([pieces[0]] + [xor_step(pieces[s], "fsdp", s) for s in (1, 2, 3)])
        else:
            expert_sums.append([lax.psum_scatter(both, "fsdp", scatter_dimension=0, tiled=True)])
    in_sums, down_sums = expert_sums
    dmix, in_sums, eo_t = lax.optimization_barrier((dmix, in_sums, eo_t))
    eo_mine = lax.psum_scatter(eo_t, "tp", scatter_dimension=0, tiled=True)

    dq_t, dkv, skew, sides = attention_bwd(
        info, far, qkv_all, docs, docs, band, mixed, lse, dmix, rows
    )
    other = lax.dynamic_slice_in_dim(dkv, (1 - ctx_at) * rows, rows)
    got = lax.ppermute(other, "ctx", [(0, 1), (1, 0)])
    got, down_sums = lax.optimization_barrier((got, down_sums))
    outs = call(
        qkv_back_kernel,
        (blocks,),
        [
            pl.BlockSpec((width, BQ), lambda i, at: (0, i)),
            pl.BlockSpec((BQ, 2 * width), lambda i, at: (at[2] + i, 0)),
            pl.BlockSpec((BQ, 2 * width), lambda i, at: (i, 0)),
            pl.BlockSpec((BQ, model), lambda i, at: (at[2] + i, 0)),
            pl.BlockSpec((BQ, model), lambda i, at: (i, 0)),
            pl.BlockSpec((1, BQ), lambda i, at: (0, at[2] + i)),
            whole(8, model),
            whole(model, cols),
            whole(part, model),
            whole(model, model),
        ],
        [
            pl.BlockSpec((model, BQ), lambda i, at: (0, i)),
            whole(8, model),
            *[whole(n, qkv_cols + model) for n in grad_rows],
        ],
        [
            shaped((model, rows), BF),
            shaped((8, model), F32),
            *[shaped((n, qkv_cols + model), BF) for n in grad_rows],
        ],
        scratch=[pltpu.VMEM((model, qkv_cols + model), F32)],
        prefetch=1,
        us=9,
        name="qkv_back",
    )(at, dq_t, dkv, got, normed_one, tokens, scale_one, gains, small_all, d_hidden, grad_out_w)
    terms, gain_sum, grad_dense = outs[0], outs[1], outs[2:]
    grad_tokens = lax.psum_scatter(terms, "tp", scatter_dimension=0, tiled=True).astype(F32)
    grad_dense = dense_scatter(grad_dense)
    grad_out_mine = grad_dense[:, qkv_cols : qkv_cols + width]
    for s in (1, 2, 3):
        first = qkv_cols + s * width
        piece_s = grad_dense[:, first : first + width].astype(BF)
        grad_out_mine = grad_out_mine + turn(piece_s, 4 - s).astype(F32)
    grad_in_mine, grad_down_mine = (
        sum(p.astype(F32) for p in after(pieces, gain_sum)) for pieces in expert_sums
    )

    diagonals = skew[0 : 3 * heads].reshape(heads, 3, 2 * BQ)
    table = jnp.einsum("htc,tcb->bh", diagonals, selector, precision=lax.Precision.HIGHEST)
    side = jnp.sum(sides[0 : 2 * heads], axis=1).reshape(heads, 2)
    bucket_ids = jnp.arange(rel_bias.shape[0])[:, None]
    table = table + jnp.where(bucket_ids == 15, side[None, :, 0], 0.0)
    table = table + jnp.where(bucket_ids == 31, side[None, :, 1], 0.0)
    slots = jnp.where(jnp.arange(tp_n)[:, None] == tp_at, table.reshape(1, -1), 0.0).reshape(-1)
    slots = jnp.concatenate((slots, jnp.zeros((-slots.shape[0] % model,), F32))).reshape(-1, model)
    late_sums = sum_all(jnp.concatenate((small_grads, gain_sum, slots)))
    table_all = late_sums[small_rows + 8 :].reshape(-1)[: tp_n * table.size]
    table_all = table_all.reshape(tp_n, rel_bias.shape[0], heads)
    table_mine = lax.dynamic_index_in_dim(table_all, tp_at, 0, keepdims=False)
    table_rows = rel_bias.shape[0] // (fsdp_n * ctx_n)
    grad_table = lax.dynamic_slice_in_dim(table_mine, dense_at * table_rows, table_rows)
    small_mine = lax.dynamic_slice_in_dim(late_sums[: small_rows + 8], dense_at * own, own, 1)
    grad_router = small_mine[0:experts].T
    grad_gain_two = small_mine[experts]
    grad_gain_one = small_mine[small_rows]

    hidden_share = lax.dynamic_slice_in_dim(hidden, columns, share, 1).T
    share_block = pl.BlockSpec((share, BQ), lambda i, *_: (0, i))
    out_share = call(
        out_kernel,
        (blocks,),
        [share_block, share_block, pl.BlockSpec((1, BQ), lambda i: (0, i))],
        share_block,
        shaped((share, rows), BF),
        name="layer_output",
    )(eo_mine, hidden_share, gate_row)
    return (
        out_share.T,
        grad_tokens.T,
        grad_dense[:, 0:qkv_cols].reshape(own, 3, width),
        grad_out_mine,
        grad_table,
        grad_gain_one,
        grad_gain_two,
        grad_router,
        grad_in_mine[None],
        grad_down_mine[None],
    )


def solution(mesh):
    placed = (
        P(("fsdp", "ctx"), None),
        P(("fsdp", "ctx"), None),
        P(("fsdp", "ctx"), None, "tp"),
        P(("fsdp", "ctx"), "tp"),
        P(None, "tp"),
        P(("fsdp", "ctx")),
        P(("fsdp", "ctx")),
        P(("fsdp", "ctx"), None),
        P("fsdp", None, "tp"),
        P("fsdp", None, "tp"),
        P(("fsdp", "ctx"), None),
        P("fsdp"),
    )
    return jax.shard_map(
        shards,
        mesh=mesh,
        in_specs=placed,
        out_specs=(
            P(("fsdp", "ctx"), "tp"),
            P(("fsdp", "ctx"), "tp"),
            P(("fsdp", "ctx"), None, "tp"),
            P(("fsdp", "ctx"), "tp"),
            P(("fsdp", "ctx"), "tp"),
            P(("fsdp", "ctx")),
            P(("fsdp", "ctx")),
            P(("fsdp", "ctx"), None),
            P("fsdp", "ctx", "tp"),
            P("fsdp", "ctx", "tp"),
        ),
        check_vma=False,
    )
```

```python
from functools import partial

import jax
import jax.numpy as jnp
from jax import lax
from jax.experimental import pallas as pl
from jax.experimental.pallas import tpu as pltpu
from jax.sharding import PartitionSpec as P

norm_eps = 1e-06
bucket_edges = (12, 16, 23, 32, 46, 64, 91)
LANES = 128
TILE = 256
MIB = 1024 * 1024
NT = (((1,), (1,)), ((), ()))
TN = (((0,), (0,)), ((), ()))


BQ = 256
BK = 256
HD = 64
NEG = -1e30
FLOOR = -1e28
F32 = jnp.float32
BF = jnp.bfloat16


def call(kernel, grid, in_specs, out_specs, out_shape, scratch=(), prefetch=0, vmem=58, name=None):
    return pl.pallas_call(
        kernel,
        grid_spec=pltpu.PrefetchScalarGridSpec(
            num_scalar_prefetch=prefetch,
            grid=grid,
            in_specs=in_specs,
            out_specs=out_specs,
            scratch_shapes=list(scratch),
        ),
        out_shape=out_shape,
        compiler_params=pltpu.CompilerParams(
            dimension_semantics=("arbitrary",) * len(grid), vmem_limit_bytes=vmem * MIB
        ),
        cost_estimate=pl.CostEstimate(
            flops=10**7, bytes_accessed=10**5, transcendentals=0
        ),
        name=name,
    )


def whole(*shape):
    return pl.BlockSpec(shape, lambda *_: (0,) * len(shape))


def shaped(shape, dtype):
    return jax.ShapeDtypeStruct(shape, dtype)


def relative_bucket(offset):
    distance = jnp.abs(offset)
    far_bucket = jnp.zeros_like(distance) + 8
    for edge in bucket_edges:
        far_bucket = far_bucket + (distance >= edge).astype(jnp.int32)
    result = jnp.where(distance < 8, distance, far_bucket)
    return result + jnp.where(offset > 0, 16, 0)


def dot(a, b, dims=None):
    if dims is None:
        return jnp.dot(a, b, preferred_element_type=F32)
    return lax.dot_general(a, b, dims, preferred_element_type=F32)


def to_row(column):
    n = column.shape[0]
    return jnp.broadcast_to(column, (n, LANES)).T[0:1, :]


def to_column(row):
    n = row.shape[1]
    return jnp.broadcast_to(row, (LANES, n)).T[:, 0:1]


def split3(x):
    hi = x.astype(BF)
    rest = x - hi.astype(F32)
    mid = rest.astype(BF)
    low = (rest - mid.astype(F32)).astype(BF)
    return hi, mid, low


def key_side(docs_col, rows):
    lane = lax.broadcasted_iota(jnp.int32, (rows, HD), 1)
    same = (docs_col == lane.astype(F32)).astype(F32)
    ones = jnp.where((lane >= 4) & (lane < 7), 1.0, 0.0)
    return jnp.where(lane < 4, same, ones)


def query_side(docs_row, cols, tail):
    row = lax.broadcasted_iota(jnp.int32, (HD, cols), 0)
    other = jnp.where((row < 4) & (docs_row != row.astype(F32)), NEG, 0.0)
    if tail is None:
        return other.astype(BF)
    hi, mid, low = (t.astype(F32) for t in split3(tail))
    part = jnp.where(row == 4, hi, jnp.where(row == 5, mid, jnp.where(row == 6, low, 0.0)))
    return jnp.where(row < 4, other, part).astype(BF)


def shifted(x, by):
    return x if by == 0 else pltpu.roll(x, x.shape[1] - by, 1)


def diagonal_sums(tile):
    total = jnp.zeros((8, 2 * BQ), F32)
    for first in range(0, BK, 8):
        strip = tile[first : first + 8, :]
        total = total + shifted(jnp.concatenate([strip, jnp.zeros((8, BQ), F32)], axis=1), first)
    result = jnp.zeros((1, 2 * BQ), F32)
    for r in range(8):
        result = result + shifted(total, r)[r : r + 1, :]
    return result


def ones_rows(cols):
    return jnp.where(lax.broadcasted_iota(jnp.int32, (16, cols), 0) == 0, 1.0, 0.0).astype(BF)


def fwd_kernel(heads, info, far, qkv_all, dcol, drow, band, mixed_ref, low_ref, lse_ref, k_aug, v_t):
    i = pl.program_id(0)
    seq = qkv_all.shape[0]
    width = heads * HD

    @pl.when(i == 0)
    def _():
        for r in range(seq // BK):
            rows = pl.ds(r * BK, BK)
            side = key_side(to_column(dcol[:, r * BK : (r + 1) * BK]), BK).astype(BF)
            vt = qkv_all[rows, 2 * width : 3 * width].astype(F32).T.astype(BF)
            for h in range(heads):
                k = qkv_all[rows, width + h * HD : width + (h + 1) * HD]
                k_aug[h, rows, :] = jnp.concatenate([k, side], axis=1)
                v_t[h, 0:HD, rows] = vt[h * HD : (h + 1) * HD, :]
                v_t[h, HD : HD + 16, rows] = ones_rows(BK)

    qb = info[0, 0] + i
    lo = info[0, 1 + i]
    hi = info[0, 1 + pl.num_programs(0) + i]
    qt = (qkv_all[pl.ds(pl.multiple_of(qb * BQ, BQ), BQ), 0:width].astype(F32) * (HD**-0.5)).T.astype(BF)
    side = query_side(drow[...], BQ, None)
    q_aug = [jnp.concatenate([qt[h * HD : (h + 1) * HD, :], side], axis=0) for h in range(heads)]

    def step(kb, carry, bias_of):
        rows = pl.ds(pl.multiple_of(kb * BK, BK), BK)
        out = []
        for h in range(heads):
            peak, acc = carry[h]
            s = jnp.dot(k_aug[h, rows, :], q_aug[h], preferred_element_type=F32)
            s = s + bias_of(h, kb)
            new = jnp.maximum(peak, jnp.max(s, axis=0, keepdims=True))
            p = jnp.exp(s - new).astype(BF)
            acc = acc * jnp.exp(peak - new) + jnp.dot(v_t[h, :, rows], p, preferred_element_type=F32)
            out.append((new, acc))
        return tuple(out)

    carry = tuple(
        (jnp.full((1, BQ), FLOOR, F32), jnp.zeros((HD + 16, BQ), F32)) for _ in range(heads)
    )
    carry = lax.fori_loop(lo, jnp.minimum(hi, qb - 1), lambda kb, c: step(kb, c, lambda h, _: far[h, 15]), carry)
    carry = lax.fori_loop(
        jnp.maximum(lo, qb - 1),
        jnp.minimum(hi, qb + 2),
        lambda kb, c: step(kb, c, lambda h, t: band[h, t - qb + 1]),
        carry,
    )
    carry = lax.fori_loop(jnp.maximum(lo, qb + 2), hi, lambda kb, c: step(kb, c, lambda h, _: far[h, 31]), carry)
    for h in range(heads):
        peak, acc = carry[h]
        total = acc[HD : HD + 1, :]
        mixed = acc[0:HD, :] / total
        mixed_ref[h * HD : (h + 1) * HD, :] = mixed
        low_ref[h * HD : (h + 1) * HD, :] = mixed.astype(BF)
        lse_ref[h : h + 1, :] = peak + jnp.log(total)


def attention_fwd(info, far, qkv_all, dcol, drow, band, rows):
    seq, cols = qkv_all.shape
    width = cols // 3
    heads = width // HD
    steps = rows // BQ
    full = lambda shape: pl.BlockSpec(shape, lambda i, info: (0,) * len(shape))
    return pl.pallas_call(
        partial(fwd_kernel, heads),
        grid_spec=pltpu.PrefetchScalarGridSpec(
            num_scalar_prefetch=1,
            grid=(steps,),
            in_specs=[
                pl.BlockSpec(memory_space=pltpu.SMEM),
                full((seq, cols)),
                full((1, seq)),
                pl.BlockSpec((1, BQ), lambda i, info: (0, info[0, 0] + i)),
                full((heads, 3, BK, BQ)),
            ],
            out_specs=[
                pl.BlockSpec((width, BQ), lambda i, info: (0, i)),
                pl.BlockSpec((width, BQ), lambda i, info: (0, i)),
                pl.BlockSpec((heads, BQ), lambda i, info: (0, i)),
            ],
            scratch_shapes=[
                pltpu.VMEM((heads, seq, 2 * HD), BF),
                pltpu.VMEM((heads, HD + 16, seq), BF),
            ],
        ),
        out_shape=[
            jax.ShapeDtypeStruct((width, rows), F32),
            jax.ShapeDtypeStruct((width, rows), BF),
            jax.ShapeDtypeStruct((heads, rows), F32),
        ],
        compiler_params=pltpu.CompilerParams(
            dimension_semantics=("arbitrary",), vmem_limit_bytes=58 * 1024 * 1024
        ),
        cost_estimate=pl.CostEstimate(
            flops=10**7, bytes_accessed=10**5, transcendentals=0
        ),
        name="attention_fwd",
    )(info, far, qkv_all, dcol, drow, band)


def bwd_kernel(
    heads, info, far, qkv_all, dcol, drow, band, mixed_ref, lse_ref, m0, m1, m2, m3,
    dq_ref, dkv_ref, skew_ref, side_ref, k_aug, v_aug, k_t, near_acc, dkv_acc,
):
    i = pl.program_id(0)
    seq = qkv_all.shape[0]
    width = heads * HD

    @pl.when(i == 0)
    def _():
        near_acc[...] = jnp.zeros_like(near_acc)
        dkv_acc[...] = jnp.zeros_like(dkv_acc)
        side_ref[...] = jnp.zeros_like(side_ref)
        for r in range(seq // BK):
            rows = pl.ds(r * BK, BK)
            side = key_side(to_column(dcol[:, r * BK : (r + 1) * BK]), BK).astype(BF)
            lane = lax.broadcasted_iota(jnp.int32, (BK, HD), 1)
            ones = jnp.where(lane < 3, 1.0, 0.0).astype(BF)
            kt = qkv_all[rows, width : 2 * width].astype(F32).T.astype(BF)
            for h in range(heads):
                k = qkv_all[rows, width + h * HD : width + (h + 1) * HD]
                v = qkv_all[rows, 2 * width + h * HD : 2 * width + (h + 1) * HD]
                k_aug[h, rows, :] = jnp.concatenate([k, side], axis=1)
                v_aug[h, rows, :] = jnp.concatenate([v, ones], axis=1)
                k_t[h, 0:HD, rows] = kt[h * HD : (h + 1) * HD, :]
                k_t[h, HD : HD + 16, rows] = ones_rows(BK)

    steps = pl.num_programs(0)
    block = lax.rem(info[0, 1 + 2 * steps] + steps - i, steps)
    qb = info[0, 0] + block
    lo = info[0, 1 + block]
    hi = info[0, 1 + steps + block]
    dmix = m0[...]
    for s, ref in ((1, m1), (2, m2), (3, m3)):
        dmix = jnp.where(i == s, ref[...], dmix)
    q_scaled = qkv_all[pl.ds(pl.multiple_of(qb * BQ, BQ), BQ), 0:width].astype(F32) * (HD**-0.5)
    qt = q_scaled.T.astype(BF)
    q_rows = q_scaled.astype(BF)
    dmix_t = dmix.astype(F32)
    dmix_rows = dmix_t.T.astype(BF)
    zero = jnp.zeros((BQ, HD), BF)
    row = lax.broadcasted_iota(jnp.int32, (HD, BQ), 0)
    q_aug, d_aug, rhs = [], [], []
    for h in range(heads):
        cols = slice(h * HD, (h + 1) * HD)
        lse = lse_ref[h : h + 1, :]
        kinds = []
        for tail in (far[h, 15] - lse, -lse, far[h, 31] - lse):
            kinds.append(jnp.concatenate([qt[cols, :], query_side(drow[...], BQ, tail)], axis=0))
        q_aug.append(kinds)
        delta = -jnp.sum(dmix_t[cols, :] * mixed_ref[cols, :], axis=0, keepdims=True)
        a, b, c = (t.astype(F32) for t in split3(delta))
        part = jnp.where(row == 0, a, jnp.where(row == 1, b, jnp.where(row == 2, c, 0.0)))
        d_aug.append(jnp.concatenate([dmix_t[cols, :].astype(BF), part.astype(BF)], axis=0))
        top = jnp.concatenate([dmix_rows[:, cols], zero], axis=1)
        low = jnp.concatenate([zero, q_rows[:, cols]], axis=1)
        rhs.append(jnp.concatenate([top, low], axis=0))

    def step(kb, carry, kind):
        rows = pl.ds(pl.multiple_of(kb * BK, BK), BK)
        out = []
        for h in range(heads):
            s = jnp.dot(k_aug[h, rows, :], q_aug[h][kind], preferred_element_type=F32)
            if kind == 1:
                s = s + band[h, kb - qb + 1]
            p = jnp.exp(s)
            dp = jnp.dot(v_aug[h, rows, :], d_aug[h], preferred_element_type=F32)
            ds = p * dp
            ds_low = ds.astype(BF)
            if kind == 1:
                near_acc[h, kb - qb + 1] = near_acc[h, kb - qb + 1] + ds_low.astype(F32)
            both = jnp.concatenate([p.astype(BF), ds_low], axis=1)
            dkv_acc[h, rows, :] += jnp.dot(both, rhs[h], preferred_element_type=F32)
            out.append(carry[h] + jnp.dot(k_t[h, :, rows], ds_low, preferred_element_type=F32))
        return tuple(out)

    zero_dq = jnp.zeros((HD + 16, BQ), F32)
    left = lax.fori_loop(lo, jnp.minimum(hi, qb - 1), lambda kb, c: step(kb, c, 0), (zero_dq,) * heads)
    near = lax.fori_loop(
        jnp.maximum(lo, qb - 1), jnp.minimum(hi, qb + 2), lambda kb, c: step(kb, c, 1), left
    )
    last = lax.fori_loop(jnp.maximum(lo, qb + 2), hi, lambda kb, c: step(kb, c, 2), near)
    for h in range(heads):
        dq_ref[h * HD : (h + 1) * HD, :] = (last[h][0:HD, :] * (HD**-0.5)).astype(BF)
        side_ref[2 * h : 2 * h + 1, :] += left[h][HD : HD + 1, :]
        side_ref[2 * h + 1 : 2 * h + 2, :] += last[h][HD : HD + 1, :] - near[h][HD : HD + 1, :]

    @pl.when(i == pl.num_programs(0) - 1)
    def _():
        for h in range(heads):
            for t in range(3):
                skew_ref[3 * h + t : 3 * h + t + 1, :] = diagonal_sums(near_acc.at[h, t])
        for r in range(seq // BK):
            rows = pl.ds(r * BK, BK)
            acc = [dkv_acc[h, rows, :] for h in range(heads)]
            dk = [a[:, HD : 2 * HD] for a in acc]
            dv = [a[:, 0:HD] for a in acc]
            dkv_ref[rows, :] = jnp.concatenate(dk + dv, axis=1).astype(BF)


def attention_bwd(info, far, qkv_all, dcol, drow, band, mixed, lse, dmix, rows):
    seq, cols = qkv_all.shape
    width = cols // 3
    heads = width // HD
    steps = rows // BQ
    full = lambda shape: pl.BlockSpec(shape, lambda i, info: (0,) * len(shape))
    block = lambda i, info: lax.rem(info[0, 1 + 2 * steps] + steps - i, steps)
    return pl.pallas_call(
        partial(bwd_kernel, heads),
        grid_spec=pltpu.PrefetchScalarGridSpec(
            num_scalar_prefetch=1,
            grid=(steps,),
            in_specs=[
                pl.BlockSpec(memory_space=pltpu.SMEM),
                full((seq, cols)),
                full((1, seq)),
                pl.BlockSpec((1, BQ), lambda i, info: (0, info[0, 0] + block(i, info))),
                full((heads, 3, BK, BQ)),
                pl.BlockSpec((width, BQ), lambda i, info: (0, block(i, info))),
                pl.BlockSpec((heads, BQ), lambda i, info: (0, block(i, info))),
                *[full((width, BQ))] * 4,
            ],
            out_specs=[
                pl.BlockSpec((width, BQ), lambda i, info: (0, block(i, info))),
                full((seq, 2 * width)),
                full((16, 2 * BK)),
                full((8, BQ)),
            ],
            scratch_shapes=[
                pltpu.VMEM((heads, seq, 2 * HD), BF),
                pltpu.VMEM((heads, seq, 2 * HD), BF),
                pltpu.VMEM((heads, HD + 16, seq), BF),
                pltpu.VMEM((heads, 3, BK, BQ), F32),
                pltpu.VMEM((heads, seq, 2 * HD), F32),
            ],
        ),
        out_shape=[
            jax.ShapeDtypeStruct((width, rows), BF),
            jax.ShapeDtypeStruct((seq, 2 * width), BF),
            jax.ShapeDtypeStruct((16, 2 * BK), F32),
            jax.ShapeDtypeStruct((8, BQ), F32),
        ],
        compiler_params=pltpu.CompilerParams(
            dimension_semantics=("arbitrary",), vmem_limit_bytes=58 * 1024 * 1024
        ),
        cost_estimate=pl.CostEstimate(
            flops=10**7, bytes_accessed=10**5, transcendentals=0
        ),
        name="attention_bwd",
    )(info, far, qkv_all, dcol, drow, band, mixed, lse, *dmix)


def plan_kernel(
    experts, own, table_rows, at, ids_ref, docs_ref, table_ref,
    pos_ref, owner_ref, chosen_ref, docs_out, info_ref, band_ref, diag_ref, spread_ref,
):
    rows = ids_ref.shape[1]
    seq = docs_ref.shape[1]
    heads = band_ref.shape[0]
    buckets = table_ref.shape[1]
    blocks = rows // BQ
    chosen = ids_ref[...].astype(F32)
    chosen_ref[...] = chosen
    docs = docs_ref[...].astype(F32)
    docs_out[...] = docs
    expert_rows = -(-experts // 8) * 8
    one_hot = lax.broadcasted_iota(jnp.int32, (expert_rows, rows), 0).astype(F32) == chosen
    one_hot = jnp.where(one_hot, 1.0, 0.0)
    low_rows = lax.broadcasted_iota(jnp.int32, (rows, rows), 0)
    before = jnp.where(low_rows < lax.broadcasted_iota(jnp.int32, (rows, rows), 1), 1.0, 0.0)
    earlier = dot(one_hot.astype(BF), before.astype(BF))
    lane = lax.broadcasted_iota(jnp.int32, (1, LANES), 1)
    lane_f = lane.astype(F32)
    pos = jnp.zeros((1, rows), F32)
    owner = jnp.zeros((1, LANES), F32)
    end = jnp.zeros((1, 1), F32)
    for e in range(experts):
        hit = one_hot[e : e + 1, :]
        count = jnp.sum(hit, axis=1, keepdims=True)
        pos = pos + hit * (earlier[e : e + 1, :] + end * TILE)
        end = end + jnp.maximum(jnp.floor((count + (TILE - 1)) * (1.0 / TILE)), 1.0)
        owner = owner + jnp.where(end <= lane_f, 1.0, 0.0)
    pos_ref[...] = pos.astype(jnp.int32)
    owner = jnp.minimum(owner, experts - 1.0)
    owner_ref[...] = jnp.where(lane == LANES - 1, end, owner).astype(jnp.int32)
    base = at[2]
    info = jnp.where(lane == 0, base, jnp.where(lane == 1 + 2 * blocks, at[0], 0)).astype(F32)
    for b in range(seq // BQ):
        first = docs[:, b * BQ : b * BQ + 1]
        last = docs[:, (b + 1) * BQ - 1 : (b + 1) * BQ]
        low = jnp.sum(jnp.where(docs < first, 1.0, 0.0), axis=1, keepdims=True)
        high = jnp.sum(jnp.where(docs <= last, 1.0, 0.0), axis=1, keepdims=True)
        here = (b >= base) & (b < base + blocks)
        low_at = (lane == 1 + b - base) & here
        high_at = (lane == 1 + blocks + b - base) & here
        info = info + jnp.where(low_at, jnp.floor(low * (1.0 / BK)), 0.0)
        info = info + jnp.where(high_at, jnp.floor((high + (BK - 1)) * (1.0 / BK)), 0.0)
    info_ref[...] = info.astype(jnp.int32)
    span = 3 * 2 * BQ
    column = lax.broadcasted_iota(jnp.int32, (8, span), 1)
    tile = (column >= 2 * BQ).astype(jnp.int32) + (column >= 4 * BQ).astype(jnp.int32)
    inside = column - tile * (2 * BQ)
    wrapped = jnp.where(inside < BQ, inside, inside - 2 * BQ)
    bucket = relative_bucket((tile - 1) * BK - wrapped)[0:1, :].astype(F32)
    which = lax.broadcasted_iota(jnp.int32, (buckets, span), 0).astype(F32)
    pick = jnp.where(which == bucket, 1.0, 0.0).astype(BF)
    wide = jnp.concatenate([table_ref[...], jnp.zeros((8 - heads, buckets), F32)], axis=0)
    vectors = sum(dot(p, pick) for p in split3(wide))
    for h in range(heads):
        for t in range(3):
            line = vectors[h : h + 1, t * 2 * BQ : (t + 1) * 2 * BQ]
            wide = jnp.broadcast_to(line, (BK, 2 * BQ))
            band_ref[h, t] = pltpu.roll(wide, 0, 1, stride=1, stride_axis=0)[:, 0:BQ]
    by_column = to_column(bucket)
    lanes = lax.broadcasted_iota(jnp.int32, (span, LANES), 1).astype(F32)
    diag_ref[...] = jnp.where(by_column == lanes, 1.0, 0.0).astype(BF)
    model = spread_ref.shape[1]
    row_ids = lax.broadcasted_iota(jnp.int32, (8, model), 1)
    target = jnp.full((8, model), -1, jnp.int32)
    for b in range(buckets):
        target = jnp.where(row_ids == b // table_rows * own + b % table_rows, b, target)
    down = lax.broadcasted_iota(jnp.int32, (LANES, model), 0).astype(F32)
    spread_ref[...] = jnp.where(down == target[0:1, :].astype(F32), 1.0, 0.0).astype(BF)


def pack_kernel(o0, o1, o2, o3, qkv_ref, router_ref, one_ref, two_ref, out_ref):
    experts, rows = router_ref.shape
    fill = jnp.zeros((LANES - experts - 2, rows), F32)
    tail = [r[...].astype(F32) for r in (router_ref, one_ref, two_ref)]
    tail = jnp.concatenate([*tail, fill], axis=0).T.astype(BF)
    parts = [r[...] for r in (o0, o1, o2, o3)] + [qkv_ref[c] for c in range(3)]
    used = sum(p.shape[1] for p in parts)
    gap = out_ref.shape[1] - used - LANES
    if gap:
        parts.append(jnp.zeros((rows, gap), BF))
    out_ref[...] = jnp.concatenate([*parts, tail], axis=1)


def qkv_kernel(
    first_col, cols, experts, count, at, own_ref, other_ref, *refs
):
    pieces = refs[:count]
    qkv_ref, norm_ref, scale_ref, small_ref, gains_ref = refs[count:]
    i = pl.program_id(0)

    @pl.when(i == 0)
    def _():
        slot = 0
        for piece in pieces:
            for s in range(piece.shape[0]):
                first = pl.multiple_of(at[4 + slot], 16)
                small_ref[pl.ds(first, piece.shape[1]), :] = piece[s]
                slot += 1
        tail = small_ref[:, small_ref.shape[1] - LANES :].astype(F32).T
        gains_ref[...] = tail[experts : experts + 8, :]

    x = jnp.where(i < pl.num_programs(0) // 2, own_ref[...], other_ref[...]).astype(F32)
    scale = lax.rsqrt(jnp.mean(x * x, axis=-1, keepdims=True) + norm_eps)
    normed = (x * scale * gains_ref[0:1, :]).astype(BF)
    norm_ref[...] = normed
    scale_ref[...] = to_row(scale)
    qkv_ref[...] = dot(normed, small_ref[:, first_col : first_col + cols]).astype(BF)


def router_parts(hidden, gain, router, chosen, experts):
    scale = lax.rsqrt(jnp.mean(hidden * hidden, axis=-1, keepdims=True) + norm_eps)
    hat = hidden * scale
    normed = (hat * gain).astype(BF)
    lane = lax.broadcasted_iota(jnp.int32, (hidden.shape[0], LANES), 1)
    logits = jnp.where(lane < experts, dot(normed, router), NEG)
    weights = jnp.exp(logits - jnp.max(logits, axis=-1, keepdims=True))
    route = weights / jnp.sum(weights, axis=-1, keepdims=True)
    one_hot = jnp.where(lane.astype(F32) == chosen, 1.0, 0.0)
    gate = jnp.sum(route * one_hot, axis=-1, keepdims=True)
    return scale, hat, normed, route, one_hot, gate


def hidden_kernel(experts, at, *refs):
    tok_ref, mix_refs, wout_ref = refs[0], refs[1:5], refs[5]
    gains_ref, small_ref, chosen_ref, hidden_ref, norm_ref, gate_ref, share_ref, turn_s = refs[6:]
    mixed = jnp.concatenate([r[...] for r in mix_refs], axis=0)
    both = mixed.astype(F32).T.astype(BF)
    hidden = tok_ref[...].astype(F32) + dot(both, wout_ref[...], NT)
    parts = router_parts(hidden, gains_ref[1:2, :], small_ref[...], to_column(chosen_ref[...]), experts)
    hidden_ref[...] = hidden
    norm_ref[...] = parts[2]
    gate_ref[...] = to_row(parts[5])
    turn_s[...] = hidden.T
    share = share_ref.shape[0]
    share_ref[...] = turn_s[pl.ds(pl.multiple_of(at[0] * share, share), share), :]


def sort_kernel(owner, pos_row, rows_ref, out_ref):
    i = pl.program_id(0)
    place = lax.broadcasted_iota(jnp.int32, (TILE, pos_row.shape[1]), 0) + i * TILE
    pick = jnp.where(pos_row[...] == place, 1.0, 0.0).astype(BF)
    out_ref[...] = dot(pick, rows_ref[...]).astype(BF)


def pick_back(pos_col, total):
    place = lax.broadcasted_iota(jnp.int32, (pos_col.shape[0], total), 1).astype(F32)
    return jnp.where(pos_col == place, 1.0, 0.0).astype(BF)


def unsort_kernel(owner, at, pos_row, sorted_ref, e0, e1, e2, e3, pos_col, turn_s):
    rows = pos_row.shape[1]
    part = turn_s.shape[1]
    pos_col[...] = jnp.broadcast_to(pos_row[...].astype(F32), (LANES, rows)).T
    for g in range(rows // part):
        mine = slice(g * part, (g + 1) * part)
        pick = pick_back(pos_col[mine, 0:1], sorted_ref.shape[0])
        turn_s[...] = dot(pick, sorted_ref[...]).T.astype(BF)
        for step, out in enumerate((e0, e1, e2, e3)):
            share = out.shape[0]
            first = pl.multiple_of(lax.rem(at[0] + step, 4) * share, share)
            out[:, mine] = turn_s[pl.ds(first, share), :]


def expert_kernel(
    owner, at, pos_row, norm_ref, cot_ref, gate_ref, w_ref,
    b0, b1, b2, b3, eo_ref, x_ref, de_ref, act_ref, di_ref, dr_s, pos_col,
):
    i = pl.program_id(0)
    z = at[0]
    rows = norm_ref.shape[0]
    width = norm_ref.shape[1]
    ff = w_ref.shape[1] // 2
    here = pl.ds(pl.multiple_of(i * TILE, TILE), TILE)
    used = i < owner[0, LANES - 1]

    @pl.when(used)
    def _():
        place = lax.broadcasted_iota(jnp.int32, (TILE, rows), 0) + i * TILE
        hit = pos_row[...] == place
        pick = jnp.where(hit, 1.0, 0.0).astype(BF)
        x = dot(pick, norm_ref[...]).astype(BF)
        cot = cot_ref[...].astype(F32)
        gate = jnp.sum(jnp.where(hit, gate_ref[...], 0.0), axis=1, keepdims=True)
        d_e = (gate * cot).astype(BF)
        w_in = w_ref[:, 0:ff]
        w_down = w_ref[:, ff : 2 * ff]
        d_act = dot(d_e, w_down)
        inner = dot(x, w_in)
        half = 0.5 * (1.0 + lax.erf(inner * (0.5**0.5)))
        active = (inner * half).astype(BF)
        slope = half + inner * (jnp.exp(-0.5 * inner * inner) * 0.3989422804014327)
        d_inner = (d_act * slope).astype(BF)
        d_rows = dot(d_inner, w_in, NT)
        terms = dot(active, w_down, NT)
        d_gate = jnp.sum(cot * terms, axis=1, keepdims=True)
        lane = lax.broadcasted_iota(jnp.int32, (TILE, LANES), 1)
        hi, mid, low = (t.astype(F32) for t in split3(d_gate))
        extra = jnp.where(lane == 0, hi, jnp.where(lane == 1, mid, jnp.where(lane == 2, low, 0.0)))
        dr_s[here, :] = jnp.concatenate([d_rows.astype(BF), extra.astype(BF)], axis=1)
        eo_ref[...] = terms.astype(BF)
        x_ref[...] = x
        de_ref[...] = d_e
        act_ref[...] = active
        di_ref[...] = d_inner

    @pl.when(jnp.logical_not(used))
    def _():
        dr_s[here, :] = jnp.zeros((TILE, dr_s.shape[1]), BF)
        for ref in (eo_ref, x_ref, de_ref, act_ref, di_ref):
            ref[...] = jnp.zeros_like(ref)

    @pl.when(i == pl.num_programs(0) - 1)
    def _():
        part = rows // 4
        pos_col[...] = jnp.broadcast_to(pos_row[...].astype(F32), (LANES, rows)).T
        for r, back_ref in enumerate((b0, b1, b2, b3)):
            g = lax.rem(z + r, 4)
            mine = pl.ds(pl.multiple_of(g * part, part), part)
            back = dot(pick_back(pos_col[mine, 0:1], dr_s.shape[0]), dr_s[...])
            back_ref[0:part, :] = back[:, 0:width].astype(BF)
            tail = back[:, width : width + LANES].T
            d_gate = tail[0:1, :] + tail[1:2, :] + tail[2:3, :]
            row = lax.broadcasted_iota(jnp.int32, (16, part), 0)
            strip = jnp.where(row == 0, jnp.broadcast_to(d_gate, (16, part)), 0.0)
            fill = jnp.zeros((16, width - part), F32)
            back_ref[part : part + 16, :] = jnp.concatenate([strip, fill], axis=1).astype(BF)


def weight_grad_kernel(owner, x_ref, di_ref, de_ref, act_ref, out_ref, acc):
    i = pl.program_id(0)
    last = pl.num_programs(0) - 1
    me = owner[0, i]
    before = owner[0, jnp.maximum(i - 1, 0)]
    after = owner[0, jnp.minimum(i + 1, last)]
    ff = di_ref.shape[1]

    first = (i == 0) | (before != me)
    used = i < owner[0, LANES - 1]

    @pl.when(first)
    def _():
        acc[:, 0:ff] = dot(x_ref[...], di_ref[...], TN)
        acc[:, ff : 2 * ff] = dot(de_ref[...], act_ref[...], TN)

    @pl.when(jnp.logical_not(first) & used)
    def _():
        acc[:, 0:ff] += dot(x_ref[...], di_ref[...], TN)
        acc[:, ff : 2 * ff] += dot(de_ref[...], act_ref[...], TN)

    @pl.when((i == last) | (after != me))
    def _():
        out_ref[...] = acc[...].astype(BF)


def split_rows(at, first_slot, acc, outs):
    if len(outs) == 1:
        outs[0][...] = acc[...].astype(BF)
        return
    slot = first_slot
    for out in outs:
        step = out.shape[0] // 4
        for s in range(4):
            first = pl.multiple_of(at[slot], 8)
            out[s * step : (s + 1) * step, :] = acc[pl.ds(first, step), :].astype(BF)
            slot += 1


def hidden_back_kernel(experts, at, *refs):
    back_refs, (hidden_ref, cot_ref, gains_ref, router_ref, chosen_ref) = refs[:4], refs[4:9]
    wout_ref, mix_refs = refs[9], refs[10:14]
    dmix_refs, dh_ref, small_ref, gout_ref = refs[14:18], refs[18], refs[19], refs[20]
    part, model = hidden_ref.shape
    back = sum(r[...].astype(F32) for r in back_refs)
    gain = gains_ref[1:2, :]
    router = router_ref[...]
    scale, hat, normed, route, one_hot, gate = router_parts(
        hidden_ref[...], gain, router, to_column(chosen_ref[...]), experts
    )
    d_gate = to_column(back[part : part + 1, 0:part])
    d_logits = (d_gate * gate) * (one_hot - route)
    parts = split3(d_logits)
    d_normed = back[0:part, :]
    g_router = jnp.zeros((LANES, model), F32)
    for p in parts:
        d_normed = d_normed + dot(p, router, NT)
        g_router = g_router + dot(p, normed, TN)
    small_ref[...] = jnp.zeros_like(small_ref)
    small_ref[0:experts, :] = g_router[0:experts, :]
    small_ref[experts : experts + 1, :] = jnp.sum(d_normed * hat, axis=0, keepdims=True)
    d_hat = d_normed * gain
    d_hidden = cot_ref[...].astype(F32) + scale * (
        d_hat - hat * jnp.mean(d_hat * hat, axis=-1, keepdims=True)
    )
    d_attn = d_hidden.astype(BF)
    d_attn_t = d_hidden.T.astype(BF)
    d_mixed = dot(d_attn, wout_ref[...]).T.astype(BF)
    width = model // 4
    for s in range(4):
        r = (4 - s) % 4
        dmix_refs[r][...] = d_mixed[s * width : (s + 1) * width, :]
    dh_ref[...] = d_hidden
    mixed = jnp.concatenate([r[...] for r in mix_refs], axis=0)
    gout_ref[...] = dot(d_attn_t, mixed, NT).astype(BF)


def qkv_back_kernel(
    first_col, experts, heads, at, dq_ref, dkv_ref, got_ref, norm_ref, tok_ref, scale_ref, gains_ref, w_ref,
    dh_ref, gout_ref, small_ref, skew_ref, sides_ref, diag_ref, spread_ref,
    terms_ref, *rest,
):
    *gw_refs, acc, gain_s = rest
    i = pl.program_id(0)
    width = dq_ref.shape[0]
    cols = 3 * width
    model = tok_ref.shape[1]
    dkv = dkv_ref[...].astype(F32) + got_ref[...].astype(F32)
    d_qkv = jnp.concatenate([dq_ref[...].astype(F32).T, dkv], axis=1).astype(BF)
    scale = to_column(scale_ref[...])
    hat = tok_ref[...].astype(F32) * scale
    terms = dot(d_qkv, w_ref[:, first_col : first_col + cols], NT)
    d_hat = terms * gains_ref[0:1, :]
    mean = jnp.mean(d_hat * hat, axis=-1, keepdims=True)
    grad = scale * (d_hat - hat * mean) + jnp.where(i == at[0], dh_ref[...], 0.0)

    @pl.when(i == 0)
    def _():
        wide = acc.shape[1] - model - LANES
        acc[:, 0:wide] = jnp.zeros((model, wide), F32)
        acc[:, wide : wide + model] = gout_ref[...].astype(F32)
        gain_s[...] = jnp.zeros_like(gain_s)

    gain_s[0:1, :] += jnp.sum(terms * hat, axis=0, keepdims=True)
    acc[:, 0:cols] += dot(norm_ref[...], d_qkv, TN)
    terms_ref[...] = grad.T.astype(BF)

    @pl.when(i == pl.num_programs(0) - 1)
    def _():
        rows = [small_ref[0 : experts + 1, :], gain_s[0:1, :]]
        lines = []
        sides = []
        for h in range(8):
            k = min(h, heads - 1)
            lines.append(jnp.concatenate([skew_ref[3 * k + t : 3 * k + t + 1, :] for t in range(3)], axis=1))
            sides.append(jnp.sum(sides_ref[2 * k : 2 * k + 2, :], axis=1, keepdims=True))
        lane = lax.broadcasted_iota(jnp.int32, (8, LANES), 1)
        table = sum(dot(p, diag_ref[...]) for p in split3(jnp.concatenate(lines, axis=0)))
        table = table + jnp.where(lane == 15, jnp.concatenate([s[0:1, :] for s in sides], axis=0), 0.0)
        table = table + jnp.where(lane == 31, jnp.concatenate([s[1:2, :] for s in sides], axis=0), 0.0)
        spread = sum(dot(p, spread_ref[...]) for p in split3(table))
        rows.append(spread[0:heads, :])
        rows.append(jnp.zeros((LANES - experts - 2 - heads, model), F32))
        acc[:, acc.shape[1] - LANES :] = jnp.concatenate(rows, axis=0).T
        split_rows(at, 4, acc, gw_refs)


def out_kernel(e0, e1, e2, e3, hidden_ref, gate_ref, out_ref):
    total = sum(r[...].astype(F32) for r in (e0, e1, e2, e3))
    out_ref[...] = (hidden_ref[...] + total * gate_ref[...]).astype(BF)


def pair_sum_kernel(keep_ref, got_ref, *outs):
    step = outs[0].shape[0]
    for s, out in enumerate(outs):
        rows = slice(s * step, (s + 1) * step)
        out[...] = (keep_ref[rows, :].astype(F32) + got_ref[rows, :].astype(F32)).astype(BF)


def dense_sum_kernel(cols, count, *refs):
    parts, (qkv_ref, late_ref, *outs) = refs[:count], refs[count:]
    total = sum(r[...].astype(F32) for r in parts)
    width = qkv_ref.shape[2]
    for c in range(3):
        qkv_ref[c] = total[:, c * width : (c + 1) * width]
    late = total[:, total.shape[1] - LANES :]
    late_ref[...] = late.T
    for s, out in enumerate(outs):
        piece = total[:, cols + s * width : cols + (s + 1) * width]
        gap = jnp.zeros((late.shape[0], out.shape[1] - LANES - width), F32)
        out[...] = jnp.concatenate([late, piece, gap], axis=1).astype(BF)


def last_sum_kernel(p0, p1, p2, p3, out_ref, late_ref):
    total = sum(r[...].astype(F32) for r in (p0, p1, p2, p3))
    out_ref[...] = total[:, LANES : LANES + out_ref.shape[1]]
    late_ref[...] = total[:, 0:LANES].T

def xor_step(x, axis, s):
    return lax.ppermute(x, axis, [(i, i ^ s) for i in range(lax.axis_size(axis))])


def turn(x, s):
    return lax.ppermute(x, "tp", [(i, (i + s) % 4) for i in range(4)])


def gather_turns(x):
    return [x] + [turn(x, s) for s in (1, 2, 3)]


def scatter_turns(pieces):
    return [pieces[0]] + [turn(pieces[r], r) for r in (1, 2, 3)]


def after(x, *others):
    return lax.optimization_barrier((x, others))[0]


def shards(
    tokens,
    grad_out,
    w_qkv,
    w_attn_out,
    rel_bias,
    gain_attn,
    gain_ffn,
    w_router,
    w_in,
    w_down,
    expert_ids,
    doc_ids,
):
    rows, model = tokens.shape
    heads = rel_bias.shape[1]
    width = w_qkv.shape[2]
    own = w_qkv.shape[0]
    experts = w_router.shape[1]
    ff = w_in.shape[2]
    seq = doc_ids.shape[0]
    fsdp_n = lax.axis_size("fsdp")
    ctx_n = lax.axis_size("ctx")
    tp_n = lax.axis_size("tp")
    fsdp_at = lax.axis_index("fsdp")
    ctx_at = lax.axis_index("ctx")
    tp_at = lax.axis_index("tp")
    dense_at = fsdp_at * ctx_n + ctx_at
    part = rows // tp_n
    share = model // tp_n
    blocks = rows // BQ
    dense = ("fsdp", "ctx")
    square = fsdp_n == 4 and ctx_n == 2

    wide_cols = -(-3 * width // LANES) * LANES
    late_at = wide_cols + model
    table_rows = rel_bias.shape[0] // (fsdp_n * ctx_n)
    if square:
        starts = [((fsdp_at ^ s) * 2 + c) * own for c in (ctx_at, 1 - ctx_at) for s in range(4)]
    else:
        starts = [0]
    at = jnp.stack([jnp.int32(v) for v in (tp_at, ctx_at, ctx_at * blocks, fsdp_at, *starts)])

    qkv_cols = 3 * width
    first_col = model
    cols = -(-(model + qkv_cols) // LANES) * LANES + LANES
    small = call(
        pack_kernel,
        (1,),
        [
            *[whole(own, width)] * 4,
            whole(3, own, width),
            whole(experts, own),
            whole(1, own),
            whole(1, own),
        ],
        whole(own, cols),
        shaped((own, cols), BF),
        name="pack_small",
    )(
        *gather_turns(w_attn_out),
        w_qkv.transpose(1, 0, 2),
        w_router.T,
        gain_attn[None, :],
        gain_ffn[None, :],
    )
    tokens_other = xor_step(tokens, "ctx", 1)
    half = model // ctx_n
    w_half = jnp.concatenate(
        [lax.dynamic_slice_in_dim(w.reshape(-1, ff), ctx_at * half, half, 0) for w in (w_in, w_down)],
        axis=1,
    )

    tiles = (rows + experts * (TILE - 1)) // TILE
    span = 6 * BQ
    table = rel_bias.T
    pos, owner, chosen, docs, info, band, diag, spread = call(
        partial(plan_kernel, experts, own, table_rows),
        (1,),
        [whole(1, rows), whole(1, seq), whole(*table.shape)],
        [
            whole(1, rows),
            whole(1, LANES),
            whole(1, rows),
            whole(1, seq),
            whole(1, LANES),
            whole(heads, 3, BK, BQ),
            whole(span, LANES),
            whole(LANES, model),
        ],
        [
            shaped((1, rows), jnp.int32),
            shaped((1, LANES), jnp.int32),
            shaped((1, rows), F32),
            shaped((1, seq), F32),
            shaped((1, LANES), jnp.int32),
            shaped((heads, 3, BK, BQ), F32),
            shaped((span, LANES), BF),
            shaped((LANES, model), BF),
        ],
        prefetch=1,
        name="plan",
    )(at, expert_ids.T, doc_ids[None, :], table)
    if square:
        near = [small] + [xor_step(small, "fsdp", s) for s in (1, 2, 3)]
        near, w_half, band = lax.optimization_barrier((near, w_half, band))
        near = jnp.stack(near)
        small_parts = [near, xor_step(near, "ctx", 1)]
    else:
        small_parts = [lax.all_gather(small, dense, axis=0, tiled=True)[None]]
    small_parts, tokens_other, w_half = lax.optimization_barrier((small_parts, tokens_other, w_half))

    w_experts = lax.all_gather(w_half, dense, axis=0, tiled=True)

    steps = seq // BQ
    n_own = steps // 2
    turned = lambda i, at: jnp.where(i < n_own, at[2] + i, i - at[2])
    qkv_all, normed_one, scale_one, small_all, gains = call(
        partial(qkv_kernel, first_col, qkv_cols, experts, len(small_parts)),
        (steps,),
        [
            pl.BlockSpec((BQ, model), lambda i, at: (jnp.minimum(i, n_own - 1), 0)),
            pl.BlockSpec((BQ, model), lambda i, at: (jnp.maximum(i - n_own, 0), 0)),
            *[whole(*p.shape) for p in small_parts],
        ],
        [
            pl.BlockSpec((BQ, qkv_cols), lambda i, at: (turned(i, at), 0)),
            pl.BlockSpec((BQ, model), lambda i, at: (turned(i, at), 0)),
            pl.BlockSpec((1, BQ), lambda i, at: (0, turned(i, at))),
            whole(model, cols),
            whole(8, model),
        ],
        [
            shaped((seq, qkv_cols), BF),
            shaped((seq, model), BF),
            shaped((1, seq), F32),
            shaped((model, cols), BF),
            shaped((8, model), F32),
        ],
        prefetch=1,
        name="norm_qkv",
    )(at, tokens, tokens_other, *small_parts)
    mixed, mixed_low, lse = attention_fwd(info, table, qkv_all, docs, docs, band, rows)
    mixed_turns = gather_turns(mixed_low)
    sorted_rows = tiles * TILE
    sorted_spec = lambda cols: pl.BlockSpec((TILE, cols), lambda i, *_: (i, 0))
    cot_sorted = call(
        sort_kernel,
        (tiles,),
        [whole(1, rows), whole(rows, model)],
        sorted_spec(model),
        shaped((sorted_rows, model), BF),
        prefetch=1,
        name="sort_cotangents",
    )(owner, pos, after(grad_out, mixed_low))
    mixed_turns, cot_sorted = lax.optimization_barrier((mixed_turns, cot_sorted))

    router_block = pl.BlockSpec((model, LANES), lambda i, at: (0, cols // LANES - 1))
    out_block = pl.BlockSpec((model, model), lambda i, at: (0, 0))
    hidden, normed_two, gate_row, hidden_share = call(
        partial(hidden_kernel, experts),
        (blocks,),
        [
            pl.BlockSpec((BQ, model), lambda i, at: (i, 0)),
            *[pl.BlockSpec((width, BQ), lambda i, at: (0, i))] * 4,
            out_block,
            whole(8, model),
            router_block,
            pl.BlockSpec((1, BQ), lambda i, at: (0, i)),
        ],
        [
            pl.BlockSpec((BQ, model), lambda i, at: (i, 0)),
            pl.BlockSpec((BQ, model), lambda i, at: (i, 0)),
            pl.BlockSpec((1, BQ), lambda i, at: (0, i)),
            pl.BlockSpec((share, BQ), lambda i, at: (0, i)),
        ],
        [
            shaped((rows, model), F32),
            shaped((rows, model), BF),
            shaped((1, rows), F32),
            shaped((share, rows), F32),
        ],
        scratch=[pltpu.VMEM((model, BQ), F32)],
        prefetch=1,
        name="hidden_router",
    )(at, tokens, *mixed_turns, small_all, gains, small_all, chosen)
    *back, eo_sorted, x_sorted, d_expert, active, d_inner = call(
        expert_kernel,
        (tiles,),
        [
            whole(1, rows),
            whole(rows, model),
            sorted_spec(model),
            whole(1, rows),
            pl.BlockSpec((model, 2 * ff), lambda i, owner, at: (owner[0, i], 0)),
        ],
        [
            *[whole(part + 16, model)] * 4,
            sorted_spec(model),
            sorted_spec(model),
            sorted_spec(model),
            sorted_spec(ff),
            sorted_spec(ff),
        ],
        [
            *[shaped((part + 16, model), BF)] * 4,
            shaped((sorted_rows, model), BF),
            shaped((sorted_rows, model), BF),
            shaped((sorted_rows, model), BF),
            shaped((sorted_rows, ff), BF),
            shaped((sorted_rows, ff), BF),
        ],
        scratch=[
            pltpu.VMEM((sorted_rows, model + LANES), BF),
            pltpu.VMEM((rows, LANES), F32),
        ],
        prefetch=2,
        name="experts",
    )(owner, at, pos, normed_two, cot_sorted, gate_row, w_experts)
    back_mine = scatter_turns(back)
    back_got = back_mine[1:]
    grad_experts = call(
        weight_grad_kernel,
        (tiles,),
        [sorted_spec(model), sorted_spec(ff), sorted_spec(model), sorted_spec(ff)],
        pl.BlockSpec((model, 2 * ff), lambda i, owner: (owner[0, i], 0)),
        shaped((experts * model, 2 * ff), BF),
        scratch=[pltpu.VMEM((model, 2 * ff), F32)],
        prefetch=1,
        name="expert_weight_grads",
    )(owner, x_sorted, d_inner, d_expert, active)
    eo_out = call(
        unsort_kernel,
        (1,),
        [whole(1, rows), whole(sorted_rows, model)],
        [whole(share, rows)] * 4,
        [shaped((share, rows), BF)] * 4,
        scratch=[pltpu.VMEM((rows, LANES), F32), pltpu.VMEM((model, part), BF)],
        prefetch=2,
        name="unsort_outputs",
    )(owner, at, pos, after(eo_sorted, grad_experts))
    back_mine, eo_out = lax.optimization_barrier((back_mine, eo_out))
    grad_experts = lax.psum_scatter(after(grad_experts, back_got), dense, scatter_dimension=0, tiled=True)

    small_rows = -(-(experts + 1) // 8) * 8
    row_block = pl.BlockSpec((part, model), lambda i, at: (at[0], 0))
    col_block = pl.BlockSpec((width, part), lambda i, at: (0, at[0]))
    piece = whole(width, part)
    grad_rows = [model // 2] * 2 if square else [model]
    outs = call(
        partial(hidden_back_kernel, experts),
        (1,),
        [
            *[whole(part + 16, model)] * 4,
            row_block,
            row_block,
            whole(8, model),
            router_block,
            pl.BlockSpec((1, part), lambda i, at: (0, at[0])),
            out_block,
            *[col_block] * 4,
        ],
        [*[piece] * 4, whole(part, model), whole(small_rows, model), whole(model, model)],
        [
            *[shaped((width, part), BF)] * 4,
            shaped((part, model), F32),
            shaped((small_rows, model), F32),
            shaped((model, model), BF),
        ],
        prefetch=1,
        name="hidden_back",
    )(at, *back_mine, hidden, grad_out, gains, small_all, chosen, small_all, *mixed_turns)
    dmix_out, d_hidden, small_grads, grad_out_w = outs[0:4], outs[4], outs[5], outs[6]
    dmix = scatter_turns(dmix_out)
    dmix, eo_out = lax.optimization_barrier((dmix, eo_out))
    eo_mine = scatter_turns(eo_out)

    dq_t, dkv, skew, sides = attention_bwd(
        info, table, qkv_all, docs, docs, band, mixed, lse, dmix, rows
    )
    dkv, eo_mine = lax.optimization_barrier((dkv, eo_mine))
    other = lax.dynamic_slice_in_dim(dkv, (1 - ctx_at) * rows, rows)
    got = lax.ppermute(other, "ctx", [(0, 1), (1, 0)])
    outs = call(
        partial(qkv_back_kernel, first_col, experts, heads),
        (blocks,),
        [
            pl.BlockSpec((width, BQ), lambda i, at: (0, i)),
            pl.BlockSpec((BQ, 2 * width), lambda i, at: (at[2] + i, 0)),
            pl.BlockSpec((BQ, 2 * width), lambda i, at: (i, 0)),
            pl.BlockSpec((BQ, model), lambda i, at: (at[2] + i, 0)),
            pl.BlockSpec((BQ, model), lambda i, at: (i, 0)),
            pl.BlockSpec((1, BQ), lambda i, at: (0, at[2] + i)),
            whole(8, model),
            whole(model, cols),
            whole(part, model),
            whole(model, model),
            whole(small_rows, model),
            whole(16, 2 * BK),
            whole(8, BQ),
            whole(span, LANES),
            whole(LANES, model),
        ],
        [
            pl.BlockSpec((model, BQ), lambda i, at: (0, i)),
            *[whole(n, late_at + LANES) for n in grad_rows],
        ],
        [
            shaped((model, rows), BF),
            *[shaped((n, late_at + LANES), BF) for n in grad_rows],
        ],
        scratch=[pltpu.VMEM((model, late_at + LANES), F32), pltpu.VMEM((8, model), F32)],
        prefetch=1,
        name="qkv_back",
    )(
        at, dq_t, dkv, got, normed_one, tokens, scale_one, gains, small_all, d_hidden, grad_out_w,
        small_grads, skew, sides, diag, spread,
    )
    terms, grad_dense = outs[0], outs[1:]
    terms, grad_experts = lax.optimization_barrier((terms, grad_experts))
    grad_tokens = lax.psum_scatter(terms, "tp", scatter_dimension=0, tiled=True).astype(F32)
    dense_cols = late_at + LANES
    piece_cols = -(-(LANES + width) // LANES) * LANES
    if square:
        keep, send = grad_dense
        pieces = call(
            pair_sum_kernel,
            (1,),
            [whole(4 * own, dense_cols)] * 2,
            [whole(own, dense_cols)] * 4,
            [shaped((own, dense_cols), BF)] * 4,
            name="dense_pair_sum",
        )(keep, xor_step(send, "ctx", 1))
        pieces = [pieces[0]] + [xor_step(pieces[s], "fsdp", s) for s in (1, 2, 3)]
    else:
        pieces = [lax.psum_scatter(grad_dense[0], dense, scatter_dimension=0, tiled=True)]
    grad_qkv, grad_late, *pieces = call(
        partial(dense_sum_kernel, wide_cols, len(pieces)),
        (1,),
        [whole(own, dense_cols)] * len(pieces),
        [whole(3, own, width), whole(LANES, own), *[whole(own, piece_cols)] * 4],
        [
            shaped((3, own, width), F32),
            shaped((LANES, own), F32),
            *[shaped((own, piece_cols), BF)] * 4,
        ],
        name="dense_sum",
    )(*pieces)
    pieces = [pieces[0]] + [turn(pieces[s], 4 - s) for s in (1, 2, 3)]
    grad_out_mine, grad_small = call(
        last_sum_kernel,
        (1,),
        [whole(own, piece_cols)] * 4,
        [whole(own, width), whole(LANES, own)],
        [shaped((own, width), F32), shaped((LANES, own), F32)],
        name="last_sum",
    )(*pieces)
    grad_table = grad_late[experts + 2 : experts + 2 + heads, 0:table_rows].T
    grad_router = grad_small[0:experts].T
    grad_gain_two = grad_small[experts]
    grad_gain_one = grad_small[experts + 1]

    hidden_share = after(hidden_share, grad_qkv)
    share_block = pl.BlockSpec((share, BQ), lambda i, *_: (0, i))
    out_share = call(
        out_kernel,
        (blocks,),
        [*[share_block] * 5, pl.BlockSpec((1, BQ), lambda i: (0, i))],
        share_block,
        shaped((share, rows), BF),
        name="layer_output",
    )(*eo_mine, hidden_share, gate_row)
    return (
        out_share.T,
        grad_tokens.T,
        grad_qkv.transpose(1, 0, 2),
        grad_out_mine,
        grad_table,
        grad_gain_one,
        grad_gain_two,
        grad_router,
        grad_experts[None, :, 0:ff].astype(F32),
        grad_experts[None, :, ff:].astype(F32),
    )


def solution(mesh):
    placed = (
        P(("fsdp", "ctx"), None),
        P(("fsdp", "ctx"), None),
        P(("fsdp", "ctx"), None, "tp"),
        P(("fsdp", "ctx"), "tp"),
        P(None, "tp"),
        P(("fsdp", "ctx")),
        P(("fsdp", "ctx")),
        P(("fsdp", "ctx"), None),
        P("fsdp", None, "tp"),
        P("fsdp", None, "tp"),
        P(("fsdp", "ctx"), None),
        P("fsdp"),
    )
    return jax.shard_map(
        shards,
        mesh=mesh,
        in_specs=placed,
        out_specs=(
            P(("fsdp", "ctx"), "tp"),
            P(("fsdp", "ctx"), "tp"),
            P(("fsdp", "ctx"), None, "tp"),
            P(("fsdp", "ctx"), "tp"),
            P(("fsdp", "ctx"), "tp"),
            P(("fsdp", "ctx")),
            P(("fsdp", "ctx")),
            P(("fsdp", "ctx"), None),
            P("fsdp", "ctx", "tp"),
            P("fsdp", "ctx", "tp"),
        ),
        check_vma=False,
    )
```

```python
from functools import partial

import jax
import jax.numpy as jnp
from jax import lax
from jax.experimental import pallas as pl
from jax.experimental.pallas import tpu as pltpu
from jax.sharding import PartitionSpec as P

norm_eps = 1e-06
bucket_edges = (12, 16, 23, 32, 46, 64, 91)
LANES = 128
TILE = 256
MIB = 1024 * 1024
NT = (((1,), (1,)), ((), ()))
TN = (((0,), (0,)), ((), ()))


BQ = 256
BK = 256
HD = 64
NEG = -1e30
FLOOR = -1e28
F32 = jnp.float32
BF = jnp.bfloat16


def call(kernel, grid, in_specs, out_specs, out_shape, scratch=(), prefetch=0, vmem=58, name=None, aliases={}):
    return pl.pallas_call(
        kernel,
        grid_spec=pltpu.PrefetchScalarGridSpec(
            num_scalar_prefetch=prefetch,
            grid=grid,
            in_specs=in_specs,
            out_specs=out_specs,
            scratch_shapes=list(scratch),
        ),
        out_shape=out_shape,
        input_output_aliases=aliases,
        compiler_params=pltpu.CompilerParams(
            dimension_semantics=("arbitrary",) * len(grid), vmem_limit_bytes=vmem * MIB
        ),
        cost_estimate=pl.CostEstimate(
            flops=10**7, bytes_accessed=10**5, transcendentals=0
        ),
        name=name,
    )


def whole(*shape):
    return pl.BlockSpec(shape, lambda *_: (0,) * len(shape))


def shaped(shape, dtype):
    return jax.ShapeDtypeStruct(shape, dtype)


def relative_bucket(offset):
    distance = jnp.abs(offset)
    far_bucket = jnp.zeros_like(distance) + 8
    for edge in bucket_edges:
        far_bucket = far_bucket + (distance >= edge).astype(jnp.int32)
    result = jnp.where(distance < 8, distance, far_bucket)
    return result + jnp.where(offset > 0, 16, 0)


def dot(a, b, dims=None):
    if dims is None:
        return jnp.dot(a, b, preferred_element_type=F32)
    return lax.dot_general(a, b, dims, preferred_element_type=F32)


def to_row(column):
    n = column.shape[0]
    return jnp.broadcast_to(column, (n, LANES)).T[0:1, :]


def to_column(row):
    n = row.shape[1]
    return jnp.broadcast_to(row, (LANES, n)).T[:, 0:1]


def split3(x):
    hi = x.astype(BF)
    rest = x - hi.astype(F32)
    mid = rest.astype(BF)
    low = (rest - mid.astype(F32)).astype(BF)
    return hi, mid, low


def key_side(docs_col, rows):
    lane = lax.broadcasted_iota(jnp.int32, (rows, HD), 1)
    same = (docs_col == lane.astype(F32)).astype(F32)
    ones = jnp.where((lane >= 4) & (lane < 7), 1.0, 0.0)
    return jnp.where(lane < 4, same, ones)


def query_side(docs_row, cols, tail):
    row = lax.broadcasted_iota(jnp.int32, (HD, cols), 0)
    other = jnp.where((row < 4) & (docs_row != row.astype(F32)), NEG, 0.0)
    if tail is None:
        return other.astype(BF)
    hi, mid, low = (t.astype(F32) for t in split3(tail))
    part = jnp.where(row == 4, hi, jnp.where(row == 5, mid, jnp.where(row == 6, low, 0.0)))
    return jnp.where(row < 4, other, part).astype(BF)


def shifted(x, by):
    return x if by == 0 else pltpu.roll(x, x.shape[1] - by, 1)


def diagonal_sums(tile):
    total = jnp.zeros((8, 2 * BQ), F32)
    for first in range(0, BK, 8):
        strip = tile[first : first + 8, :]
        total = total + shifted(jnp.concatenate([strip, jnp.zeros((8, BQ), F32)], axis=1), first)
    result = jnp.zeros((1, 2 * BQ), F32)
    for r in range(8):
        result = result + shifted(total, r)[r : r + 1, :]
    return result


def ones_rows(cols):
    return jnp.where(lax.broadcasted_iota(jnp.int32, (16, cols), 0) == 0, 1.0, 0.0).astype(BF)


def fwd_kernel(heads, first_block, blocks, info, far, qkv_ref, dcol, drow, band, *refs):
    i = pl.program_id(0)
    width = heads * HD
    block = first_block + i
    qb = info[0, 0] + block
    lo = info[0, 1 + block]
    hi = info[0, 1 + blocks + block]
    if first_block:
        k_aug, v_t, _, _, mixed_ref, low_ref, lse_ref = refs
        q = qkv_ref[:, 0:width]
    else:
        mixed_ref, low_ref, lse_ref, k_aug, v_t = refs
        q = qkv_ref[pl.ds(pl.multiple_of(qb * BQ, BQ), BQ), 0:width]

        @pl.when(i == 0)
        def _():
            for r in range(qkv_ref.shape[0] // BK):
                rows = pl.ds(r * BK, BK)
                side = key_side(to_column(dcol[:, r * BK : (r + 1) * BK]), BK).astype(BF)
                vt = qkv_ref[rows, 2 * width : 3 * width].astype(F32).T.astype(BF)
                for h in range(heads):
                    k = qkv_ref[rows, width + h * HD : width + (h + 1) * HD]
                    k_aug[h, rows, :] = jnp.concatenate([k, side], axis=1)
                    v_t[h, 0:HD, rows] = vt[h * HD : (h + 1) * HD, :]
                    v_t[h, HD : HD + 16, rows] = ones_rows(BK)

    qt = (q.astype(F32) * (HD**-0.5)).T.astype(BF)
    side = query_side(drow[...], BQ, None)
    q_aug = [jnp.concatenate([qt[h * HD : (h + 1) * HD, :], side], axis=0) for h in range(heads)]

    def step(kb, carry, bias_of):
        rows = pl.ds(pl.multiple_of(kb * BK, BK), BK)
        out = []
        for h in range(heads):
            peak, acc = carry[h]
            s = jnp.dot(k_aug[h, rows, :], q_aug[h], preferred_element_type=F32)
            s = s + bias_of(h, kb)
            new = jnp.maximum(peak, jnp.max(s, axis=0, keepdims=True))
            p = jnp.exp(s - new).astype(BF)
            acc = acc * jnp.exp(peak - new) + jnp.dot(v_t[h, :, rows], p, preferred_element_type=F32)
            out.append((new, acc))
        return tuple(out)

    carry = tuple(
        (jnp.full((1, BQ), FLOOR, F32), jnp.zeros((HD + 16, BQ), F32)) for _ in range(heads)
    )
    carry = lax.fori_loop(lo, jnp.minimum(hi, qb - 1), lambda kb, c: step(kb, c, lambda h, _: far[h, 15]), carry)
    carry = lax.fori_loop(
        jnp.maximum(lo, qb - 1),
        jnp.minimum(hi, qb + 2),
        lambda kb, c: step(kb, c, lambda h, t: band[h, t - qb + 1]),
        carry,
    )
    carry = lax.fori_loop(jnp.maximum(lo, qb + 2), hi, lambda kb, c: step(kb, c, lambda h, _: far[h, 31]), carry)
    for h in range(heads):
        peak, acc = carry[h]
        total = acc[HD : HD + 1, :]
        mixed = acc[0:HD, :] / total
        mixed_ref[h * HD : (h + 1) * HD, :] = mixed
        low_ref[h * HD : (h + 1) * HD, :] = mixed.astype(BF)
        lse_ref[h : h + 1, :] = peak + jnp.log(total)


def attention_fwd(info, far, qkv_all, docs, band, rows, before=None):
    seq, cols = qkv_all.shape
    width = cols // 3
    heads = width // HD
    blocks = rows // BQ
    steps = blocks // 2
    first = 0 if before is None else steps
    full = lambda shape: pl.BlockSpec(shape, lambda i, info: (0,) * len(shape))
    kept = [(heads, seq, 2 * HD), (heads, HD + 16, seq)]
    out_specs = [
        pl.BlockSpec((width, BQ), lambda i, info: (0, first + i)),
        pl.BlockSpec((width, BQ), lambda i, info: (0, i)),
        pl.BlockSpec((heads, BQ), lambda i, info: (0, first + i)),
    ]
    out_shape = [
        jax.ShapeDtypeStruct((width, rows), F32),
        jax.ShapeDtypeStruct((width, rows // 2), BF),
        jax.ShapeDtypeStruct((heads, rows), F32),
    ]
    in_specs = [
        pl.BlockSpec(memory_space=pltpu.SMEM),
        full((seq, cols)) if before is None else pl.BlockSpec((BQ, cols), lambda i, info: (info[0, 0] + first + i, 0)),
        full((1, seq)),
        pl.BlockSpec((1, BQ), lambda i, info: (0, info[0, 0] + first + i)),
        full((heads, 3, BK, BQ)),
    ]
    operands = [info, far, qkv_all, docs, docs, band]
    aliases = {}
    if before is None:
        out_specs += [full(s) for s in kept]
        out_shape += [jax.ShapeDtypeStruct(s, BF) for s in kept]
    else:
        mixed, lse, k_aug, v_t = before
        in_specs += [full(s) for s in kept] + [pl.BlockSpec(memory_space=pl.ANY)] * 2
        operands += [k_aug, v_t, mixed, lse]
        aliases = {8: 0, 9: 2}
    return pl.pallas_call(
        partial(fwd_kernel, heads, first, blocks),
        grid_spec=pltpu.PrefetchScalarGridSpec(
            num_scalar_prefetch=1, grid=(steps,), in_specs=in_specs, out_specs=out_specs
        ),
        out_shape=out_shape,
        input_output_aliases=aliases,
        compiler_params=pltpu.CompilerParams(
            dimension_semantics=("arbitrary",), vmem_limit_bytes=58 * 1024 * 1024
        ),
        cost_estimate=pl.CostEstimate(flops=10**7, bytes_accessed=10**5, transcendentals=0),
        name="attention_fwd",
    )(*operands)


def bwd_kernel(
    heads, info, far, qkv_all, dcol, drow, band, mixed_ref, lse_ref, m0, m1, m2, m3, k_aug,
    dq_ref, dkv_ref, skew_ref, side_ref, v_aug, k_t, near_acc, dkv_acc,
):
    i = pl.program_id(0)
    seq = qkv_all.shape[0]
    width = heads * HD

    @pl.when(i == 0)
    def _():
        near_acc[...] = jnp.zeros_like(near_acc)
        dkv_acc[...] = jnp.zeros_like(dkv_acc)
        side_ref[...] = jnp.zeros_like(side_ref)
        for r in range(seq // BK):
            rows = pl.ds(r * BK, BK)
            lane = lax.broadcasted_iota(jnp.int32, (BK, HD), 1)
            ones = jnp.where(lane < 3, 1.0, 0.0).astype(BF)
            kt = qkv_all[rows, width : 2 * width].astype(F32).T.astype(BF)
            for h in range(heads):
                v = qkv_all[rows, 2 * width + h * HD : 2 * width + (h + 1) * HD]
                v_aug[h, rows, :] = jnp.concatenate([v, ones], axis=1)
                k_t[h, 0:HD, rows] = kt[h * HD : (h + 1) * HD, :]
                k_t[h, HD : HD + 16, rows] = ones_rows(BK)

    steps = pl.num_programs(0)
    block = lax.rem(info[0, 1 + 2 * steps] + steps - i, steps)
    qb = info[0, 0] + block
    lo = info[0, 1 + block]
    hi = info[0, 1 + steps + block]
    dmix = m0[...]
    for s, ref in ((1, m1), (2, m2), (3, m3)):
        dmix = jnp.where(i == s, ref[...], dmix)
    q_scaled = qkv_all[pl.ds(pl.multiple_of(qb * BQ, BQ), BQ), 0:width].astype(F32) * (HD**-0.5)
    qt = q_scaled.T.astype(BF)
    q_rows = q_scaled.astype(BF)
    dmix_t = dmix.astype(F32)
    dmix_rows = dmix_t.T.astype(BF)
    zero = jnp.zeros((BQ, HD), BF)
    row = lax.broadcasted_iota(jnp.int32, (HD, BQ), 0)
    q_aug, d_aug, rhs = [], [], []
    for h in range(heads):
        cols = slice(h * HD, (h + 1) * HD)
        lse = lse_ref[h : h + 1, :]
        kinds = []
        for tail in (far[h, 15] - lse, -lse, far[h, 31] - lse):
            kinds.append(jnp.concatenate([qt[cols, :], query_side(drow[...], BQ, tail)], axis=0))
        q_aug.append(kinds)
        delta = -jnp.sum(dmix_t[cols, :] * mixed_ref[cols, :], axis=0, keepdims=True)
        a, b, c = (t.astype(F32) for t in split3(delta))
        part = jnp.where(row == 0, a, jnp.where(row == 1, b, jnp.where(row == 2, c, 0.0)))
        d_aug.append(jnp.concatenate([dmix_t[cols, :].astype(BF), part.astype(BF)], axis=0))
        top = jnp.concatenate([dmix_rows[:, cols], zero], axis=1)
        low = jnp.concatenate([zero, q_rows[:, cols]], axis=1)
        rhs.append(jnp.concatenate([top, low], axis=0))

    def step(kb, carry, kind):
        rows = pl.ds(pl.multiple_of(kb * BK, BK), BK)
        out = []
        for h in range(heads):
            s = jnp.dot(k_aug[h, rows, :], q_aug[h][kind], preferred_element_type=F32)
            if kind == 1:
                s = s + band[h, kb - qb + 1]
            p = jnp.exp(s)
            dp = jnp.dot(v_aug[h, rows, :], d_aug[h], preferred_element_type=F32)
            ds = p * dp
            ds_low = ds.astype(BF)
            if kind == 1:
                near_acc[h, kb - qb + 1] = near_acc[h, kb - qb + 1] + ds_low.astype(F32)
            both = jnp.concatenate([p.astype(BF), ds_low], axis=1)
            dkv_acc[h, rows, :] += jnp.dot(both, rhs[h], preferred_element_type=F32)
            out.append(carry[h] + jnp.dot(k_t[h, :, rows], ds_low, preferred_element_type=F32))
        return tuple(out)

    zero_dq = jnp.zeros((HD + 16, BQ), F32)
    left = lax.fori_loop(lo, jnp.minimum(hi, qb - 1), lambda kb, c: step(kb, c, 0), (zero_dq,) * heads)
    near = lax.fori_loop(
        jnp.maximum(lo, qb - 1), jnp.minimum(hi, qb + 2), lambda kb, c: step(kb, c, 1), left
    )
    last = lax.fori_loop(jnp.maximum(lo, qb + 2), hi, lambda kb, c: step(kb, c, 2), near)
    for h in range(heads):
        dq_ref[h * HD : (h + 1) * HD, :] = (last[h][0:HD, :] * (HD**-0.5)).astype(BF)
        side_ref[2 * h : 2 * h + 1, :] += left[h][HD : HD + 1, :]
        side_ref[2 * h + 1 : 2 * h + 2, :] += last[h][HD : HD + 1, :] - near[h][HD : HD + 1, :]

    @pl.when(i == pl.num_programs(0) - 1)
    def _():
        for h in range(heads):
            for t in range(3):
                skew_ref[3 * h + t : 3 * h + t + 1, :] = diagonal_sums(near_acc.at[h, t])
        for r in range(seq // BK):
            rows = pl.ds(r * BK, BK)
            acc = [dkv_acc[h, rows, :] for h in range(heads)]
            dk = [a[:, HD : 2 * HD] for a in acc]
            dv = [a[:, 0:HD] for a in acc]
            dkv_ref[rows, :] = jnp.concatenate(dk + dv, axis=1).astype(BF)


def attention_bwd(info, far, qkv_all, dcol, drow, band, mixed, lse, dmix, k_aug, rows):
    seq, cols = qkv_all.shape
    width = cols // 3
    heads = width // HD
    steps = rows // BQ
    full = lambda shape: pl.BlockSpec(shape, lambda i, info: (0,) * len(shape))
    block = lambda i, info: lax.rem(info[0, 1 + 2 * steps] + steps - i, steps)
    return pl.pallas_call(
        partial(bwd_kernel, heads),
        grid_spec=pltpu.PrefetchScalarGridSpec(
            num_scalar_prefetch=1,
            grid=(steps,),
            in_specs=[
                pl.BlockSpec(memory_space=pltpu.SMEM),
                full((seq, cols)),
                full((1, seq)),
                pl.BlockSpec((1, BQ), lambda i, info: (0, info[0, 0] + block(i, info))),
                full((heads, 3, BK, BQ)),
                pl.BlockSpec((width, BQ), lambda i, info: (0, block(i, info))),
                pl.BlockSpec((heads, BQ), lambda i, info: (0, block(i, info))),
                *[full((width, BQ))] * 4,
                full((heads, seq, 2 * HD)),
            ],
            out_specs=[
                pl.BlockSpec((width, BQ), lambda i, info: (0, block(i, info))),
                full((seq, 2 * width)),
                full((16, 2 * BK)),
                full((8, BQ)),
            ],
            scratch_shapes=[
                pltpu.VMEM((heads, seq, 2 * HD), BF),
                pltpu.VMEM((heads, HD + 16, seq), BF),
                pltpu.VMEM((heads, 3, BK, BQ), F32),
                pltpu.VMEM((heads, seq, 2 * HD), F32),
            ],
        ),
        out_shape=[
            jax.ShapeDtypeStruct((width, rows), BF),
            jax.ShapeDtypeStruct((seq, 2 * width), BF),
            jax.ShapeDtypeStruct((16, 2 * BK), F32),
            jax.ShapeDtypeStruct((8, BQ), F32),
        ],
        compiler_params=pltpu.CompilerParams(
            dimension_semantics=("arbitrary",), vmem_limit_bytes=58 * 1024 * 1024
        ),
        cost_estimate=pl.CostEstimate(
            flops=10**7, bytes_accessed=10**5, transcendentals=0
        ),
        name="attention_bwd",
    )(info, far, qkv_all, dcol, drow, band, mixed, lse, *dmix, k_aug)


def plan_kernel(
    experts, own, table_rows, at, ids_ref, docs_ref, table_ref,
    pos_ref, owner_ref, chosen_ref, docs_out, info_ref, band_ref, diag_ref, spread_ref,
):
    rows = ids_ref.shape[1]
    seq = docs_ref.shape[1]
    heads = band_ref.shape[0]
    buckets = table_ref.shape[1]
    blocks = rows // BQ
    chosen = ids_ref[...].astype(F32)
    chosen_ref[...] = chosen
    docs = docs_ref[...].astype(F32)
    docs_out[...] = docs
    expert_rows = -(-experts // 8) * 8
    one_hot = lax.broadcasted_iota(jnp.int32, (expert_rows, rows), 0).astype(F32) == chosen
    one_hot = jnp.where(one_hot, 1.0, 0.0)
    low_rows = lax.broadcasted_iota(jnp.int32, (rows, rows), 0)
    before = jnp.where(low_rows < lax.broadcasted_iota(jnp.int32, (rows, rows), 1), 1.0, 0.0)
    earlier = dot(one_hot.astype(BF), before.astype(BF))
    lane = lax.broadcasted_iota(jnp.int32, (1, LANES), 1)
    lane_f = lane.astype(F32)
    pos = jnp.zeros((1, rows), F32)
    owner = jnp.zeros((1, LANES), F32)
    end = jnp.zeros((1, 1), F32)
    for e in range(experts):
        hit = one_hot[e : e + 1, :]
        count = jnp.sum(hit, axis=1, keepdims=True)
        pos = pos + hit * (earlier[e : e + 1, :] + end * TILE)
        end = end + jnp.maximum(jnp.floor((count + (TILE - 1)) * (1.0 / TILE)), 1.0)
        owner = owner + jnp.where(end <= lane_f, 1.0, 0.0)
    pos_ref[...] = pos.astype(jnp.int32)
    owner = jnp.minimum(owner, experts - 1.0)
    owner_ref[...] = jnp.where(lane == LANES - 1, end, owner).astype(jnp.int32)
    base = at[2]
    info = jnp.where(lane == 0, base, jnp.where(lane == 1 + 2 * blocks, at[0], 0)).astype(F32)
    for b in range(seq // BQ):
        first = docs[:, b * BQ : b * BQ + 1]
        last = docs[:, (b + 1) * BQ - 1 : (b + 1) * BQ]
        low = jnp.sum(jnp.where(docs < first, 1.0, 0.0), axis=1, keepdims=True)
        high = jnp.sum(jnp.where(docs <= last, 1.0, 0.0), axis=1, keepdims=True)
        here = (b >= base) & (b < base + blocks)
        low_at = (lane == 1 + b - base) & here
        high_at = (lane == 1 + blocks + b - base) & here
        info = info + jnp.where(low_at, jnp.floor(low * (1.0 / BK)), 0.0)
        info = info + jnp.where(high_at, jnp.floor((high + (BK - 1)) * (1.0 / BK)), 0.0)
    info_ref[...] = info.astype(jnp.int32)
    span = 3 * 2 * BQ
    column = lax.broadcasted_iota(jnp.int32, (8, span), 1)
    tile = (column >= 2 * BQ).astype(jnp.int32) + (column >= 4 * BQ).astype(jnp.int32)
    inside = column - tile * (2 * BQ)
    wrapped = jnp.where(inside < BQ, inside, inside - 2 * BQ)
    bucket = relative_bucket((tile - 1) * BK - wrapped)[0:1, :].astype(F32)
    which = lax.broadcasted_iota(jnp.int32, (buckets, span), 0).astype(F32)
    pick = jnp.where(which == bucket, 1.0, 0.0).astype(BF)
    wide = jnp.concatenate([table_ref[...], jnp.zeros((8 - heads, buckets), F32)], axis=0)
    vectors = sum(dot(p, pick) for p in split3(wide))
    for h in range(heads):
        for t in range(3):
            line = vectors[h : h + 1, t * 2 * BQ : (t + 1) * 2 * BQ]
            wide = jnp.broadcast_to(line, (BK, 2 * BQ))
            band_ref[h, t] = pltpu.roll(wide, 0, 1, stride=1, stride_axis=0)[:, 0:BQ]
    by_column = to_column(bucket)
    lanes = lax.broadcasted_iota(jnp.int32, (span, LANES), 1).astype(F32)
    diag_ref[...] = jnp.where(by_column == lanes, 1.0, 0.0).astype(BF)
    model = spread_ref.shape[1]
    row_ids = lax.broadcasted_iota(jnp.int32, (8, model), 1)
    target = jnp.full((8, model), -1, jnp.int32)
    for b in range(buckets):
        target = jnp.where(row_ids == b // table_rows * own + b % table_rows, b, target)
    down = lax.broadcasted_iota(jnp.int32, (LANES, model), 0).astype(F32)
    spread_ref[...] = jnp.where(down == target[0:1, :].astype(F32), 1.0, 0.0).astype(BF)


def pack_kernel(qkv_ref, router_ref, one_ref, two_ref, out_ref):
    experts, rows = router_ref.shape
    fill = jnp.zeros((LANES - experts - 2, rows), F32)
    tail = [r[...].astype(F32) for r in (router_ref, one_ref, two_ref)]
    tail = jnp.concatenate([*tail, fill], axis=0).T.astype(BF)
    parts = [qkv_ref[c] for c in range(3)]
    used = sum(p.shape[1] for p in parts)
    gap = out_ref.shape[1] - used - LANES
    if gap:
        parts.append(jnp.zeros((rows, gap), BF))
    out_ref[...] = jnp.concatenate([*parts, tail], axis=1)


def qkv_kernel(
    first_col, cols, experts, count, at, own_ref, other_ref, *refs
):
    pieces = refs[:count]
    qkv_ref, norm_ref, scale_ref, small_ref, gains_ref = refs[count:]
    i = pl.program_id(0)

    @pl.when(i == 0)
    def _():
        slot = 0
        for piece in pieces:
            for s in range(piece.shape[0]):
                first = pl.multiple_of(at[4 + slot], 16)
                small_ref[pl.ds(first, piece.shape[1]), :] = piece[s]
                slot += 1
        tail = small_ref[:, small_ref.shape[1] - LANES :].astype(F32).T
        gains_ref[...] = tail[experts : experts + 8, :]

    x = jnp.where(i < pl.num_programs(0) // 2, own_ref[...], other_ref[...]).astype(F32)
    scale = lax.rsqrt(jnp.mean(x * x, axis=-1, keepdims=True) + norm_eps)
    normed = (x * scale * gains_ref[0:1, :]).astype(BF)
    norm_ref[...] = normed
    scale_ref[...] = to_row(scale)
    qkv_ref[...] = dot(normed, small_ref[:, first_col : first_col + cols]).astype(BF)


def router_parts(hidden, gain, router, chosen, experts):
    scale = lax.rsqrt(jnp.mean(hidden * hidden, axis=-1, keepdims=True) + norm_eps)
    hat = hidden * scale
    normed = (hat * gain).astype(BF)
    lane = lax.broadcasted_iota(jnp.int32, (hidden.shape[0], LANES), 1)
    logits = jnp.where(lane < experts, dot(normed, router), NEG)
    weights = jnp.exp(logits - jnp.max(logits, axis=-1, keepdims=True))
    route = weights / jnp.sum(weights, axis=-1, keepdims=True)
    one_hot = jnp.where(lane.astype(F32) == chosen, 1.0, 0.0)
    gate = jnp.sum(route * one_hot, axis=-1, keepdims=True)
    return scale, hat, normed, route, one_hot, gate


def hidden_kernel(experts, skipped, at, *refs):
    tok_ref, mix_refs, wout_ref = refs[0], refs[1:5], refs[5]
    gains_ref, small_ref, chosen_ref = refs[6:9]
    hidden_ref, norm_ref, gate_ref, share_ref, turn_s = refs[9 + skipped :]
    mixed = jnp.concatenate([r[...] for r in mix_refs], axis=0).astype(F32).T.astype(BF)
    hidden = tok_ref[...].astype(F32) + dot(mixed, wout_ref[...], NT)
    parts = router_parts(hidden, gains_ref[1:2, :], small_ref[...], to_column(chosen_ref[...]), experts)
    hidden_ref[...] = hidden
    norm_ref[...] = parts[2]
    gate_ref[...] = to_row(parts[5])
    turn_s[...] = hidden.T
    share = share_ref.shape[0]
    share_ref[...] = turn_s[pl.ds(pl.multiple_of(at[0] * share, share), share), :]


def pick_back(pos_col, total):
    place = lax.broadcasted_iota(jnp.int32, (pos_col.shape[0], total), 1).astype(F32)
    return jnp.where(pos_col == place, 1.0, 0.0).astype(BF)


def unsort_kernel(owner, at, pos_row, sorted_ref, e0, e1, e2, e3, pos_col, turn_s):
    rows = pos_row.shape[1]
    part = turn_s.shape[1]
    pos_col[...] = jnp.broadcast_to(pos_row[...].astype(F32), (LANES, rows)).T
    for g in range(rows // part):
        mine = slice(g * part, (g + 1) * part)
        pick = pick_back(pos_col[mine, 0:1], sorted_ref.shape[0])
        turn_s[...] = dot(pick, sorted_ref[...]).T.astype(BF)
        for step, out in enumerate((e0, e1, e2, e3)):
            share = out.shape[0]
            first = pl.multiple_of(lax.rem(at[0] + step, 4) * share, share)
            out[:, mine] = turn_s[pl.ds(first, share), :]


def expert_kernel(
    owner, at, pos_row, norm_ref, cot_ref, gate_ref, w_ref,
    b0, b1, b2, b3, eo_ref, x_ref, de_ref, act_ref, di_ref, dr_s, pos_col,
):
    i = pl.program_id(0)
    z = at[0]
    rows = norm_ref.shape[0]
    width = norm_ref.shape[1]
    ff = w_ref.shape[1] // 2
    here = pl.ds(pl.multiple_of(i * TILE, TILE), TILE)
    used = i < owner[0, LANES - 1]

    @pl.when(used)
    def _():
        place = lax.broadcasted_iota(jnp.int32, (TILE, rows), 0) + i * TILE
        hit = pos_row[...] == place
        pick = jnp.where(hit, 1.0, 0.0).astype(BF)
        x = dot(pick, norm_ref[...]).astype(BF)
        cot = dot(pick, cot_ref[...])
        gate = jnp.sum(jnp.where(hit, gate_ref[...], 0.0), axis=1, keepdims=True)
        d_e = (gate * cot).astype(BF)
        w_in = w_ref[:, 0:ff]
        w_down = w_ref[:, ff : 2 * ff]
        d_act = dot(d_e, w_down)
        inner = dot(x, w_in)
        half = 0.5 * (1.0 + lax.erf(inner * (0.5**0.5)))
        active = (inner * half).astype(BF)
        slope = half + inner * (jnp.exp(-0.5 * inner * inner) * 0.3989422804014327)
        d_inner = (d_act * slope).astype(BF)
        d_rows = dot(d_inner, w_in, NT)
        terms = dot(active, w_down, NT)
        d_gate = jnp.sum(cot * terms, axis=1, keepdims=True)
        lane = lax.broadcasted_iota(jnp.int32, (TILE, LANES), 1)
        hi, mid, low = (t.astype(F32) for t in split3(d_gate))
        extra = jnp.where(lane == 0, hi, jnp.where(lane == 1, mid, jnp.where(lane == 2, low, 0.0)))
        dr_s[here, :] = jnp.concatenate([d_rows.astype(BF), extra.astype(BF)], axis=1)
        eo_ref[...] = terms.astype(BF)
        x_ref[...] = x
        de_ref[...] = d_e
        act_ref[...] = active
        di_ref[...] = d_inner

    @pl.when(jnp.logical_not(used))
    def _():
        dr_s[here, :] = jnp.zeros((TILE, dr_s.shape[1]), BF)
        for ref in (eo_ref, x_ref, de_ref, act_ref, di_ref):
            ref[...] = jnp.zeros_like(ref)

    @pl.when(i == pl.num_programs(0) - 1)
    def _():
        part = rows // 4
        pos_col[...] = jnp.broadcast_to(pos_row[...].astype(F32), (LANES, rows)).T
        for r, back_ref in enumerate((b0, b1, b2, b3)):
            g = lax.rem(z + r, 4)
            mine = pl.ds(pl.multiple_of(g * part, part), part)
            back = dot(pick_back(pos_col[mine, 0:1], dr_s.shape[0]), dr_s[...])
            back_ref[0:part, :] = back[:, 0:width].astype(BF)
            tail = back[:, width : width + LANES].T
            d_gate = tail[0:1, :] + tail[1:2, :] + tail[2:3, :]
            row = lax.broadcasted_iota(jnp.int32, (16, part), 0)
            strip = jnp.where(row == 0, jnp.broadcast_to(d_gate, (16, part)), 0.0)
            fill = jnp.zeros((16, width - part), F32)
            back_ref[part : part + 16, :] = jnp.concatenate([strip, fill], axis=1).astype(BF)


def weight_grad_kernel(owner, x_ref, di_ref, de_ref, act_ref, out_ref, acc):
    i = pl.program_id(0)
    last = pl.num_programs(0) - 1
    me = owner[0, i]
    before = owner[0, jnp.maximum(i - 1, 0)]
    after = owner[0, jnp.minimum(i + 1, last)]
    ff = di_ref.shape[1]

    first = (i == 0) | (before != me)
    used = i < owner[0, LANES - 1]

    @pl.when(first)
    def _():
        acc[:, 0:ff] = dot(x_ref[...], di_ref[...], TN)
        acc[:, ff : 2 * ff] = dot(de_ref[...], act_ref[...], TN)

    @pl.when(jnp.logical_not(first) & used)
    def _():
        acc[:, 0:ff] += dot(x_ref[...], di_ref[...], TN)
        acc[:, ff : 2 * ff] += dot(de_ref[...], act_ref[...], TN)

    @pl.when((i == last) | (after != me))
    def _():
        out_ref[...] = acc[...].astype(BF)


def split_rows(at, first_slot, acc, outs):
    if len(outs) == 1:
        outs[0][...] = acc[...].astype(BF)
        return
    slot = first_slot
    for out in outs:
        step = out.shape[0] // 4
        for s in range(4):
            first = pl.multiple_of(at[slot], 8)
            out[s * step : (s + 1) * step, :] = acc[pl.ds(first, step), :].astype(BF)
            slot += 1


def hidden_back_kernel(experts, at, *refs):
    back_refs, (hidden_ref, cot_ref, gains_ref, router_ref, chosen_ref) = refs[:4], refs[4:9]
    wout_ref, mix_refs = refs[9], refs[10:18]
    dmix_refs, dh_ref, small_ref, gout_ref = refs[18:22], refs[22], refs[23], refs[24]
    part, model = hidden_ref.shape
    back = sum(r[...].astype(F32) for r in back_refs)
    gain = gains_ref[1:2, :]
    router = router_ref[...]
    scale, hat, normed, route, one_hot, gate = router_parts(
        hidden_ref[...], gain, router, to_column(chosen_ref[...]), experts
    )
    d_gate = to_column(back[part : part + 1, 0:part])
    d_logits = (d_gate * gate) * (one_hot - route)
    parts = split3(d_logits)
    d_normed = back[0:part, :]
    g_router = jnp.zeros((LANES, model), F32)
    for p in parts:
        d_normed = d_normed + dot(p, router, NT)
        g_router = g_router + dot(p, normed, TN)
    small_ref[...] = jnp.zeros_like(small_ref)
    small_ref[0:experts, :] = g_router[0:experts, :]
    small_ref[experts : experts + 1, :] = jnp.sum(d_normed * hat, axis=0, keepdims=True)
    d_hat = d_normed * gain
    d_hidden = cot_ref[...].astype(F32) + scale * (
        d_hat - hat * jnp.mean(d_hat * hat, axis=-1, keepdims=True)
    )
    d_attn = d_hidden.astype(BF)
    d_attn_t = d_hidden.T.astype(BF)
    d_mixed = dot(d_attn, wout_ref[...]).T.astype(BF)
    width = model // 4
    for s in range(4):
        dmix_refs[(4 - s) % 4][...] = d_mixed[s * width : (s + 1) * width, :]
    dh_ref[...] = d_hidden
    one, two = (jnp.concatenate([r[...] for r in mix_refs[n : n + 4]], axis=0) for n in (0, 4))
    mixed = jnp.where(at[0] < 2, one, two)
    gout_ref[...] = dot(d_attn_t, mixed, NT).astype(BF)


def qkv_back_kernel(
    first_col, experts, heads, at, dq_ref, dkv_ref, got_ref, norm_ref, tok_ref, scale_ref, gains_ref, w_ref,
    dh_ref, gout_ref, small_ref, skew_ref, sides_ref, diag_ref, spread_ref,
    terms_ref, *rest,
):
    *gw_refs, acc, gain_s = rest
    i = pl.program_id(0)
    width = dq_ref.shape[0]
    cols = 3 * width
    model = tok_ref.shape[1]
    dkv = dkv_ref[...].astype(F32) + got_ref[...].astype(F32)
    d_qkv = jnp.concatenate([dq_ref[...].astype(F32).T, dkv], axis=1).astype(BF)
    scale = to_column(scale_ref[...])
    hat = tok_ref[...].astype(F32) * scale
    terms = dot(d_qkv, w_ref[:, first_col : first_col + cols], NT)
    d_hat = terms * gains_ref[0:1, :]
    mean = jnp.mean(d_hat * hat, axis=-1, keepdims=True)
    grad = scale * (d_hat - hat * mean) + jnp.where(i == at[0], dh_ref[...], 0.0)

    @pl.when(i == 0)
    def _():
        wide = acc.shape[1] - model - LANES
        acc[:, 0:wide] = jnp.zeros((model, wide), F32)
        acc[:, wide : wide + model] = gout_ref[...].astype(F32)
        gain_s[...] = jnp.zeros_like(gain_s)

    gain_s[0:1, :] += jnp.sum(terms * hat, axis=0, keepdims=True)
    acc[:, 0:cols] += dot(norm_ref[...], d_qkv, TN)
    terms_ref[...] = grad.T.astype(BF)

    @pl.when(i == pl.num_programs(0) - 1)
    def _():
        rows = [small_ref[0 : experts + 1, :], gain_s[0:1, :]]
        lines = []
        sides = []
        for h in range(8):
            k = min(h, heads - 1)
            lines.append(jnp.concatenate([skew_ref[3 * k + t : 3 * k + t + 1, :] for t in range(3)], axis=1))
            sides.append(jnp.sum(sides_ref[2 * k : 2 * k + 2, :], axis=1, keepdims=True))
        lane = lax.broadcasted_iota(jnp.int32, (8, LANES), 1)
        table = sum(dot(p, diag_ref[...]) for p in split3(jnp.concatenate(lines, axis=0)))
        table = table + jnp.where(lane == 15, jnp.concatenate([s[0:1, :] for s in sides], axis=0), 0.0)
        table = table + jnp.where(lane == 31, jnp.concatenate([s[1:2, :] for s in sides], axis=0), 0.0)
        spread = sum(dot(p, spread_ref[...]) for p in split3(table))
        rows.append(spread[0:heads, :])
        rows.append(jnp.zeros((LANES - experts - 2 - heads, model), F32))
        acc[:, acc.shape[1] - LANES :] = jnp.concatenate(rows, axis=0).T
        split_rows(at, 4, acc, gw_refs)


def out_kernel(e0, e1, e2, e3, hidden_ref, gate_ref, out_ref):
    total = sum(r[...].astype(F32) for r in (e0, e1, e2, e3))
    out_ref[...] = (hidden_ref[...] + total * gate_ref[...]).astype(BF)


def pair_sum_kernel(keep_ref, got_ref, *outs):
    step = outs[0].shape[0]
    for s, out in enumerate(outs):
        rows = slice(s * step, (s + 1) * step)
        out[...] = (keep_ref[rows, :].astype(F32) + got_ref[rows, :].astype(F32)).astype(BF)


def dense_sum_kernel(cols, count, table_at, *refs):
    parts, (qkv_ref, table_ref, *outs) = refs[:count], refs[count:]
    total = sum(r[...].astype(F32) for r in parts)
    width = qkv_ref.shape[2]
    for c in range(3):
        qkv_ref[c] = total[:, c * width : (c + 1) * width]
    late = total[:, total.shape[1] - LANES :]
    table_rows, heads = table_ref.shape
    table_ref[...] = late[0:table_rows, table_at : table_at + heads]
    for s, out in enumerate(outs):
        piece = total[:, cols + s * width : cols + (s + 1) * width]
        gap = jnp.zeros((late.shape[0], out.shape[1] - LANES - width), F32)
        out[...] = jnp.concatenate([late, piece, gap], axis=1).astype(BF)


def last_sum_kernel(p0, p1, p2, p3, out_ref, router_ref, two_ref, one_ref):
    total = sum(r[...].astype(F32) for r in (p0, p1, p2, p3))
    out_ref[...] = total[:, LANES : LANES + out_ref.shape[1]]
    late = total[:, 0:LANES].T
    experts = router_ref.shape[0]
    router_ref[...] = late[0:experts, :]
    two_ref[...] = late[experts : experts + 1, :]
    one_ref[...] = late[experts + 1 : experts + 2, :]

def xor_step(x, axis, s):
    return lax.ppermute(x, axis, [(i, i ^ s) for i in range(lax.axis_size(axis))])


def turn(x, s):
    return lax.ppermute(x, "tp", [(i, (i + s) % 4) for i in range(4)])


def gather_turns(x):
    return [x] + [turn(x, s) for s in (1, 2, 3)]


def scatter_turns(pieces):
    return [pieces[0]] + [turn(pieces[r], r) for r in (1, 2, 3)]


def after(x, *others):
    return lax.optimization_barrier((x, others))[0]


def shards(
    tokens,
    grad_out,
    w_qkv,
    w_attn_out,
    rel_bias,
    gain_attn,
    gain_ffn,
    w_router,
    w_in,
    w_down,
    expert_ids,
    doc_ids,
):
    rows, model = tokens.shape
    heads = rel_bias.shape[1]
    width = w_qkv.shape[2]
    own = w_qkv.shape[0]
    experts = w_router.shape[1]
    ff = w_in.shape[2]
    seq = doc_ids.shape[0]
    fsdp_n = lax.axis_size("fsdp")
    ctx_n = lax.axis_size("ctx")
    tp_n = lax.axis_size("tp")
    fsdp_at = lax.axis_index("fsdp")
    ctx_at = lax.axis_index("ctx")
    tp_at = lax.axis_index("tp")
    dense_at = fsdp_at * ctx_n + ctx_at
    part = rows // tp_n
    share = model // tp_n
    blocks = rows // BQ
    dense = ("fsdp", "ctx")
    square = fsdp_n == 4 and ctx_n == 2

    wide_cols = -(-3 * width // LANES) * LANES
    late_at = wide_cols + model
    table_rows = rel_bias.shape[0] // (fsdp_n * ctx_n)
    if square:
        starts = [((fsdp_at ^ s) * 2 + c) * own for c in (ctx_at, 1 - ctx_at) for s in range(4)]
    else:
        starts = [0]
    at = jnp.stack([jnp.int32(v) for v in (tp_at, ctx_at, ctx_at * blocks, fsdp_at, *starts)])

    qkv_cols = 3 * width
    first_col = 0
    cols = -(-qkv_cols // LANES) * LANES + LANES
    small = call(
        pack_kernel,
        (1,),
        [
            whole(3, own, width),
            whole(experts, own),
            whole(1, own),
            whole(1, own),
        ],
        whole(own, cols),
        shaped((own, cols), BF),
        name="pack_small",
    )(
        w_qkv.transpose(1, 0, 2),
        w_router.T,
        gain_attn[None, :],
        gain_ffn[None, :],
    )
    out_line = jnp.concatenate(gather_turns(after(w_attn_out, small)), axis=1)
    out_all = lax.all_gather(out_line, dense, axis=0, tiled=True)
    tokens_other = xor_step(tokens, "ctx", 1)
    half = model // ctx_n
    w_half = jnp.concatenate(
        [lax.dynamic_slice_in_dim(w.reshape(-1, ff), ctx_at * half, half, 0) for w in (w_in, w_down)],
        axis=1,
    )

    tiles = (rows + experts * (TILE - 1)) // TILE
    span = 6 * BQ
    table = rel_bias.T
    pos, owner, chosen, docs, info, band, diag, spread = call(
        partial(plan_kernel, experts, own, table_rows),
        (1,),
        [whole(1, rows), whole(1, seq), whole(*table.shape)],
        [
            whole(1, rows),
            whole(1, LANES),
            whole(1, rows),
            whole(1, seq),
            whole(1, LANES),
            whole(heads, 3, BK, BQ),
            whole(span, LANES),
            whole(LANES, model),
        ],
        [
            shaped((1, rows), jnp.int32),
            shaped((1, LANES), jnp.int32),
            shaped((1, rows), F32),
            shaped((1, seq), F32),
            shaped((1, LANES), jnp.int32),
            shaped((heads, 3, BK, BQ), F32),
            shaped((span, LANES), BF),
            shaped((LANES, model), BF),
        ],
        prefetch=1,
        name="plan",
    )(at, expert_ids.T, doc_ids[None, :], table)
    if square:
        near = [small] + [xor_step(small, "fsdp", s) for s in (1, 2, 3)]
        near, w_half, band = lax.optimization_barrier((near, w_half, band))
        near = jnp.stack(near)
        small_parts = [near, xor_step(near, "ctx", 1)]
    else:
        small_parts = [lax.all_gather(small, dense, axis=0, tiled=True)[None]]
    small_parts, tokens_other, w_half = lax.optimization_barrier((small_parts, tokens_other, w_half))

    w_experts = lax.all_gather(w_half, dense, axis=0, tiled=True)

    steps = seq // BQ
    n_own = steps // 2
    turned = lambda i, at: jnp.where(i < n_own, at[2] + i, i - at[2])
    qkv_all, normed_one, scale_one, small_all, gains = call(
        partial(qkv_kernel, first_col, qkv_cols, experts, len(small_parts)),
        (steps,),
        [
            pl.BlockSpec((BQ, model), lambda i, at: (jnp.minimum(i, n_own - 1), 0)),
            pl.BlockSpec((BQ, model), lambda i, at: (jnp.maximum(i - n_own, 0), 0)),
            *[whole(*p.shape) for p in small_parts],
        ],
        [
            pl.BlockSpec((BQ, qkv_cols), lambda i, at: (turned(i, at), 0)),
            pl.BlockSpec((BQ, model), lambda i, at: (turned(i, at), 0)),
            pl.BlockSpec((1, BQ), lambda i, at: (0, turned(i, at))),
            whole(model, cols),
            whole(8, model),
        ],
        [
            shaped((seq, qkv_cols), BF),
            shaped((seq, model), BF),
            shaped((1, seq), F32),
            shaped((model, cols), BF),
            shaped((8, model), F32),
        ],
        prefetch=1,
        name="norm_qkv",
    )(at, tokens, tokens_other, *small_parts)
    mixed, low_one, lse, *kept = attention_fwd(info, table, qkv_all, docs, band, rows)
    turns_one = gather_turns(low_one)
    mixed, low_two, lse = attention_fwd(info, table, qkv_all, docs, band, rows, (mixed, lse, *kept))
    turns_one, low_two = lax.optimization_barrier((turns_one, low_two))
    turns_two = gather_turns(low_two)

    router_block = pl.BlockSpec((model, LANES), lambda i, at: (0, cols // LANES - 1))
    out_block = whole(model, model)

    def hidden_half(first, turns, before):
        anywhere = pl.BlockSpec(memory_space=pl.ANY)
        return call(
            partial(hidden_kernel, experts, len(before)),
            (blocks // 2,),
            [
                pl.BlockSpec((BQ, model), lambda i, at: (first + i, 0)),
                *[pl.BlockSpec((width, BQ), lambda i, at: (0, i))] * 4,
                out_block,
                whole(8, model),
                router_block,
                pl.BlockSpec((1, BQ), lambda i, at: (0, first + i)),
                *[anywhere] * len(before),
            ],
            [
                pl.BlockSpec((BQ, model), lambda i, at: (first + i, 0)),
                pl.BlockSpec((BQ, model), lambda i, at: (first + i, 0)),
                pl.BlockSpec((1, BQ), lambda i, at: (0, first + i)),
                pl.BlockSpec((share, BQ), lambda i, at: (0, first + i)),
            ],
            [
                shaped((rows, model), F32),
                shaped((rows, model), BF),
                shaped((1, rows), F32),
                shaped((share, rows), F32),
            ],
            scratch=[pltpu.VMEM((model, BQ), F32)],
            prefetch=1,
            aliases={10 + n: n for n in range(len(before))},
            name="hidden_router",
        )(at, tokens, *turns, out_all, gains, small_all, chosen, *before)

    half_done = hidden_half(0, turns_one, ())
    sorted_rows = tiles * TILE
    sorted_spec = lambda cols: pl.BlockSpec((TILE, cols), lambda i, *_: (i, 0))
    turns_two, half_done = lax.optimization_barrier((turns_two, half_done))
    hidden, normed_two, gate_row, hidden_share = hidden_half(blocks // 2, turns_two, half_done)
    *back, eo_sorted, x_sorted, d_expert, active, d_inner = call(
        expert_kernel,
        (tiles,),
        [
            whole(1, rows),
            whole(rows, model),
            whole(rows, model),
            whole(1, rows),
            pl.BlockSpec((model, 2 * ff), lambda i, owner, at: (owner[0, i], 0)),
        ],
        [
            *[whole(part + 16, model)] * 4,
            sorted_spec(model),
            sorted_spec(model),
            sorted_spec(model),
            sorted_spec(ff),
            sorted_spec(ff),
        ],
        [
            *[shaped((part + 16, model), BF)] * 4,
            shaped((sorted_rows, model), BF),
            shaped((sorted_rows, model), BF),
            shaped((sorted_rows, model), BF),
            shaped((sorted_rows, ff), BF),
            shaped((sorted_rows, ff), BF),
        ],
        scratch=[
            pltpu.VMEM((sorted_rows, model + LANES), BF),
            pltpu.VMEM((rows, LANES), F32),
        ],
        prefetch=2,
        name="experts",
    )(owner, at, pos, normed_two, grad_out, gate_row, w_experts)
    back_mine = scatter_turns(back)
    back_got = back_mine[1:]
    grad_experts = call(
        weight_grad_kernel,
        (tiles,),
        [sorted_spec(model), sorted_spec(ff), sorted_spec(model), sorted_spec(ff)],
        pl.BlockSpec((model, 2 * ff), lambda i, owner: (owner[0, i], 0)),
        shaped((experts * model, 2 * ff), BF),
        scratch=[pltpu.VMEM((model, 2 * ff), F32)],
        prefetch=1,
        name="expert_weight_grads",
    )(owner, x_sorted, d_inner, d_expert, active)
    eo_out = call(
        unsort_kernel,
        (1,),
        [whole(1, rows), whole(sorted_rows, model)],
        [whole(share, rows)] * 4,
        [shaped((share, rows), BF)] * 4,
        scratch=[pltpu.VMEM((rows, LANES), F32), pltpu.VMEM((model, part), BF)],
        prefetch=2,
        name="unsort_outputs",
    )(owner, at, pos, after(eo_sorted, grad_experts))
    grad_experts = lax.psum_scatter(after(grad_experts, back_got, eo_out), dense, scatter_dimension=0, tiled=True)

    back_mine, eo_out = lax.optimization_barrier((back_mine, eo_out))

    small_rows = -(-(experts + 1) // 8) * 8
    row_block = pl.BlockSpec((part, model), lambda i, at: (at[0], 0))
    col_one = pl.BlockSpec((width, part), lambda i, at: (0, jnp.minimum(at[0], 1)))
    col_two = pl.BlockSpec((width, part), lambda i, at: (0, jnp.maximum(at[0] - 2, 0)))
    piece = whole(width, part)
    grad_rows = [model // 2] * 2 if square else [model]
    outs = call(
        partial(hidden_back_kernel, experts),
        (1,),
        [
            *[whole(part + 16, model)] * 4,
            row_block,
            row_block,
            whole(8, model),
            router_block,
            pl.BlockSpec((1, part), lambda i, at: (0, at[0])),
            out_block,
            *[col_one] * 4,
            *[col_two] * 4,
        ],
        [*[piece] * 4, whole(part, model), whole(small_rows, model), whole(model, model)],
        [
            *[shaped((width, part), BF)] * 4,
            shaped((part, model), F32),
            shaped((small_rows, model), F32),
            shaped((model, model), BF),
        ],
        prefetch=1,
        name="hidden_back",
    )(at, *back_mine, hidden, grad_out, gains, small_all, chosen, out_all, *turns_one, *turns_two)
    dmix_out, d_hidden, small_grads, grad_out_w = outs[0:4], outs[4], outs[5], outs[6]
    dmix = scatter_turns(dmix_out)
    dmix, eo_out = lax.optimization_barrier((dmix, eo_out))
    eo_mine = scatter_turns(eo_out)

    dq_t, dkv, skew, sides = attention_bwd(
        info, table, qkv_all, docs, docs, band, mixed, lse, dmix, kept[0], rows
    )
    dkv, eo_mine = lax.optimization_barrier((dkv, eo_mine))
    other = lax.dynamic_slice_in_dim(dkv, (1 - ctx_at) * rows, rows)
    got = lax.ppermute(other, "ctx", [(0, 1), (1, 0)])
    outs = call(
        partial(qkv_back_kernel, first_col, experts, heads),
        (blocks,),
        [
            pl.BlockSpec((width, BQ), lambda i, at: (0, i)),
            pl.BlockSpec((BQ, 2 * width), lambda i, at: (at[2] + i, 0)),
            pl.BlockSpec((BQ, 2 * width), lambda i, at: (i, 0)),
            pl.BlockSpec((BQ, model), lambda i, at: (at[2] + i, 0)),
            pl.BlockSpec((BQ, model), lambda i, at: (i, 0)),
            pl.BlockSpec((1, BQ), lambda i, at: (0, at[2] + i)),
            whole(8, model),
            whole(model, cols),
            whole(part, model),
            whole(model, model),
            whole(small_rows, model),
            whole(16, 2 * BK),
            whole(8, BQ),
            whole(span, LANES),
            whole(LANES, model),
        ],
        [
            pl.BlockSpec((model, BQ), lambda i, at: (0, i)),
            *[whole(n, late_at + LANES) for n in grad_rows],
        ],
        [
            shaped((model, rows), BF),
            *[shaped((n, late_at + LANES), BF) for n in grad_rows],
        ],
        scratch=[pltpu.VMEM((model, late_at + LANES), F32), pltpu.VMEM((8, model), F32)],
        prefetch=1,
        name="qkv_back",
    )(
        at, dq_t, dkv, got, normed_one, tokens, scale_one, gains, small_all, d_hidden, grad_out_w,
        small_grads, skew, sides, diag, spread,
    )
    terms, grad_dense = outs[0], outs[1:]
    dense_cols = late_at + LANES
    piece_cols = -(-(LANES + width) // LANES) * LANES
    if square:
        keep, send = grad_dense
        pieces = call(
            pair_sum_kernel,
            (1,),
            [whole(4 * own, dense_cols)] * 2,
            [whole(own, dense_cols)] * 4,
            [shaped((own, dense_cols), BF)] * 4,
            name="dense_pair_sum",
        )(keep, xor_step(send, "ctx", 1))
        first_pieces = pieces
        pieces = [pieces[0]] + [xor_step(pieces[s], "fsdp", s) for s in (1, 2, 3)]
    else:
        first_pieces = []
        pieces = [lax.psum_scatter(grad_dense[0], dense, scatter_dimension=0, tiled=True)]
    terms = after(terms, grad_experts, first_pieces)
    grad_tokens = lax.psum_scatter(terms, "tp", scatter_dimension=0, tiled=True).astype(F32)
    grad_qkv, grad_table, *pieces = call(
        partial(dense_sum_kernel, wide_cols, len(pieces), experts + 2),
        (1,),
        [whole(own, dense_cols)] * len(pieces),
        [whole(3, own, width), whole(table_rows, heads), *[whole(own, piece_cols)] * 4],
        [
            shaped((3, own, width), F32),
            shaped((table_rows, heads), F32),
            *[shaped((own, piece_cols), BF)] * 4,
        ],
        name="dense_sum",
    )(*pieces)
    pieces = [pieces[0]] + [turn(pieces[s], 4 - s) for s in (1, 2, 3)]
    grad_in, grad_down = grad_experts[:, 0:ff].astype(F32), grad_experts[:, ff:].astype(F32)
    pieces, grad_in, grad_down = lax.optimization_barrier((pieces, grad_in, grad_down))
    grad_out_mine, grad_router, grad_gain_two, grad_gain_one = call(
        last_sum_kernel,
        (1,),
        [whole(own, piece_cols)] * 4,
        [whole(own, width), whole(experts, own), whole(1, own), whole(1, own)],
        [
            shaped((own, width), F32),
            shaped((experts, own), F32),
            shaped((1, own), F32),
            shaped((1, own), F32),
        ],
        name="last_sum",
    )(*pieces)
    hidden_share = after(hidden_share, grad_qkv)
    share_block = pl.BlockSpec((share, BQ), lambda i, *_: (0, i))
    out_share = call(
        out_kernel,
        (blocks,),
        [*[share_block] * 5, pl.BlockSpec((1, BQ), lambda i: (0, i))],
        share_block,
        shaped((share, rows), BF),
        name="layer_output",
    )(*eo_mine, hidden_share, gate_row)
    return (
        out_share.T,
        grad_tokens.T,
        grad_qkv.transpose(1, 0, 2),
        grad_out_mine,
        grad_table,
        grad_gain_one.reshape(own),
        grad_gain_two.reshape(own),
        grad_router.T,
        grad_in[None],
        grad_down[None],
    )


def solution(mesh):
    placed = (
        P(("fsdp", "ctx"), None),
        P(("fsdp", "ctx"), None),
        P(("fsdp", "ctx"), None, "tp"),
        P(("fsdp", "ctx"), "tp"),
        P(None, "tp"),
        P(("fsdp", "ctx")),
        P(("fsdp", "ctx")),
        P(("fsdp", "ctx"), None),
        P("fsdp", None, "tp"),
        P("fsdp", None, "tp"),
        P(("fsdp", "ctx"), None),
        P("fsdp"),
    )
    return jax.shard_map(
        shards,
        mesh=mesh,
        in_specs=placed,
        out_specs=(
            P(("fsdp", "ctx"), "tp"),
            P(("fsdp", "ctx"), "tp"),
            P(("fsdp", "ctx"), None, "tp"),
            P(("fsdp", "ctx"), "tp"),
            P(("fsdp", "ctx"), "tp"),
            P(("fsdp", "ctx")),
            P(("fsdp", "ctx")),
            P(("fsdp", "ctx"), None),
            P("fsdp", "ctx", "tp"),
            P("fsdp", "ctx", "tp"),
        ),
        check_vma=False,
    )
```

```python
from functools import partial

import jax
import jax.numpy as jnp
from jax import lax
from jax.experimental import pallas as pl
from jax.experimental.pallas import tpu as pltpu
from jax.sharding import PartitionSpec as P

norm_eps = 1e-06
bucket_edges = (12, 16, 23, 32, 46, 64, 91)
LANES = 128
TILE = 256
MIB = 1024 * 1024
NT = (((1,), (1,)), ((), ()))
TN = (((0,), (0,)), ((), ()))


BQ = 256
BK = 256
HD = 64
NEG = -1e30
FLOOR = -1e28
F32 = jnp.float32
BF = jnp.bfloat16


def call(kernel, grid, in_specs, out_specs, out_shape, scratch=(), prefetch=0, vmem=58, name=None, aliases={}):
    return pl.pallas_call(
        kernel,
        grid_spec=pltpu.PrefetchScalarGridSpec(
            num_scalar_prefetch=prefetch,
            grid=grid,
            in_specs=in_specs,
            out_specs=out_specs,
            scratch_shapes=list(scratch),
        ),
        out_shape=out_shape,
        input_output_aliases=aliases,
        compiler_params=pltpu.CompilerParams(
            dimension_semantics=("arbitrary",) * len(grid), vmem_limit_bytes=vmem * MIB
        ),
        cost_estimate=pl.CostEstimate(
            flops=10**7, bytes_accessed=10**5, transcendentals=0
        ),
        name=name,
    )


def whole(*shape):
    return pl.BlockSpec(shape, lambda *_: (0,) * len(shape))


def shaped(shape, dtype):
    return jax.ShapeDtypeStruct(shape, dtype)


def relative_bucket(offset):
    distance = jnp.abs(offset)
    far_bucket = jnp.zeros_like(distance) + 8
    for edge in bucket_edges:
        far_bucket = far_bucket + (distance >= edge).astype(jnp.int32)
    result = jnp.where(distance < 8, distance, far_bucket)
    return result + jnp.where(offset > 0, 16, 0)


def dot(a, b, dims=None):
    if dims is None:
        return jnp.dot(a, b, preferred_element_type=F32)
    return lax.dot_general(a, b, dims, preferred_element_type=F32)


def to_row(column):
    n = column.shape[0]
    return jnp.broadcast_to(column, (n, LANES)).T[0:1, :]


def to_column(row):
    n = row.shape[1]
    return jnp.broadcast_to(row, (LANES, n)).T[:, 0:1]


def split3(x):
    hi = x.astype(BF)
    rest = x - hi.astype(F32)
    mid = rest.astype(BF)
    low = (rest - mid.astype(F32)).astype(BF)
    return hi, mid, low


def key_side(docs_col, rows):
    lane = lax.broadcasted_iota(jnp.int32, (rows, HD), 1)
    same = (docs_col == lane.astype(F32)).astype(F32)
    ones = jnp.where((lane >= 4) & (lane < 7), 1.0, 0.0)
    return jnp.where(lane < 4, same, ones)


def query_side(docs_row, cols, tail):
    row = lax.broadcasted_iota(jnp.int32, (HD, cols), 0)
    other = jnp.where((row < 4) & (docs_row != row.astype(F32)), NEG, 0.0)
    if tail is None:
        return other.astype(BF)
    hi, mid, low = (t.astype(F32) for t in split3(tail))
    part = jnp.where(row == 4, hi, jnp.where(row == 5, mid, jnp.where(row == 6, low, 0.0)))
    return jnp.where(row < 4, other, part).astype(BF)


def shifted(x, by):
    return x if by == 0 else pltpu.roll(x, x.shape[1] - by, 1)


def diagonal_sums(tile):
    total = jnp.zeros((8, 2 * BQ), F32)
    for first in range(0, BK, 8):
        strip = tile[first : first + 8, :]
        total = total + shifted(jnp.concatenate([strip, jnp.zeros((8, BQ), F32)], axis=1), first)
    result = jnp.zeros((1, 2 * BQ), F32)
    for r in range(8):
        result = result + shifted(total, r)[r : r + 1, :]
    return result


def ones_rows(cols):
    return jnp.where(lax.broadcasted_iota(jnp.int32, (16, cols), 0) == 0, 1.0, 0.0).astype(BF)


def fwd_kernel(heads, first_block, blocks, info, far, qkv_ref, dcol, drow, band, *refs):
    i = pl.program_id(0)
    width = heads * HD
    block = first_block + i
    qb = info[0, 0] + block
    lo = info[0, 1 + block]
    hi = info[0, 1 + blocks + block]
    if first_block:
        k_aug, v_t, _, _, mixed_ref, low_ref, lse_ref = refs
        q = qkv_ref[:, 0:width]
    else:
        mixed_ref, low_ref, lse_ref, k_aug, v_t = refs
        q = qkv_ref[pl.ds(pl.multiple_of(qb * BQ, BQ), BQ), 0:width]

        @pl.when(i == 0)
        def _():
            for r in range(qkv_ref.shape[0] // BK):
                rows = pl.ds(r * BK, BK)
                side = key_side(to_column(dcol[:, r * BK : (r + 1) * BK]), BK).astype(BF)
                vt = qkv_ref[rows, 2 * width : 3 * width].astype(F32).T.astype(BF)
                for h in range(heads):
                    k = qkv_ref[rows, width + h * HD : width + (h + 1) * HD]
                    k_aug[h, rows, :] = jnp.concatenate([k, side], axis=1)
                    v_t[h, 0:HD, rows] = vt[h * HD : (h + 1) * HD, :]
                    v_t[h, HD : HD + 16, rows] = ones_rows(BK)

    qt = (q.astype(F32) * (HD**-0.5)).T.astype(BF)
    side = query_side(drow[...], BQ, None)
    q_aug = [jnp.concatenate([qt[h * HD : (h + 1) * HD, :], side], axis=0) for h in range(heads)]

    def step(kb, carry, bias_of):
        rows = pl.ds(pl.multiple_of(kb * BK, BK), BK)
        out = []
        for h in range(heads):
            peak, acc = carry[h]
            s = jnp.dot(k_aug[h, rows, :], q_aug[h], preferred_element_type=F32)
            s = s + bias_of(h, kb)
            new = jnp.maximum(peak, jnp.max(s, axis=0, keepdims=True))
            p = jnp.exp(s - new).astype(BF)
            acc = acc * jnp.exp(peak - new) + jnp.dot(v_t[h, :, rows], p, preferred_element_type=F32)
            out.append((new, acc))
        return tuple(out)

    carry = tuple(
        (jnp.full((1, BQ), FLOOR, F32), jnp.zeros((HD + 16, BQ), F32)) for _ in range(heads)
    )
    carry = lax.fori_loop(lo, jnp.minimum(hi, qb - 1), lambda kb, c: step(kb, c, lambda h, _: far[h, 15]), carry)
    carry = lax.fori_loop(
        jnp.maximum(lo, qb - 1),
        jnp.minimum(hi, qb + 2),
        lambda kb, c: step(kb, c, lambda h, t: band[h, t - qb + 1]),
        carry,
    )
    carry = lax.fori_loop(jnp.maximum(lo, qb + 2), hi, lambda kb, c: step(kb, c, lambda h, _: far[h, 31]), carry)
    for h in range(heads):
        peak, acc = carry[h]
        total = acc[HD : HD + 1, :]
        mixed = acc[0:HD, :] / total
        mixed_ref[h * HD : (h + 1) * HD, :] = mixed
        low_ref[h * HD : (h + 1) * HD, :] = mixed.astype(BF)
        lse_ref[h : h + 1, :] = peak + jnp.log(total)


def attention_fwd(info, far, qkv_all, docs, band, rows, before=None):
    seq, cols = qkv_all.shape
    width = cols // 3
    heads = width // HD
    blocks = rows // BQ
    steps = blocks // 2
    first = 0 if before is None else steps
    full = lambda shape: pl.BlockSpec(shape, lambda i, info: (0,) * len(shape))
    kept = [(heads, seq, 2 * HD), (heads, HD + 16, seq)]
    out_specs = [
        pl.BlockSpec((width, BQ), lambda i, info: (0, first + i)),
        pl.BlockSpec((width, BQ), lambda i, info: (0, i)),
        pl.BlockSpec((heads, BQ), lambda i, info: (0, first + i)),
    ]
    out_shape = [
        jax.ShapeDtypeStruct((width, rows), F32),
        jax.ShapeDtypeStruct((width, rows // 2), BF),
        jax.ShapeDtypeStruct((heads, rows), F32),
    ]
    in_specs = [
        pl.BlockSpec(memory_space=pltpu.SMEM),
        full((seq, cols)) if before is None else pl.BlockSpec((BQ, cols), lambda i, info: (info[0, 0] + first + i, 0)),
        full((1, seq)),
        pl.BlockSpec((1, BQ), lambda i, info: (0, info[0, 0] + first + i)),
        full((heads, 3, BK, BQ)),
    ]
    operands = [info, far, qkv_all, docs, docs, band]
    aliases = {}
    if before is None:
        out_specs += [full(s) for s in kept]
        out_shape += [jax.ShapeDtypeStruct(s, BF) for s in kept]
    else:
        mixed, lse, k_aug, v_t = before
        in_specs += [full(s) for s in kept] + [pl.BlockSpec(memory_space=pl.ANY)] * 2
        operands += [k_aug, v_t, mixed, lse]
        aliases = {8: 0, 9: 2}
    return pl.pallas_call(
        partial(fwd_kernel, heads, first, blocks),
        grid_spec=pltpu.PrefetchScalarGridSpec(
            num_scalar_prefetch=1, grid=(steps,), in_specs=in_specs, out_specs=out_specs
        ),
        out_shape=out_shape,
        input_output_aliases=aliases,
        compiler_params=pltpu.CompilerParams(
            dimension_semantics=("arbitrary",), vmem_limit_bytes=58 * 1024 * 1024
        ),
        cost_estimate=pl.CostEstimate(flops=10**7, bytes_accessed=10**5, transcendentals=0),
        name="attention_fwd",
    )(*operands)


def bwd_kernel(
    heads, info, far, qkv_all, dcol, drow, band, mixed_ref, lse_ref, m0, m1, m2, m3, k_aug,
    dq_ref, dkv_ref, skew_ref, side_ref, v_aug, k_t, near_acc, dkv_acc,
):
    i = pl.program_id(0)
    seq = qkv_all.shape[0]
    width = heads * HD

    @pl.when(i == 0)
    def _():
        near_acc[...] = jnp.zeros_like(near_acc)
        dkv_acc[...] = jnp.zeros_like(dkv_acc)
        side_ref[...] = jnp.zeros_like(side_ref)
        for r in range(seq // BK):
            rows = pl.ds(r * BK, BK)
            lane = lax.broadcasted_iota(jnp.int32, (BK, HD), 1)
            ones = jnp.where(lane < 3, 1.0, 0.0).astype(BF)
            kt = qkv_all[rows, width : 2 * width].astype(F32).T.astype(BF)
            for h in range(heads):
                v = qkv_all[rows, 2 * width + h * HD : 2 * width + (h + 1) * HD]
                v_aug[h, rows, :] = jnp.concatenate([v, ones], axis=1)
                k_t[h, 0:HD, rows] = kt[h * HD : (h + 1) * HD, :]
                k_t[h, HD : HD + 16, rows] = ones_rows(BK)

    steps = pl.num_programs(0)
    block = lax.rem(info[0, 1 + 2 * steps] + steps - i, steps)
    qb = info[0, 0] + block
    lo = info[0, 1 + block]
    hi = info[0, 1 + steps + block]
    dmix = m0[...]
    for s, ref in ((1, m1), (2, m2), (3, m3)):
        dmix = jnp.where(i == s, ref[...], dmix)
    q_scaled = qkv_all[pl.ds(pl.multiple_of(qb * BQ, BQ), BQ), 0:width].astype(F32) * (HD**-0.5)
    qt = q_scaled.T.astype(BF)
    q_rows = q_scaled.astype(BF)
    dmix_t = dmix.astype(F32)
    dmix_rows = dmix_t.T.astype(BF)
    zero = jnp.zeros((BQ, HD), BF)
    row = lax.broadcasted_iota(jnp.int32, (HD, BQ), 0)
    q_aug, d_aug, rhs = [], [], []
    for h in range(heads):
        cols = slice(h * HD, (h + 1) * HD)
        lse = lse_ref[h : h + 1, :]
        kinds = []
        for tail in (far[h, 15] - lse, -lse, far[h, 31] - lse):
            kinds.append(jnp.concatenate([qt[cols, :], query_side(drow[...], BQ, tail)], axis=0))
        q_aug.append(kinds)
        delta = -jnp.sum(dmix_t[cols, :] * mixed_ref[cols, :], axis=0, keepdims=True)
        a, b, c = (t.astype(F32) for t in split3(delta))
        part = jnp.where(row == 0, a, jnp.where(row == 1, b, jnp.where(row == 2, c, 0.0)))
        d_aug.append(jnp.concatenate([dmix_t[cols, :].astype(BF), part.astype(BF)], axis=0))
        top = jnp.concatenate([dmix_rows[:, cols], zero], axis=1)
        low = jnp.concatenate([zero, q_rows[:, cols]], axis=1)
        rhs.append(jnp.concatenate([top, low], axis=0))

    def step(kb, carry, kind):
        rows = pl.ds(pl.multiple_of(kb * BK, BK), BK)
        out = []
        for h in range(heads):
            s = jnp.dot(k_aug[h, rows, :], q_aug[h][kind], preferred_element_type=F32)
            if kind == 1:
                s = s + band[h, kb - qb + 1]
            p = jnp.exp(s)
            dp = jnp.dot(v_aug[h, rows, :], d_aug[h], preferred_element_type=F32)
            ds = p * dp
            ds_low = ds.astype(BF)
            if kind == 1:
                near_acc[h, kb - qb + 1] = near_acc[h, kb - qb + 1] + ds_low.astype(F32)
            both = jnp.concatenate([p.astype(BF), ds_low], axis=1)
            dkv_acc[h, rows, :] += jnp.dot(both, rhs[h], preferred_element_type=F32)
            out.append(carry[h] + jnp.dot(k_t[h, :, rows], ds_low, preferred_element_type=F32))
        return tuple(out)

    zero_dq = jnp.zeros((HD + 16, BQ), F32)
    left = lax.fori_loop(lo, jnp.minimum(hi, qb - 1), lambda kb, c: step(kb, c, 0), (zero_dq,) * heads)
    near = lax.fori_loop(
        jnp.maximum(lo, qb - 1), jnp.minimum(hi, qb + 2), lambda kb, c: step(kb, c, 1), left
    )
    last = lax.fori_loop(jnp.maximum(lo, qb + 2), hi, lambda kb, c: step(kb, c, 2), near)
    for h in range(heads):
        dq_ref[h * HD : (h + 1) * HD, :] = (last[h][0:HD, :] * (HD**-0.5)).astype(BF)
        side_ref[2 * h : 2 * h + 1, :] += left[h][HD : HD + 1, :]
        side_ref[2 * h + 1 : 2 * h + 2, :] += last[h][HD : HD + 1, :] - near[h][HD : HD + 1, :]

    @pl.when(i == pl.num_programs(0) - 1)
    def _():
        for h in range(heads):
            for t in range(3):
                skew_ref[3 * h + t : 3 * h + t + 1, :] = diagonal_sums(near_acc.at[h, t])
        for r in range(seq // BK):
            rows = pl.ds(r * BK, BK)
            acc = [dkv_acc[h, rows, :] for h in range(heads)]
            dk = [a[:, HD : 2 * HD] for a in acc]
            dv = [a[:, 0:HD] for a in acc]
            dkv_ref[rows, :] = jnp.concatenate(dk + dv, axis=1).astype(BF)


def attention_bwd(info, far, qkv_all, dcol, drow, band, mixed, lse, dmix, k_aug, rows):
    seq, cols = qkv_all.shape
    width = cols // 3
    heads = width // HD
    steps = rows // BQ
    full = lambda shape: pl.BlockSpec(shape, lambda i, info: (0,) * len(shape))
    block = lambda i, info: lax.rem(info[0, 1 + 2 * steps] + steps - i, steps)
    return pl.pallas_call(
        partial(bwd_kernel, heads),
        grid_spec=pltpu.PrefetchScalarGridSpec(
            num_scalar_prefetch=1,
            grid=(steps,),
            in_specs=[
                pl.BlockSpec(memory_space=pltpu.SMEM),
                full((seq, cols)),
                full((1, seq)),
                pl.BlockSpec((1, BQ), lambda i, info: (0, info[0, 0] + block(i, info))),
                full((heads, 3, BK, BQ)),
                pl.BlockSpec((width, BQ), lambda i, info: (0, block(i, info))),
                pl.BlockSpec((heads, BQ), lambda i, info: (0, block(i, info))),
                *[full((width, BQ))] * 4,
                full((heads, seq, 2 * HD)),
            ],
            out_specs=[
                pl.BlockSpec((width, BQ), lambda i, info: (0, block(i, info))),
                full((seq, 2 * width)),
                full((16, 2 * BK)),
                full((8, BQ)),
            ],
            scratch_shapes=[
                pltpu.VMEM((heads, seq, 2 * HD), BF),
                pltpu.VMEM((heads, HD + 16, seq), BF),
                pltpu.VMEM((heads, 3, BK, BQ), F32),
                pltpu.VMEM((heads, seq, 2 * HD), F32),
            ],
        ),
        out_shape=[
            jax.ShapeDtypeStruct((width, rows), BF),
            jax.ShapeDtypeStruct((seq, 2 * width), BF),
            jax.ShapeDtypeStruct((16, 2 * BK), F32),
            jax.ShapeDtypeStruct((8, BQ), F32),
        ],
        compiler_params=pltpu.CompilerParams(
            dimension_semantics=("arbitrary",), vmem_limit_bytes=58 * 1024 * 1024
        ),
        cost_estimate=pl.CostEstimate(
            flops=10**7, bytes_accessed=10**5, transcendentals=0
        ),
        name="attention_bwd",
    )(info, far, qkv_all, dcol, drow, band, mixed, lse, *dmix, k_aug)


def plan_kernel(
    experts, own, table_rows, at, ids_ref, docs_ref, table_ref,
    pos_ref, owner_ref, chosen_ref, docs_out, info_ref, band_ref, diag_ref, spread_ref,
):
    rows = ids_ref.shape[1]
    seq = docs_ref.shape[1]
    heads = band_ref.shape[0]
    buckets = table_ref.shape[1]
    blocks = rows // BQ
    chosen = ids_ref[...].astype(F32)
    chosen_ref[...] = chosen
    docs = docs_ref[...].astype(F32)
    docs_out[...] = docs
    expert_rows = -(-experts // 8) * 8
    one_hot = lax.broadcasted_iota(jnp.int32, (expert_rows, rows), 0).astype(F32) == chosen
    one_hot = jnp.where(one_hot, 1.0, 0.0)
    low_rows = lax.broadcasted_iota(jnp.int32, (rows, rows), 0)
    before = jnp.where(low_rows < lax.broadcasted_iota(jnp.int32, (rows, rows), 1), 1.0, 0.0)
    earlier = dot(one_hot.astype(BF), before.astype(BF))
    lane = lax.broadcasted_iota(jnp.int32, (1, LANES), 1)
    lane_f = lane.astype(F32)
    pos = jnp.zeros((1, rows), F32)
    owner = jnp.zeros((1, LANES), F32)
    end = jnp.zeros((1, 1), F32)
    for e in range(experts):
        hit = one_hot[e : e + 1, :]
        count = jnp.sum(hit, axis=1, keepdims=True)
        pos = pos + hit * (earlier[e : e + 1, :] + end * TILE)
        end = end + jnp.maximum(jnp.floor((count + (TILE - 1)) * (1.0 / TILE)), 1.0)
        owner = owner + jnp.where(end <= lane_f, 1.0, 0.0)
    pos_ref[...] = pos.astype(jnp.int32)
    owner = jnp.minimum(owner, experts - 1.0)
    owner_ref[...] = jnp.where(lane == LANES - 1, end, owner).astype(jnp.int32)
    base = at[2]
    info = jnp.where(lane == 0, base, jnp.where(lane == 1 + 2 * blocks, at[0], 0)).astype(F32)
    for b in range(seq // BQ):
        first = docs[:, b * BQ : b * BQ + 1]
        last = docs[:, (b + 1) * BQ - 1 : (b + 1) * BQ]
        low = jnp.sum(jnp.where(docs < first, 1.0, 0.0), axis=1, keepdims=True)
        high = jnp.sum(jnp.where(docs <= last, 1.0, 0.0), axis=1, keepdims=True)
        here = (b >= base) & (b < base + blocks)
        low_at = (lane == 1 + b - base) & here
        high_at = (lane == 1 + blocks + b - base) & here
        info = info + jnp.where(low_at, jnp.floor(low * (1.0 / BK)), 0.0)
        info = info + jnp.where(high_at, jnp.floor((high + (BK - 1)) * (1.0 / BK)), 0.0)
    info_ref[...] = info.astype(jnp.int32)
    span = 3 * 2 * BQ
    column = lax.broadcasted_iota(jnp.int32, (8, span), 1)
    tile = (column >= 2 * BQ).astype(jnp.int32) + (column >= 4 * BQ).astype(jnp.int32)
    inside = column - tile * (2 * BQ)
    wrapped = jnp.where(inside < BQ, inside, inside - 2 * BQ)
    bucket = relative_bucket((tile - 1) * BK - wrapped)[0:1, :].astype(F32)
    which = lax.broadcasted_iota(jnp.int32, (buckets, span), 0).astype(F32)
    pick = jnp.where(which == bucket, 1.0, 0.0).astype(BF)
    wide = jnp.concatenate([table_ref[...], jnp.zeros((8 - heads, buckets), F32)], axis=0)
    vectors = sum(dot(p, pick) for p in split3(wide))
    for h in range(heads):
        for t in range(3):
            line = vectors[h : h + 1, t * 2 * BQ : (t + 1) * 2 * BQ]
            wide = jnp.broadcast_to(line, (BK, 2 * BQ))
            band_ref[h, t] = pltpu.roll(wide, 0, 1, stride=1, stride_axis=0)[:, 0:BQ]
    by_column = to_column(bucket)
    lanes = lax.broadcasted_iota(jnp.int32, (span, LANES), 1).astype(F32)
    diag_ref[...] = jnp.where(by_column == lanes, 1.0, 0.0).astype(BF)
    model = spread_ref.shape[1]
    row_ids = lax.broadcasted_iota(jnp.int32, (8, model), 1)
    target = jnp.full((8, model), -1, jnp.int32)
    for b in range(buckets):
        target = jnp.where(row_ids == b // table_rows * own + b % table_rows, b, target)
    down = lax.broadcasted_iota(jnp.int32, (LANES, model), 0).astype(F32)
    spread_ref[...] = jnp.where(down == target[0:1, :].astype(F32), 1.0, 0.0).astype(BF)


def pack_kernel(qkv_ref, router_ref, one_ref, two_ref, out_ref):
    experts, rows = router_ref.shape
    fill = jnp.zeros((LANES - experts - 2, rows), F32)
    tail = [r[...].astype(F32) for r in (router_ref, one_ref, two_ref)]
    tail = jnp.concatenate([*tail, fill], axis=0).T.astype(BF)
    parts = [qkv_ref[c] for c in range(3)]
    used = sum(p.shape[1] for p in parts)
    gap = out_ref.shape[1] - used - LANES
    if gap:
        parts.append(jnp.zeros((rows, gap), BF))
    out_ref[...] = jnp.concatenate([*parts, tail], axis=1)


def qkv_kernel(
    first_col, cols, experts, count, at, own_ref, other_ref, *refs
):
    pieces = refs[:count]
    qkv_ref, norm_ref, scale_ref, small_ref, gains_ref = refs[count:]
    i = pl.program_id(0)

    @pl.when(i == 0)
    def _():
        slot = 0
        for piece in pieces:
            for s in range(piece.shape[0]):
                first = pl.multiple_of(at[4 + slot], 16)
                small_ref[pl.ds(first, piece.shape[1]), :] = piece[s]
                slot += 1
        tail = small_ref[:, small_ref.shape[1] - LANES :].astype(F32).T
        gains_ref[...] = tail[experts : experts + 8, :]

    x = jnp.where(i < pl.num_programs(0) // 2, own_ref[...], other_ref[...]).astype(F32)
    scale = lax.rsqrt(jnp.mean(x * x, axis=-1, keepdims=True) + norm_eps)
    normed = (x * scale * gains_ref[0:1, :]).astype(BF)
    norm_ref[...] = normed
    scale_ref[...] = to_row(scale)
    qkv_ref[...] = dot(normed, small_ref[:, first_col : first_col + cols]).astype(BF)


def router_parts(hidden, gain, router, chosen, experts):
    scale = lax.rsqrt(jnp.mean(hidden * hidden, axis=-1, keepdims=True) + norm_eps)
    hat = hidden * scale
    normed = (hat * gain).astype(BF)
    lane = lax.broadcasted_iota(jnp.int32, (hidden.shape[0], LANES), 1)
    logits = jnp.where(lane < experts, dot(normed, router), NEG)
    weights = jnp.exp(logits - jnp.max(logits, axis=-1, keepdims=True))
    route = weights / jnp.sum(weights, axis=-1, keepdims=True)
    one_hot = jnp.where(lane.astype(F32) == chosen, 1.0, 0.0)
    gate = jnp.sum(route * one_hot, axis=-1, keepdims=True)
    return scale, hat, normed, route, one_hot, gate


def hidden_kernel(experts, skipped, at, *refs):
    tok_ref, mix_refs, wout_ref = refs[0], refs[1:5], refs[5]
    gains_ref, small_ref, chosen_ref = refs[6:9]
    hidden_ref, norm_ref, gate_ref, share_ref, turn_s = refs[9 + skipped :]
    mixed = jnp.concatenate([r[...] for r in mix_refs], axis=0).astype(F32).T.astype(BF)
    hidden = tok_ref[...].astype(F32) + dot(mixed, wout_ref[...], NT)
    parts = router_parts(hidden, gains_ref[1:2, :], small_ref[...], to_column(chosen_ref[...]), experts)
    hidden_ref[...] = hidden
    norm_ref[...] = parts[2]
    gate_ref[...] = to_row(parts[5])
    turn_s[...] = hidden.T
    share = share_ref.shape[0]
    share_ref[...] = turn_s[pl.ds(pl.multiple_of(at[0] * share, share), share), :]


def pick_back(pos_col, total):
    place = lax.broadcasted_iota(jnp.int32, (pos_col.shape[0], total), 1).astype(F32)
    return jnp.where(pos_col == place, 1.0, 0.0).astype(BF)


def unsort_kernel(owner, at, pos_row, sorted_ref, e0, e1, e2, e3, pos_col, turn_s):
    rows = pos_row.shape[1]
    part = turn_s.shape[1]
    pos_col[...] = jnp.broadcast_to(pos_row[...].astype(F32), (LANES, rows)).T
    for g in range(rows // part):
        mine = slice(g * part, (g + 1) * part)
        pick = pick_back(pos_col[mine, 0:1], sorted_ref.shape[0])
        turn_s[...] = dot(pick, sorted_ref[...]).T.astype(BF)
        for step, out in enumerate((e0, e1, e2, e3)):
            share = out.shape[0]
            first = pl.multiple_of(lax.rem(at[0] + step, 4) * share, share)
            out[:, mine] = turn_s[pl.ds(first, share), :]


def expert_kernel(
    owner, at, pos_row, norm_ref, cot_ref, gate_ref, w_ref,
    b0, b1, b2, b3, eo_ref, x_ref, de_ref, act_ref, di_ref, dr_s, pos_col,
):
    i = pl.program_id(0)
    z = at[0]
    rows = norm_ref.shape[0]
    width = norm_ref.shape[1]
    ff = w_ref.shape[1] // 2
    here = pl.ds(pl.multiple_of(i * TILE, TILE), TILE)
    used = i < owner[0, LANES - 1]

    @pl.when(used)
    def _():
        place = lax.broadcasted_iota(jnp.int32, (TILE, rows), 0) + i * TILE
        hit = pos_row[...] == place
        pick = jnp.where(hit, 1.0, 0.0).astype(BF)
        x = dot(pick, norm_ref[...]).astype(BF)
        cot = dot(pick, cot_ref[...])
        gate = jnp.sum(jnp.where(hit, gate_ref[...], 0.0), axis=1, keepdims=True)
        d_e = (gate * cot).astype(BF)
        w_in = w_ref[:, 0:ff]
        w_down = w_ref[:, ff : 2 * ff]
        d_act = dot(d_e, w_down)
        inner = dot(x, w_in)
        half = 0.5 * (1.0 + lax.erf(inner * (0.5**0.5)))
        active = (inner * half).astype(BF)
        slope = half + inner * (jnp.exp(-0.5 * inner * inner) * 0.3989422804014327)
        d_inner = (d_act * slope).astype(BF)
        d_rows = dot(d_inner, w_in, NT)
        terms = dot(active, w_down, NT)
        d_gate = jnp.sum(cot * terms, axis=1, keepdims=True)
        lane = lax.broadcasted_iota(jnp.int32, (TILE, LANES), 1)
        hi, mid, low = (t.astype(F32) for t in split3(d_gate))
        extra = jnp.where(lane == 0, hi, jnp.where(lane == 1, mid, jnp.where(lane == 2, low, 0.0)))
        dr_s[here, :] = jnp.concatenate([d_rows.astype(BF), extra.astype(BF)], axis=1)
        eo_ref[...] = terms.astype(BF)
        x_ref[...] = x
        de_ref[...] = d_e
        act_ref[...] = active
        di_ref[...] = d_inner

    @pl.when(jnp.logical_not(used))
    def _():
        dr_s[here, :] = jnp.zeros((TILE, dr_s.shape[1]), BF)
        for ref in (eo_ref, x_ref, de_ref, act_ref, di_ref):
            ref[...] = jnp.zeros_like(ref)

    @pl.when(i == pl.num_programs(0) - 1)
    def _():
        part = rows // 4
        pos_col[...] = jnp.broadcast_to(pos_row[...].astype(F32), (LANES, rows)).T
        for r, back_ref in enumerate((b0, b1, b2, b3)):
            g = lax.rem(z + r, 4)
            mine = pl.ds(pl.multiple_of(g * part, part), part)
            back = dot(pick_back(pos_col[mine, 0:1], dr_s.shape[0]), dr_s[...])
            back_ref[0:part, :] = back[:, 0:width].astype(BF)
            tail = back[:, width : width + LANES].T
            d_gate = tail[0:1, :] + tail[1:2, :] + tail[2:3, :]
            row = lax.broadcasted_iota(jnp.int32, (16, part), 0)
            strip = jnp.where(row == 0, jnp.broadcast_to(d_gate, (16, part)), 0.0)
            fill = jnp.zeros((16, width - part), F32)
            back_ref[part : part + 16, :] = jnp.concatenate([strip, fill], axis=1).astype(BF)


def weight_grad_kernel(owner, x_ref, di_ref, de_ref, act_ref, out_ref, acc):
    i = pl.program_id(0)
    last = pl.num_programs(0) - 1
    me = owner[0, i]
    before = owner[0, jnp.maximum(i - 1, 0)]
    after = owner[0, jnp.minimum(i + 1, last)]
    ff = di_ref.shape[1]

    first = (i == 0) | (before != me)
    used = i < owner[0, LANES - 1]

    @pl.when(first)
    def _():
        acc[:, 0:ff] = dot(x_ref[...], di_ref[...], TN)
        acc[:, ff : 2 * ff] = dot(de_ref[...], act_ref[...], TN)

    @pl.when(jnp.logical_not(first) & used)
    def _():
        acc[:, 0:ff] += dot(x_ref[...], di_ref[...], TN)
        acc[:, ff : 2 * ff] += dot(de_ref[...], act_ref[...], TN)

    @pl.when((i == last) | (after != me))
    def _():
        out_ref[...] = acc[...].astype(BF)


def split_rows(at, first_slot, acc, outs):
    if len(outs) == 1:
        outs[0][...] = acc[...].astype(BF)
        return
    slot = first_slot
    for out in outs:
        step = out.shape[0] // 4
        for s in range(4):
            first = pl.multiple_of(at[slot], 8)
            out[s * step : (s + 1) * step, :] = acc[pl.ds(first, step), :].astype(BF)
            slot += 1


def hidden_back_kernel(experts, at, *refs):
    back_refs, (hidden_ref, cot_ref, gains_ref, router_ref, chosen_ref) = refs[:4], refs[4:9]
    wout_ref = refs[9]
    dmix_refs, dh_ref, small_ref = refs[10:14], refs[14], refs[15]
    part, model = hidden_ref.shape
    back = sum(r[...].astype(F32) for r in back_refs)
    gain = gains_ref[1:2, :]
    router = router_ref[...]
    scale, hat, normed, route, one_hot, gate = router_parts(
        hidden_ref[...], gain, router, to_column(chosen_ref[...]), experts
    )
    d_gate = to_column(back[part : part + 1, 0:part])
    d_logits = (d_gate * gate) * (one_hot - route)
    parts = split3(d_logits)
    d_normed = back[0:part, :]
    g_router = jnp.zeros((LANES, model), F32)
    for p in parts:
        d_normed = d_normed + dot(p, router, NT)
        g_router = g_router + dot(p, normed, TN)
    small_ref[...] = jnp.zeros_like(small_ref)
    small_ref[0:experts, :] = g_router[0:experts, :]
    small_ref[experts : experts + 1, :] = jnp.sum(d_normed * hat, axis=0, keepdims=True)
    d_hat = d_normed * gain
    d_hidden = cot_ref[...].astype(F32) + scale * (
        d_hat - hat * jnp.mean(d_hat * hat, axis=-1, keepdims=True)
    )
    d_attn = d_hidden.astype(BF)
    d_mixed = dot(d_attn, wout_ref[...]).T.astype(BF)
    width = model // 4
    for s in range(4):
        dmix_refs[(4 - s) % 4][...] = d_mixed[s * width : (s + 1) * width, :]
    dh_ref[...] = d_hidden


def out_grad_kernel(at, dh_ref, *refs):
    mix_refs, gout_ref = refs[:8], refs[8]
    one, two = (jnp.concatenate([r[...] for r in mix_refs[n : n + 4]], axis=0) for n in (0, 4))
    mixed = jnp.where(at[0] < 2, one, two)
    gout_ref[...] = dot(dh_ref[...].T.astype(BF), mixed, NT).astype(BF)


def qkv_back_kernel(
    first_col, experts, heads, at, dq_ref, dkv_ref, got_ref, norm_ref, tok_ref, scale_ref, gains_ref, w_ref,
    dh_ref, gout_ref, small_ref, skew_ref, sides_ref, diag_ref, spread_ref,
    terms_ref, *rest,
):
    *gw_refs, acc, gain_s = rest
    i = pl.program_id(0)
    width = dq_ref.shape[0]
    cols = 3 * width
    model = tok_ref.shape[1]
    dkv = dkv_ref[...].astype(F32) + got_ref[...].astype(F32)
    d_qkv = jnp.concatenate([dq_ref[...].astype(F32).T, dkv], axis=1).astype(BF)
    scale = to_column(scale_ref[...])
    hat = tok_ref[...].astype(F32) * scale
    terms = dot(d_qkv, w_ref[:, first_col : first_col + cols], NT)
    d_hat = terms * gains_ref[0:1, :]
    mean = jnp.mean(d_hat * hat, axis=-1, keepdims=True)
    grad = scale * (d_hat - hat * mean) + jnp.where(i == at[0], dh_ref[...], 0.0)

    @pl.when(i == 0)
    def _():
        wide = acc.shape[1] - model - LANES
        acc[:, 0:wide] = jnp.zeros((model, wide), F32)
        acc[:, wide : wide + model] = gout_ref[...].astype(F32)
        gain_s[...] = jnp.zeros_like(gain_s)

    gain_s[0:1, :] += jnp.sum(terms * hat, axis=0, keepdims=True)
    acc[:, 0:cols] += dot(norm_ref[...], d_qkv, TN)
    terms_ref[...] = grad.T.astype(BF)

    @pl.when(i == pl.num_programs(0) - 1)
    def _():
        rows = [small_ref[0 : experts + 1, :], gain_s[0:1, :]]
        lines = []
        sides = []
        for h in range(8):
            k = min(h, heads - 1)
            lines.append(jnp.concatenate([skew_ref[3 * k + t : 3 * k + t + 1, :] for t in range(3)], axis=1))
            sides.append(jnp.sum(sides_ref[2 * k : 2 * k + 2, :], axis=1, keepdims=True))
        lane = lax.broadcasted_iota(jnp.int32, (8, LANES), 1)
        table = sum(dot(p, diag_ref[...]) for p in split3(jnp.concatenate(lines, axis=0)))
        table = table + jnp.where(lane == 15, jnp.concatenate([s[0:1, :] for s in sides], axis=0), 0.0)
        table = table + jnp.where(lane == 31, jnp.concatenate([s[1:2, :] for s in sides], axis=0), 0.0)
        spread = sum(dot(p, spread_ref[...]) for p in split3(table))
        rows.append(spread[0:heads, :])
        rows.append(jnp.zeros((LANES - experts - 2 - heads, model), F32))
        acc[:, acc.shape[1] - LANES :] = jnp.concatenate(rows, axis=0).T
        split_rows(at, 4, acc, gw_refs)


def out_kernel(e0, e1, e2, e3, hidden_ref, gate_ref, out_ref):
    total = sum(r[...].astype(F32) for r in (e0, e1, e2, e3))
    out_ref[...] = (hidden_ref[...] + total * gate_ref[...]).astype(BF)


def pair_sum_kernel(keep_ref, got_ref, *outs):
    step = outs[0].shape[0]
    for s, out in enumerate(outs):
        rows = slice(s * step, (s + 1) * step)
        out[...] = (keep_ref[rows, :].astype(F32) + got_ref[rows, :].astype(F32)).astype(BF)


def dense_sum_kernel(cols, count, table_at, *refs):
    parts, (qkv_ref, table_ref, *outs) = refs[:count], refs[count:]
    total = sum(r[...].astype(F32) for r in parts)
    width = qkv_ref.shape[2]
    for c in range(3):
        qkv_ref[c] = total[:, c * width : (c + 1) * width]
    late = total[:, total.shape[1] - LANES :]
    table_rows, heads = table_ref.shape
    table_ref[...] = late[0:table_rows, table_at : table_at + heads]
    for s, out in enumerate(outs):
        piece = total[:, cols + s * width : cols + (s + 1) * width]
        gap = jnp.zeros((late.shape[0], out.shape[1] - LANES - width), F32)
        out[...] = jnp.concatenate([late, piece, gap], axis=1).astype(BF)


def last_sum_kernel(p0, p1, p2, p3, out_ref, router_ref, two_ref, one_ref):
    total = sum(r[...].astype(F32) for r in (p0, p1, p2, p3))
    out_ref[...] = total[:, LANES : LANES + out_ref.shape[1]]
    late = total[:, 0:LANES].T
    experts = router_ref.shape[0]
    router_ref[...] = late[0:experts, :]
    two_ref[...] = late[experts : experts + 1, :]
    one_ref[...] = late[experts + 1 : experts + 2, :]

def xor_step(x, axis, s):
    return lax.ppermute(x, axis, [(i, i ^ s) for i in range(lax.axis_size(axis))])


def turn(x, s):
    return lax.ppermute(x, "tp", [(i, (i + s) % 4) for i in range(4)])


def gather_turns(x):
    return [x] + [turn(x, s) for s in (1, 2, 3)]


def scatter_turns(pieces):
    return [pieces[0]] + [turn(pieces[r], r) for r in (1, 2, 3)]


def after(x, *others):
    return lax.optimization_barrier((x, others))[0]


def shards(
    tokens,
    grad_out,
    w_qkv,
    w_attn_out,
    rel_bias,
    gain_attn,
    gain_ffn,
    w_router,
    w_in,
    w_down,
    expert_ids,
    doc_ids,
):
    rows, model = tokens.shape
    heads = rel_bias.shape[1]
    width = w_qkv.shape[2]
    own = w_qkv.shape[0]
    experts = w_router.shape[1]
    ff = w_in.shape[2]
    seq = doc_ids.shape[0]
    fsdp_n = lax.axis_size("fsdp")
    ctx_n = lax.axis_size("ctx")
    tp_n = lax.axis_size("tp")
    fsdp_at = lax.axis_index("fsdp")
    ctx_at = lax.axis_index("ctx")
    tp_at = lax.axis_index("tp")
    dense_at = fsdp_at * ctx_n + ctx_at
    part = rows // tp_n
    share = model // tp_n
    blocks = rows // BQ
    dense = ("fsdp", "ctx")
    square = fsdp_n == 4 and ctx_n == 2

    wide_cols = -(-3 * width // LANES) * LANES
    late_at = wide_cols + model
    table_rows = rel_bias.shape[0] // (fsdp_n * ctx_n)
    if square:
        starts = [((fsdp_at ^ s) * 2 + c) * own for c in (ctx_at, 1 - ctx_at) for s in range(4)]
    else:
        starts = [0]
    at = jnp.stack([jnp.int32(v) for v in (tp_at, ctx_at, ctx_at * blocks, fsdp_at, *starts)])

    qkv_cols = 3 * width
    first_col = 0
    cols = -(-qkv_cols // LANES) * LANES + LANES
    small = call(
        pack_kernel,
        (1,),
        [
            whole(3, own, width),
            whole(experts, own),
            whole(1, own),
            whole(1, own),
        ],
        whole(own, cols),
        shaped((own, cols), BF),
        name="pack_small",
    )(
        w_qkv.transpose(1, 0, 2),
        w_router.T,
        gain_attn[None, :],
        gain_ffn[None, :],
    )
    out_line = jnp.concatenate(gather_turns(after(w_attn_out, small)), axis=1)
    out_all = lax.all_gather(out_line, dense, axis=0, tiled=True)
    tokens_other = xor_step(tokens, "ctx", 1)
    half = model // ctx_n
    w_half = jnp.concatenate(
        [lax.dynamic_slice_in_dim(w.reshape(-1, ff), ctx_at * half, half, 0) for w in (w_in, w_down)],
        axis=1,
    )

    tiles = (rows + experts * (TILE - 1)) // TILE
    span = 6 * BQ
    table = rel_bias.T
    pos, owner, chosen, docs, info, band, diag, spread = call(
        partial(plan_kernel, experts, own, table_rows),
        (1,),
        [whole(1, rows), whole(1, seq), whole(*table.shape)],
        [
            whole(1, rows),
            whole(1, LANES),
            whole(1, rows),
            whole(1, seq),
            whole(1, LANES),
            whole(heads, 3, BK, BQ),
            whole(span, LANES),
            whole(LANES, model),
        ],
        [
            shaped((1, rows), jnp.int32),
            shaped((1, LANES), jnp.int32),
            shaped((1, rows), F32),
            shaped((1, seq), F32),
            shaped((1, LANES), jnp.int32),
            shaped((heads, 3, BK, BQ), F32),
            shaped((span, LANES), BF),
            shaped((LANES, model), BF),
        ],
        prefetch=1,
        name="plan",
    )(at, expert_ids.T, doc_ids[None, :], table)
    if square:
        near = [small] + [xor_step(small, "fsdp", s) for s in (1, 2, 3)]
        near, w_half, band = lax.optimization_barrier((near, w_half, band))
        near = jnp.stack(near)
        small_parts = [near, xor_step(near, "ctx", 1)]
    else:
        small_parts = [lax.all_gather(small, dense, axis=0, tiled=True)[None]]
    small_parts, tokens_other, w_half = lax.optimization_barrier((small_parts, tokens_other, w_half))

    w_experts = lax.all_gather(w_half, dense, axis=0, tiled=True)

    steps = seq // BQ
    n_own = steps // 2
    turned = lambda i, at: jnp.where(i < n_own, at[2] + i, i - at[2])
    qkv_all, normed_one, scale_one, small_all, gains = call(
        partial(qkv_kernel, first_col, qkv_cols, experts, len(small_parts)),
        (steps,),
        [
            pl.BlockSpec((BQ, model), lambda i, at: (jnp.minimum(i, n_own - 1), 0)),
            pl.BlockSpec((BQ, model), lambda i, at: (jnp.maximum(i - n_own, 0), 0)),
            *[whole(*p.shape) for p in small_parts],
        ],
        [
            pl.BlockSpec((BQ, qkv_cols), lambda i, at: (turned(i, at), 0)),
            pl.BlockSpec((BQ, model), lambda i, at: (turned(i, at), 0)),
            pl.BlockSpec((1, BQ), lambda i, at: (0, turned(i, at))),
            whole(model, cols),
            whole(8, model),
        ],
        [
            shaped((seq, qkv_cols), BF),
            shaped((seq, model), BF),
            shaped((1, seq), F32),
            shaped((model, cols), BF),
            shaped((8, model), F32),
        ],
        prefetch=1,
        name="norm_qkv",
    )(at, tokens, tokens_other, *small_parts)
    mixed, low_one, lse, *kept = attention_fwd(info, table, qkv_all, docs, band, rows)
    turns_one = gather_turns(low_one)
    mixed, low_two, lse = attention_fwd(info, table, qkv_all, docs, band, rows, (mixed, lse, *kept))
    turns_one, low_two = lax.optimization_barrier((turns_one, low_two))
    turns_two = gather_turns(low_two)

    router_block = pl.BlockSpec((model, LANES), lambda i, at: (0, cols // LANES - 1))
    out_block = whole(model, model)

    def hidden_half(first, turns, before):
        anywhere = pl.BlockSpec(memory_space=pl.ANY)
        return call(
            partial(hidden_kernel, experts, len(before)),
            (blocks // 2,),
            [
                pl.BlockSpec((BQ, model), lambda i, at: (first + i, 0)),
                *[pl.BlockSpec((width, BQ), lambda i, at: (0, i))] * 4,
                out_block,
                whole(8, model),
                router_block,
                pl.BlockSpec((1, BQ), lambda i, at: (0, first + i)),
                *[anywhere] * len(before),
            ],
            [
                pl.BlockSpec((BQ, model), lambda i, at: (first + i, 0)),
                pl.BlockSpec((BQ, model), lambda i, at: (first + i, 0)),
                pl.BlockSpec((1, BQ), lambda i, at: (0, first + i)),
                pl.BlockSpec((share, BQ), lambda i, at: (0, first + i)),
            ],
            [
                shaped((rows, model), F32),
                shaped((rows, model), BF),
                shaped((1, rows), F32),
                shaped((share, rows), F32),
            ],
            scratch=[pltpu.VMEM((model, BQ), F32)],
            prefetch=1,
            aliases={10 + n: n for n in range(len(before))},
            name="hidden_router",
        )(at, tokens, *turns, out_all, gains, small_all, chosen, *before)

    half_done = hidden_half(0, turns_one, ())
    sorted_rows = tiles * TILE
    sorted_spec = lambda cols: pl.BlockSpec((TILE, cols), lambda i, *_: (i, 0))
    turns_two, half_done = lax.optimization_barrier((turns_two, half_done))
    hidden, normed_two, gate_row, hidden_share = hidden_half(blocks // 2, turns_two, half_done)
    *back, eo_sorted, x_sorted, d_expert, active, d_inner = call(
        expert_kernel,
        (tiles,),
        [
            whole(1, rows),
            whole(rows, model),
            whole(rows, model),
            whole(1, rows),
            pl.BlockSpec((model, 2 * ff), lambda i, owner, at: (owner[0, i], 0)),
        ],
        [
            *[whole(part + 16, model)] * 4,
            sorted_spec(model),
            sorted_spec(model),
            sorted_spec(model),
            sorted_spec(ff),
            sorted_spec(ff),
        ],
        [
            *[shaped((part + 16, model), BF)] * 4,
            shaped((sorted_rows, model), BF),
            shaped((sorted_rows, model), BF),
            shaped((sorted_rows, model), BF),
            shaped((sorted_rows, ff), BF),
            shaped((sorted_rows, ff), BF),
        ],
        scratch=[
            pltpu.VMEM((sorted_rows, model + LANES), BF),
            pltpu.VMEM((rows, LANES), F32),
        ],
        prefetch=2,
        name="experts",
    )(owner, at, pos, normed_two, grad_out, gate_row, w_experts)
    back_mine = scatter_turns(back)
    back_got = back_mine[1:]
    grad_experts = call(
        weight_grad_kernel,
        (tiles,),
        [sorted_spec(model), sorted_spec(ff), sorted_spec(model), sorted_spec(ff)],
        pl.BlockSpec((model, 2 * ff), lambda i, owner: (owner[0, i], 0)),
        shaped((experts * model, 2 * ff), BF),
        scratch=[pltpu.VMEM((model, 2 * ff), F32)],
        prefetch=1,
        name="expert_weight_grads",
    )(owner, x_sorted, d_inner, d_expert, active)
    eo_out = call(
        unsort_kernel,
        (1,),
        [whole(1, rows), whole(sorted_rows, model)],
        [whole(share, rows)] * 4,
        [shaped((share, rows), BF)] * 4,
        scratch=[pltpu.VMEM((rows, LANES), F32), pltpu.VMEM((model, part), BF)],
        prefetch=2,
        name="unsort_outputs",
    )(owner, at, pos, after(eo_sorted, grad_experts))
    grad_experts = lax.psum_scatter(after(grad_experts, back_got, eo_out), dense, scatter_dimension=0, tiled=True)

    back_mine, eo_out = lax.optimization_barrier((back_mine, eo_out))

    small_rows = -(-(experts + 1) // 8) * 8
    row_block = pl.BlockSpec((part, model), lambda i, at: (at[0], 0))
    col_one = pl.BlockSpec((width, part), lambda i, at: (0, jnp.minimum(at[0], 1)))
    col_two = pl.BlockSpec((width, part), lambda i, at: (0, jnp.maximum(at[0] - 2, 0)))
    piece = whole(width, part)
    grad_rows = [model // 2] * 2 if square else [model]
    outs = call(
        partial(hidden_back_kernel, experts),
        (1,),
        [
            *[whole(part + 16, model)] * 4,
            row_block,
            row_block,
            whole(8, model),
            router_block,
            pl.BlockSpec((1, part), lambda i, at: (0, at[0])),
            out_block,
        ],
        [*[piece] * 4, whole(part, model), whole(small_rows, model)],
        [
            *[shaped((width, part), BF)] * 4,
            shaped((part, model), F32),
            shaped((small_rows, model), F32),
        ],
        prefetch=1,
        name="hidden_back",
    )(at, *back_mine, hidden, grad_out, gains, small_all, chosen, out_all)
    dmix_out, d_hidden, small_grads = outs[0:4], outs[4], outs[5]
    grad_out_w = call(
        out_grad_kernel,
        (1,),
        [whole(part, model), *[col_one] * 4, *[col_two] * 4],
        whole(model, model),
        shaped((model, model), BF),
        prefetch=1,
        name="out_projection_grad",
    )(at, d_hidden, *turns_one, *turns_two)
    dmix = scatter_turns(dmix_out)
    dmix, eo_out, grad_out_w = lax.optimization_barrier((dmix, eo_out, grad_out_w))
    eo_mine = scatter_turns(eo_out)

    dq_t, dkv, skew, sides = attention_bwd(
        info, table, qkv_all, docs, docs, band, mixed, lse, dmix, kept[0], rows
    )
    dkv, eo_mine = lax.optimization_barrier((dkv, eo_mine))
    other = lax.dynamic_slice_in_dim(dkv, (1 - ctx_at) * rows, rows)
    got = lax.ppermute(other, "ctx", [(0, 1), (1, 0)])
    outs = call(
        partial(qkv_back_kernel, first_col, experts, heads),
        (blocks,),
        [
            pl.BlockSpec((width, BQ), lambda i, at: (0, i)),
            pl.BlockSpec((BQ, 2 * width), lambda i, at: (at[2] + i, 0)),
            pl.BlockSpec((BQ, 2 * width), lambda i, at: (i, 0)),
            pl.BlockSpec((BQ, model), lambda i, at: (at[2] + i, 0)),
            pl.BlockSpec((BQ, model), lambda i, at: (i, 0)),
            pl.BlockSpec((1, BQ), lambda i, at: (0, at[2] + i)),
            whole(8, model),
            whole(model, cols),
            whole(part, model),
            whole(model, model),
            whole(small_rows, model),
            whole(16, 2 * BK),
            whole(8, BQ),
            whole(span, LANES),
            whole(LANES, model),
        ],
        [
            pl.BlockSpec((model, BQ), lambda i, at: (0, i)),
            *[whole(n, late_at + LANES) for n in grad_rows],
        ],
        [
            shaped((model, rows), BF),
            *[shaped((n, late_at + LANES), BF) for n in grad_rows],
        ],
        scratch=[pltpu.VMEM((model, late_at + LANES), F32), pltpu.VMEM((8, model), F32)],
        prefetch=1,
        name="qkv_back",
    )(
        at, dq_t, dkv, got, normed_one, tokens, scale_one, gains, small_all, d_hidden, grad_out_w,
        small_grads, skew, sides, diag, spread,
    )
    terms, grad_dense = outs[0], outs[1:]
    dense_cols = late_at + LANES
    piece_cols = -(-(LANES + width) // LANES) * LANES
    if square:
        keep, send = grad_dense
        pieces = call(
            pair_sum_kernel,
            (1,),
            [whole(4 * own, dense_cols)] * 2,
            [whole(own, dense_cols)] * 4,
            [shaped((own, dense_cols), BF)] * 4,
            name="dense_pair_sum",
        )(keep, xor_step(send, "ctx", 1))
        first_pieces = pieces
        pieces = [pieces[0]] + [xor_step(pieces[s], "fsdp", s) for s in (1, 2, 3)]
    else:
        first_pieces = []
        pieces = [lax.psum_scatter(grad_dense[0], dense, scatter_dimension=0, tiled=True)]
    terms = after(terms, grad_experts, first_pieces)
    grad_tokens = lax.psum_scatter(terms, "tp", scatter_dimension=0, tiled=True).astype(F32)
    grad_qkv, grad_table, *pieces = call(
        partial(dense_sum_kernel, wide_cols, len(pieces), experts + 2),
        (1,),
        [whole(own, dense_cols)] * len(pieces),
        [whole(3, own, width), whole(table_rows, heads), *[whole(own, piece_cols)] * 4],
        [
            shaped((3, own, width), F32),
            shaped((table_rows, heads), F32),
            *[shaped((own, piece_cols), BF)] * 4,
        ],
        name="dense_sum",
    )(*pieces)
    pieces = [pieces[0]] + [turn(pieces[s], 4 - s) for s in (1, 2, 3)]
    grad_in, grad_down = grad_experts[:, 0:ff].astype(F32), grad_experts[:, ff:].astype(F32)
    pieces, grad_in, grad_down = lax.optimization_barrier((pieces, grad_in, grad_down))
    grad_out_mine, grad_router, grad_gain_two, grad_gain_one = call(
        last_sum_kernel,
        (1,),
        [whole(own, piece_cols)] * 4,
        [whole(own, width), whole(experts, own), whole(1, own), whole(1, own)],
        [
            shaped((own, width), F32),
            shaped((experts, own), F32),
            shaped((1, own), F32),
            shaped((1, own), F32),
        ],
        name="last_sum",
    )(*pieces)
    hidden_share = after(hidden_share, grad_qkv)
    share_block = pl.BlockSpec((share, BQ), lambda i, *_: (0, i))
    out_share = call(
        out_kernel,
        (blocks,),
        [*[share_block] * 5, pl.BlockSpec((1, BQ), lambda i: (0, i))],
        share_block,
        shaped((share, rows), BF),
        name="layer_output",
    )(*eo_mine, hidden_share, gate_row)
    return (
        out_share.T,
        grad_tokens.T,
        grad_qkv.transpose(1, 0, 2),
        grad_out_mine,
        grad_table,
        grad_gain_one.reshape(own),
        grad_gain_two.reshape(own),
        grad_router.T,
        grad_in[None],
        grad_down[None],
    )


def solution(mesh):
    placed = (
        P(("fsdp", "ctx"), None),
        P(("fsdp", "ctx"), None),
        P(("fsdp", "ctx"), None, "tp"),
        P(("fsdp", "ctx"), "tp"),
        P(None, "tp"),
        P(("fsdp", "ctx")),
        P(("fsdp", "ctx")),
        P(("fsdp", "ctx"), None),
        P("fsdp", None, "tp"),
        P("fsdp", None, "tp"),
        P(("fsdp", "ctx"), None),
        P("fsdp"),
    )
    return jax.shard_map(
        shards,
        mesh=mesh,
        in_specs=placed,
        out_specs=(
            P(("fsdp", "ctx"), "tp"),
            P(("fsdp", "ctx"), "tp"),
            P(("fsdp", "ctx"), None, "tp"),
            P(("fsdp", "ctx"), "tp"),
            P(("fsdp", "ctx"), "tp"),
            P(("fsdp", "ctx")),
            P(("fsdp", "ctx")),
            P(("fsdp", "ctx"), None),
            P("fsdp", "ctx", "tp"),
            P("fsdp", "ctx", "tp"),
        ),
        check_vma=False,
    )
```
